32 devices in a mesh: dp: 8 (over z, x), fsdp: 4 (over y, core).
Axes of the slice: x: 2, y: 2, z: 4, core: 2. Of those that a mesh axis runs over, the one named last changes fastest.
Arguments:
- char_inputs: bfloat16 [16, 1024, 16, 256], P('dp', 'fsdp'), may hold values from -6 to 6
- language_ids: int32 [16], P('dp'), may hold values from 0 to 31
- char_counts: int32 [16, 1024], P('dp', 'fsdp'), may hold values from 1 to 16
- row_lengths: int32 [16], P('dp'), may hold values from 512 to 1024, as said below
- cotangent: bfloat16 [16, 1024, 512], P('dp', 'fsdp'), may hold values from -6 to 6
- language_table: bfloat16 [32, 256], P(None, ('dp', 'fsdp')), may hold values from -3 to 3
- char_gain_one: bfloat16 [256], P(('dp', 'fsdp')), may hold values from 0.5 to 1.5
- char_bias_one: bfloat16 [256], P(('dp', 'fsdp')), may hold values from -1 to 1
- char_inward: bfloat16 [256, 768], P(('dp', 'fsdp')), may hold values from -0.375 to 0.375
- char_outward: bfloat16 [256, 256], P(('dp', 'fsdp')), may hold values from -0.75 to 0.75
- char_gain_two: bfloat16 [256], P(('dp', 'fsdp')), may hold values from 0.5 to 1.5
- char_bias_two: bfloat16 [256], P(('dp', 'fsdp')), may hold values from -1 to 1
- char_expand: bfloat16 [256, 1024], P(('dp', 'fsdp')), may hold values from -0.375 to 0.375
- char_expand_bias: bfloat16 [1024], P(('dp', 'fsdp')), may hold values from -1 to 1
- char_reduce: bfloat16 [1024, 256], P(('dp', 'fsdp')), may hold values from -0.1875 to 0.1875
- char_reduce_bias: bfloat16 [256], P(('dp', 'fsdp')), may hold values from -1 to 1
- char_to_word: bfloat16 [256, 512], P(('dp', 'fsdp')), may hold values from -0.375 to 0.375
- char_to_word_bias: bfloat16 [512], P(('dp', 'fsdp')), may hold values from -1 to 1
- word_gain_one: bfloat16 [512], P(('dp', 'fsdp')), may hold values from 0.5 to 1.5
- word_bias_one: bfloat16 [512], P(('dp', 'fsdp')), may hold values from -1 to 1
- word_inward: bfloat16 [512, 1536], P(('dp', 'fsdp')), may hold values from -0.25 to 0.25
- word_outward: bfloat16 [512, 512], P(('dp', 'fsdp')), may hold values from -1 to 1
- word_gain_two: bfloat16 [512], P(('dp', 'fsdp')), may hold values from 0.5 to 1.5
- word_bias_two: bfloat16 [512], P(('dp', 'fsdp')), may hold values from -1 to 1
- word_expand: bfloat16 [512, 2048], P(('dp', 'fsdp')), may hold values from -0.25 to 0.25
- word_expand_bias: bfloat16 [2048], P(('dp', 'fsdp')), may hold values from -1 to 1
- word_reduce: bfloat16 [2048, 512], P(('dp', 'fsdp')), may hold values from -0.125 to 0.125
- word_reduce_bias: bfloat16 [512], P(('dp', 'fsdp')), may hold values from -1 to 1
Outputs:
- words_out: float32 [16, 1024, 512], P('dp', 'fsdp')
- char_input_grad: float32 [16, 1024, 16, 256], P('dp', 'fsdp')
- grad_language_table: float32 [32, 256], P(None, ('dp', 'fsdp'))
- grad_char_gain_one: float32 [256], P(('dp', 'fsdp'))
- grad_char_bias_one: float32 [256], P(('dp', 'fsdp'))
- grad_char_inward: float32 [256, 768], P(('dp', 'fsdp'))
- grad_char_outward: float32 [256, 256], P(('dp', 'fsdp'))
- grad_char_gain_two: float32 [256], P(('dp', 'fsdp'))
- grad_char_bias_two: float32 [256], P(('dp', 'fsdp'))
- grad_char_expand: float32 [256, 1024], P(('dp', 'fsdp'))
- grad_char_expand_bias: float32 [1024], P(('dp', 'fsdp'))
- grad_char_reduce: float32 [1024, 256], P(('dp', 'fsdp'))
- grad_char_reduce_bias: float32 [256], P(('dp', 'fsdp'))
- grad_char_to_word: float32 [256, 512], P(('dp', 'fsdp'))
- grad_char_to_word_bias: float32 [512], P(('dp', 'fsdp'))
- grad_word_gain_one: float32 [512], P(('dp', 'fsdp'))
- grad_word_bias_one: float32 [512], P(('dp', 'fsdp'))
- grad_word_inward: float32 [512, 1536], P(('dp', 'fsdp'))
- grad_word_outward: float32 [512, 512], P(('dp', 'fsdp'))
- grad_word_gain_two: float32 [512], P(('dp', 'fsdp'))
- grad_word_bias_two: float32 [512], P(('dp', 'fsdp'))
- grad_word_expand: float32 [512, 2048], P(('dp', 'fsdp'))
- grad_word_expand_bias: float32 [2048], P(('dp', 'fsdp'))
- grad_word_reduce: float32 [2048, 512], P(('dp', 'fsdp'))
- grad_word_reduce_bias: float32 [512], P(('dp', 'fsdp'))
The draws below stay inside these ranges and needn't reach their ends.
Inputs may be any that keep to these rules, and one draw needn't show every extreme that they name: `row_lengths`: in each aligned group of 2 rows one row has all 1024 words. The live characters of a word are its first char_counts ones.
All inputs are finite; a program needn't handle non-finite values.
Results may differ from the reference program's by a relative error of at most 0.013.
Values may be sent and summed in bfloat16 or wider, within the bound.
No kernel may reach another device: no remote copies, remote signals or barrier semaphores. Data moves between devices by JAX's collectives and lax.ppermute only.
A program may use at most 384 MiB of HBM per device.

```python
import jax
import jax.numpy as jnp
from jax import lax

CD = 256
CF = 1024
CHEADS = 4
CHARS = 16
D = 512
FF = 2048
WHEADS = 8
LANGS = 32
WORDS = 1024
ROWS_G = 2
ROWS = 16


def draw_row_lengths(key, part):
    key = jax.random.fold_in(key, 11)
    first_key, second_key = jax.random.split(key)
    lengths = jax.random.randint(first_key, (ROWS,), WORDS // 2, WORDS + 1)
    full_member = jax.random.randint(second_key, (ROWS // ROWS_G,), 0, ROWS_G)
    row_index = jnp.arange(ROWS)
    is_full = row_index % ROWS_G == full_member[row_index // ROWS_G]
    return jnp.where(is_full, WORDS, lengths).astype(jnp.int32)


def plant(values, stream_key, smallest, top_value):
    shape = values.shape
    spot = [jax.random.randint(jax.random.fold_in(stream_key, axis), (), 0, shape[axis]) for axis in range(len(shape))]
    values = values.at[tuple(spot)].set(smallest)
    longest = shape.index(max(shape))
    spot[longest] = (spot[longest] + 1) % shape[longest]
    return values.at[tuple(spot)].set(top_value)


def block_scale(own_key, extent, cuts, low, largest):
    factor_of, own = 1.0, jax.random.fold_in(own_key, 6)
    for dim, blocks in cuts:
        draws = jnp.exp(jax.random.uniform(jax.random.fold_in(own, dim), (blocks,), jnp.float32, low / len(cuts), largest / len(cuts)))
        factor_of = factor_of * jnp.repeat(draws, extent[dim] // blocks).reshape([-1 if axis == dim else 1 for axis in range(len(extent))])
    return factor_of


def scatter_about(stream_key, extent, width, bound, cuts=(), held_as=jnp.bfloat16):
    values = width * jax.random.normal(stream_key, extent, jnp.float32)
    if cuts:
        values = values * block_scale(stream_key, extent, cuts, -0.22, 0.18)
    return jnp.clip(values, -bound, bound).astype(held_as)


def setup_inputs(seed: int = 0) -> dict:
    splits = jax.random.split(jax.random.key(seed), 29)
    char_inputs = scatter_about(splits[0], (ROWS, WORDS, CHARS, CD), 1.0, 6.0, ((0, 8), (1, 4)))
    language_ids = plant(jax.random.randint(splits[1], (ROWS,), 0, LANGS), jax.random.fold_in(splits[1], 1), 0, LANGS - 1).astype(jnp.int32)
    char_counts = plant(jax.random.randint(splits[2], (ROWS, WORDS), 1, CHARS + 1), jax.random.fold_in(splits[2], 1), 1, CHARS).astype(jnp.int32)
    row_lengths = draw_row_lengths(jax.random.fold_in(splits[28], 71), 0)
    cotangent = scatter_about(splits[4], (ROWS, WORDS, D), 1.0, 6.0, ((0, 8), (1, 4)))
    language_table = scatter_about(splits[5], (LANGS, CD), 0.5, 3.0, ((1, 32),))
    char_gain_one = jnp.clip(1.0 + 0.1 * jax.random.normal(splits[6], (CD,), jnp.float32), 0.5, 1.5).astype(jnp.bfloat16)
    char_bias_one = scatter_about(splits[7], (CD,), 0.2, 1.0, ((0, 32),))
    char_inward = scatter_about(splits[8], (CD, 3 * CD), CD ** -0.5, 0.375, ((0, 32),))
    char_outward = scatter_about(splits[9], (CD, CD), (CD // 4) ** -0.5, 0.75, ((0, 32),))
    char_gain_two = jnp.clip(1.0 + 0.1 * jax.random.normal(splits[10], (CD,), jnp.float32), 0.5, 1.5).astype(jnp.bfloat16)
    char_bias_two = scatter_about(splits[11], (CD,), 0.2, 1.0, ((0, 32),))
    char_expand = scatter_about(splits[12], (CD, CF), CD ** -0.5, 0.375, ((0, 32),))
    char_expand_bias = scatter_about(splits[13], (CF,), 0.2, 1.0, ((0, 32),))
    char_reduce = scatter_about(splits[14], (CF, CD), CF ** -0.5, 0.1875, ((0, 32),))
    char_reduce_bias = scatter_about(splits[15], (CD,), 0.2, 1.0, ((0, 32),))
    char_to_word = scatter_about(splits[16], (CD, D), CD ** -0.5, 0.375, ((0, 32),))
    char_to_word_bias = scatter_about(splits[17], (D,), 0.2, 1.0, ((0, 32),))
    word_gain_one = jnp.clip(1.0 + 0.1 * jax.random.normal(splits[18], (D,), jnp.float32), 0.5, 1.5).astype(jnp.bfloat16)
    word_bias_one = scatter_about(splits[19], (D,), 0.2, 1.0, ((0, 32),))
    word_inward = scatter_about(splits[20], (D, 3 * D), D ** -0.5, 0.25, ((0, 32),))
    word_outward = scatter_about(splits[21], (D, D), (D // 16) ** -0.5, 1.0, ((0, 32),))
    word_gain_two = jnp.clip(1.0 + 0.1 * jax.random.normal(splits[22], (D,), jnp.float32), 0.5, 1.5).astype(jnp.bfloat16)
    word_bias_two = scatter_about(splits[23], (D,), 0.2, 1.0, ((0, 32),))
    word_expand = scatter_about(splits[24], (D, FF), D ** -0.5, 0.25, ((0, 32),))
    word_expand_bias = scatter_about(splits[25], (FF,), 0.2, 1.0, ((0, 32),))
    word_reduce = scatter_about(splits[26], (FF, D), FF ** -0.5, 0.125, ((0, 32),))
    word_reduce_bias = scatter_about(splits[27], (D,), 0.2, 1.0, ((0, 32),))
    return dict(char_inputs=char_inputs, language_ids=language_ids, char_counts=char_counts, row_lengths=row_lengths, cotangent=cotangent, language_table=language_table, char_gain_one=char_gain_one, char_bias_one=char_bias_one, char_inward=char_inward, char_outward=char_outward, char_gain_two=char_gain_two, char_bias_two=char_bias_two, char_expand=char_expand, char_expand_bias=char_expand_bias, char_reduce=char_reduce, char_reduce_bias=char_reduce_bias, char_to_word=char_to_word, char_to_word_bias=char_to_word_bias, word_gain_one=word_gain_one, word_bias_one=word_bias_one, word_inward=word_inward, word_outward=word_outward, word_gain_two=word_gain_two, word_bias_two=word_bias_two, word_expand=word_expand, word_expand_bias=word_expand_bias, word_reduce=word_reduce, word_reduce_bias=word_reduce_bias)


EPS = 1e-05
NEG_BIG = -1000000000.0
HIGHEST = lax.Precision.HIGHEST

@jax.custom_vjp
def low(v):
    return lax.optimization_barrier(v.astype(jnp.bfloat16)).astype(jnp.float32)

@jax.custom_vjp
def low_back(v):
    return v

def low_keep(v):
    return (low(v), None)

def low_pass(kept, grad):
    return (grad,)

def back_keep(v):
    return (v, None)

def back_low(kept, grad):
    return (low(grad),)
low.defvjp(low_keep, low_pass)
low_back.defvjp(back_keep, back_low)

def product(left_side, right_side):
    return jnp.dot(left_side, right_side, precision=HIGHEST)

def norm_apply(hidden, norm_gain, norm_bias):
    row_mean = lax.optimization_barrier(jnp.mean(hidden, -1, keepdims=True))
    centred = hidden - row_mean
    variance = lax.optimization_barrier(jnp.mean(centred * centred, -1, keepdims=True))
    return centred * lax.rsqrt(variance + EPS) * norm_gain + norm_bias

def char_row(params, char_rows, language, counts):
    table, gain_one, bias_one, inward, outward, gain_two, bias_two, expand, expand_bias, reduce_weight, reduce_bias, to_word, to_word_bias = params[:13]
    head_size = CD // CHEADS
    score_scale = head_size ** (-0.5)
    one_hot = (jnp.arange(LANGS) == language).astype(jnp.float32)
    char_start = char_rows + product(one_hot, table)[None, None, :]
    live_mask = jnp.arange(CHARS)[None, :] < counts[:, None]
    normed = low(norm_apply(char_start, gain_one, bias_one))
    projected = low_back(low(product(normed, inward)))
    queries = projected[..., :CD].reshape(WORDS, CHARS, CHEADS, head_size)
    key_rows = projected[..., CD:2 * CD].reshape(WORDS, CHARS, CHEADS, head_size)
    values = projected[..., 2 * CD:].reshape(WORDS, CHARS, CHEADS, head_size)
    scores = jnp.einsum('nchx,ndhx->hcdn', queries, key_rows, precision=HIGHEST) * score_scale
    scores = low_back(jnp.where(live_mask.T[None, None], scores, NEG_BIG))
    soft_weights = jax.nn.softmax(scores, axis=2)
    mixed_low = jnp.einsum('hcdn,ndhx->nchx', low(soft_weights), values, precision=HIGHEST)
    mixed_low = low_back(low(mixed_low.reshape(WORDS, CHARS, CD)))
    after_attn = char_start + low_back(product(mixed_low, outward))
    normed_two = low(norm_apply(after_attn, gain_two, bias_two))
    pre_gelu = low_back(product(normed_two, expand) + expand_bias)
    after_mlp = after_attn + low_back(product(low(jax.nn.gelu(pre_gelu)), reduce_weight) + reduce_bias)
    live_float = live_mask.astype(jnp.float32)
    pooled = lax.optimization_barrier(jnp.sum(after_mlp * live_float[..., None], 1)) / counts.astype(jnp.float32)[:, None]
    return low_back(product(low(pooled), to_word) + to_word_bias)

def word_row(params, word_in, length):
    gain_one, bias_one, inward, outward, gain_two, bias_two, expand, expand_bias, reduce_weight, reduce_bias = params[13:]
    head_size = D // WHEADS
    score_scale = head_size ** (-0.5)
    normed = low(norm_apply(word_in, gain_one, bias_one))
    projected = low_back(low(product(normed, inward)))
    queries = projected[:, :D].reshape(WORDS, WHEADS, head_size)
    key_rows = projected[:, D:2 * D].reshape(WORDS, WHEADS, head_size)
    values = projected[:, 2 * D:].reshape(WORDS, WHEADS, head_size)
    position = jnp.arange(WORDS)
    allowed = (position[None, :] <= position[:, None]) & (position[None, :] < length)
    scores = jnp.einsum('ihx,jhx->hij', queries, key_rows, precision=HIGHEST) * score_scale
    scores = low_back(jnp.where(allowed[None], scores, NEG_BIG))
    soft_weights = jax.nn.softmax(scores, axis=-1)
    mixed_low = jnp.einsum('hij,jhx->ihx', low(soft_weights), values, precision=HIGHEST)
    mixed_low = low_back(low(mixed_low.reshape(WORDS, D)))
    after_attn = word_in + low_back(product(mixed_low, outward))
    normed_two = low(norm_apply(after_attn, gain_two, bias_two))
    pre_gelu = low_back(product(normed_two, expand) + expand_bias)
    after_mlp = after_attn + low_back(product(low(jax.nn.gelu(pre_gelu)), reduce_weight) + reduce_bias)
    valid_mask = position < length
    return jnp.where(valid_mask[:, None], after_mlp, 0.0)

def add_up(earlier, addition):
    return earlier + addition

def reference(char_inputs, language_ids, char_counts, row_lengths, cotangent, language_table, char_gain_one, char_bias_one, char_inward, char_outward, char_gain_two, char_bias_two, char_expand, char_expand_bias, char_reduce, char_reduce_bias, char_to_word, char_to_word_bias, word_gain_one, word_bias_one, word_inward, word_outward, word_gain_two, word_bias_two, word_expand, word_expand_bias, word_reduce, word_reduce_bias):
    params = tuple((weight.astype(jnp.float32) for weight in (language_table, char_gain_one, char_bias_one, char_inward, char_outward, char_gain_two, char_bias_two, char_expand, char_expand_bias, char_reduce, char_reduce_bias, char_to_word, char_to_word_bias, word_gain_one, word_bias_one, word_inward, word_outward, word_gain_two, word_bias_two, word_expand, word_expand_bias, word_reduce, word_reduce_bias)))

    def row_step(totals, row_inputs):
        char_rows, language, counts, length, upstream = row_inputs

        def forward(weights, char_float):
            return word_row(weights, char_row(weights, char_float, language, counts), length)
        result, pullback = jax.vjp(forward, params, char_rows.astype(jnp.float32))
        weight_grads, char_grad = pullback(upstream.astype(jnp.float32))
        totals = jax.tree.map(add_up, totals, weight_grads)
        return (totals, (result, char_grad))
    zeros = tuple((jnp.zeros_like(weight) for weight in params))
    totals, outputs = lax.scan(row_step, zeros, (char_inputs, language_ids, char_counts, row_lengths, cotangent))
    words_out, char_input_grad = outputs
    return (words_out, char_input_grad, totals[0], totals[1], totals[2], totals[3], totals[4], totals[5], totals[6], totals[7], totals[8], totals[9], totals[10], totals[11], totals[12], totals[13], totals[14], totals[15], totals[16], totals[17], totals[18], totals[19], totals[20], totals[21], totals[22])
```

```python
import functools

import jax
import jax.numpy as jnp
from jax import lax
from jax.experimental import pallas as pl
from jax.experimental.pallas import tpu as pltpu
from jax.sharding import PartitionSpec as P

BF = jnp.bfloat16
F32 = jnp.float32
EPS = 1e-05
MASKED = -1e30
CHEADS = 4
WHEADS = 8
HEAD = 64
SCALE = HEAD ** (-0.5)
GROUP = 128
BLOCK = 512
SPLIT = BLOCK // GROUP
FOLD = 4
SMALL = 128
GELU_A = 0.7978845608028654
GELU_B = 0.044715
MIB = 1024 * 1024


def dot(a, b):
    return jnp.dot(a, b, preferred_element_type=F32)


def dot_t(a, b):
    return lax.dot_general(a, b, (((1,), (1,)), ((), ())), preferred_element_type=F32)


def t_dot(a, b):
    return lax.dot_general(a, b, (((0,), (0,)), ((), ())), preferred_element_type=F32)


def norm_parts(hidden):
    centred = hidden - jnp.mean(hidden, -1, keepdims=True)
    spread = lax.rsqrt(jnp.mean(centred * centred, -1, keepdims=True) + EPS)
    return centred * spread, spread


def norm_back(unit, spread, gained):
    return (
        gained
        - jnp.mean(gained, -1, keepdims=True)
        - unit * jnp.mean(gained * unit, -1, keepdims=True)
    ) * spread


def gelu_both(pre):
    square = pre * pre
    turn = jnp.tanh(pre * (GELU_A + (GELU_A * GELU_B) * square))
    half = 0.5 + 0.5 * turn
    slope = half + pre * half * (1.0 - turn) * (GELU_A + (3.0 * GELU_A * GELU_B) * square)
    return pre * half, slope


def fold_rows(values):
    rows, width = values.shape
    return jnp.sum(values.reshape(rows // 8, 8, width), 0)


def head_masks(width, heads):
    lanes = lax.broadcasted_iota(jnp.int32, (1, width), 1) // HEAD
    return [(lanes == h).astype(F32).astype(BF) for h in range(heads)]


def live_steps(kernel):
    def run(settings, blocks, *refs):
        @pl.when(pl.program_id(0) < blocks[0])
        def _():
            kernel(settings, blocks, *refs)

    return run


def full(shape):
    return pl.BlockSpec(shape, lambda *_: (0,) * len(shape))


def pack_kernel(
    per_row, counts, chars, packed, bias, hot, offs, first, rows_of, blocks, tags, *wide
):
    words, slots, width = chars.shape
    for part in wide:
        part[...] = jnp.zeros_like(part)
    tags[...] = jnp.full_like(tags, -1.0)

    def clear(g, carry):
        first[g] = 0
        rows_of[g] = 0
        return carry

    lax.fori_loop(0, first.shape[0], clear, 0)
    slot = lax.broadcasted_iota(jnp.int32, (slots, GROUP), 0)

    def place(w, at):
        live = counts[w]
        inside = lax.rem(at, GROUP)
        fresh = (inside + live > GROUP) | (lax.rem(w, per_row) == 0)
        at = jnp.where(fresh, lax.div(at + (GROUP - 1), GROUP) * GROUP, at)

        @pl.when(lax.rem(at, GROUP) == 0)
        def _():
            first[lax.div(at, GROUP)] = w
            rows_of[lax.div(at, GROUP)] = lax.div(w, per_row)

        for k, part in enumerate(wide):
            part[pl.ds(at, slots), :] = chars[w, :, k * GROUP : (k + 1) * GROUP].astype(F32)
        tags[pl.ds(at, slots), :] = jnp.where(slot < live, w.astype(F32), -1.0)
        offs[w] = at
        return at + live

    end = lax.fori_loop(0, words, place, 0)
    used = lax.div(end + (BLOCK - 1), BLOCK)
    blocks[0] = used
    lane = lax.broadcasted_iota(jnp.int32, (GROUP, GROUP), 1).astype(F32)

    def finish(g, carry):
        here = pl.ds(pl.multiple_of(g * GROUP, GROUP), GROUP)
        tag = tags[here, :]
        bias[here, :] = jnp.where(tag == tag.T, 0.0, MASKED).astype(BF)
        hot[here, :] = (tag - first[g].astype(F32) == lane).astype(F32).astype(BF)
        for k, part in enumerate(wide):
            packed[here, k * GROUP : (k + 1) * GROUP] = part[here, :].astype(BF)
        return carry

    lax.fori_loop(0, used * SPLIT, finish, 0)


def pack(counts, chars, per_row):
    words, slots, width = chars.shape
    groups = (words * slots) // (GROUP - slots + 1) + 1 + words // per_row
    groups = -(-groups // SPLIT) * SPLIT
    rows = groups * GROUP
    smem = pl.BlockSpec(memory_space=pltpu.SMEM)
    vmem = pl.BlockSpec(memory_space=pltpu.VMEM)
    return pl.pallas_call(
        functools.partial(pack_kernel, per_row),
        out_shape=(
            jax.ShapeDtypeStruct((rows, width), BF),
            jax.ShapeDtypeStruct((rows, GROUP), BF),
            jax.ShapeDtypeStruct((rows, GROUP), BF),
            jax.ShapeDtypeStruct((words,), jnp.int32),
            jax.ShapeDtypeStruct((groups,), jnp.int32),
            jax.ShapeDtypeStruct((groups,), jnp.int32),
            jax.ShapeDtypeStruct((1,), jnp.int32),
        ),
        in_specs=[smem, vmem],
        out_specs=(vmem, vmem, vmem, smem, smem, smem, smem),
        scratch_shapes=[pltpu.VMEM((rows + slots, GROUP), F32)] * (1 + width // GROUP),
        compiler_params=pltpu.CompilerParams(vmem_limit_bytes=48 * MIB),
        cost_estimate=pl.CostEstimate(
            flops=rows * width * 4, bytes_accessed=rows * width * 6, transcendentals=0
        ),
    )(counts, chars)


def unpack_kernel(offs, counts, *refs):
    packed, out = refs[:-1], refs[-1]
    here = pl.program_id(0) * out.shape[0]
    slots = out.shape[1]
    slot = lax.broadcasted_iota(jnp.int32, (slots, GROUP), 0)

    def take(k, carry):
        w = here + k
        for j, part in enumerate(packed):
            rows = part[pl.ds(offs[w], slots), :]
            out[k, :, j * GROUP : (j + 1) * GROUP] = jnp.where(slot < counts[w], rows, 0.0)
        return carry

    lax.fori_loop(0, out.shape[0], take, 0)


def unpack(offs, counts, packed, words, slots):
    width = len(packed) * GROUP
    step = words // 8
    return pl.pallas_call(
        unpack_kernel,
        out_shape=jax.ShapeDtypeStruct((words, slots, width), F32),
        grid_spec=pltpu.PrefetchScalarGridSpec(
            num_scalar_prefetch=2,
            grid=(words // step,),
            in_specs=[full(part.shape) for part in packed],
            out_specs=pl.BlockSpec((step, slots, width), lambda i, *_: (i, 0, 0)),
        ),
        compiler_params=pltpu.CompilerParams(vmem_limit_bytes=48 * MIB),
        cost_estimate=pl.CostEstimate(
            flops=words * slots * width, bytes_accessed=words * slots * width * 8, transcendentals=0
        ),
    )(offs, counts, *packed)


def with_language(i, rows_of, ids, packed, small_rows):
    parts = []
    for g in range(SPLIT):
        row = small_rows[pl.ds(ids[rows_of[i * SPLIT + g]], 1), :]
        parts.append(packed[g * GROUP : (g + 1) * GROUP, :].astype(F32) + row)
    return jnp.concatenate(parts, 0)


def stack_heads(values, masks):
    return jnp.concatenate([values * mask for mask in masks], 0)


@live_steps
def char_attend_kernel(
    langs,
    blocks,
    rows_of, ids, packed, bias, weights, qkv_out, soft_out, mixed_out, after_out, small_rows
):
    i = pl.program_id(0)
    width = packed.shape[1]

    @pl.when(i == 0)
    def _():
        small_rows[...] = weights[:, 4 * width :].astype(F32).T

    start = with_language(i, rows_of, ids, packed, small_rows)
    unit, _ = norm_parts(start)
    normed = (unit * small_rows[langs : langs + 1, :] + small_rows[langs + 1 : langs + 2, :]).astype(BF)
    qkv_out[...] = dot(normed, weights[:, : 3 * width]).astype(BF)
    masks = head_masks(width, CHEADS)
    for g in range(SPLIT):
        here = slice(g * GROUP, (g + 1) * GROUP)
        keys = stack_heads(qkv_out[here, width : 2 * width], masks)
        scores = dot_t(qkv_out[here, :width], keys) * SCALE
        blocked = bias[here, :].astype(F32)
        parts = []
        for h in range(CHEADS):
            one = scores[:, h * GROUP : (h + 1) * GROUP] + blocked
            one = jnp.exp(one - jnp.max(one, -1, keepdims=True))
            parts.append((one * (1.0 / jnp.sum(one, -1, keepdims=True))).astype(BF))
        soft = jnp.concatenate(parts, 1)
        soft_out[here, :] = soft
        values = stack_heads(qkv_out[here, 2 * width :], masks)
        mixed_out[here, :] = dot(soft, values).astype(BF)
    after_out[...] = start + dot(mixed_out[...], weights[:, 3 * width : 4 * width])


@live_steps
def char_ffn_kernel(
    langs,
    blocks,
    first, after, hot, inverse, small, weights, act_out, slope_out, pooled_out, small_rows, *total
):
    i = pl.program_id(0)
    width = after.shape[1]
    hidden = FOLD * width

    @pl.when(i == 0)
    def _():
        small_rows[...] = small[...].astype(F32).T
        for part in total:
            part[...] = jnp.zeros_like(part)

    unit, _ = norm_parts(after[...])
    normed = (unit * small_rows[langs + 2 : langs + 3, :] + small_rows[langs + 3 : langs + 4, :]).astype(BF)
    out = after[...] + small_rows[langs + 4 : langs + 5, :]
    for j in range(FOLD):
        cols = slice(j * width, (j + 1) * width)
        pre = dot(normed, weights[:, cols]) + small_rows[langs + 5 + j : langs + 6 + j, :]
        act, slope = gelu_both(pre)
        act = act.astype(BF)
        act_out[:, cols] = act
        slope_out[:, cols] = slope.astype(BF)
        out = out + dot(act, weights[:, hidden + j * width : hidden + (j + 1) * width])
    out = out.astype(BF)
    for g in range(SPLIT):
        here = slice(g * GROUP, (g + 1) * GROUP)
        words = pl.ds(first[i * SPLIT + g], GROUP)
        found = t_dot(hot[here, :], out[here, :])
        for k, part in enumerate(total):
            part[words, :] = part[words, :] + found[:, k * GROUP : (k + 1) * GROUP]

    @pl.when(i == blocks[0] - 1)
    def _():
        for k, part in enumerate(total):
            pooled_out[:, k * GROUP : (k + 1) * GROUP] = (
                part[: pooled_out.shape[0], :] * inverse[...]
            ).astype(BF)


def rows_spec(width):
    return pl.BlockSpec((BLOCK, width), lambda i, blocks, *_: (jnp.minimum(i, blocks[0] - 1), 0))


def char_attend(langs, blocks, rows_of, ids, packed, bias, weights):
    rows, width = packed.shape
    return pl.pallas_call(
        functools.partial(char_attend_kernel, langs),
        out_shape=(
            jax.ShapeDtypeStruct((rows, 3 * width), BF),
            jax.ShapeDtypeStruct((rows, CHEADS * GROUP), BF),
            jax.ShapeDtypeStruct((rows, width), BF),
            jax.ShapeDtypeStruct((rows, width), F32),
        ),
        grid_spec=pltpu.PrefetchScalarGridSpec(
            num_scalar_prefetch=3,
            grid=(rows // BLOCK,),
            in_specs=[rows_spec(width), rows_spec(GROUP), full(weights.shape)],
            out_specs=(
                rows_spec(3 * width),
                rows_spec(CHEADS * GROUP),
                rows_spec(width),
                rows_spec(width),
            ),
            scratch_shapes=[pltpu.VMEM((SMALL, width), F32)],
        ),
        compiler_params=pltpu.CompilerParams(vmem_limit_bytes=48 * MIB),
        cost_estimate=pl.CostEstimate(
            flops=rows * width * width * 12, bytes_accessed=rows * width * 12, transcendentals=rows * 512
        ),
    )(blocks, rows_of, ids, packed, bias, weights)


def char_ffn(langs, blocks, first, after, hot, inverse, small_of, weights):
    rows, width = after.shape
    words = inverse.shape[0]
    hidden = FOLD * width
    return pl.pallas_call(
        functools.partial(char_ffn_kernel, langs),
        out_shape=(
            jax.ShapeDtypeStruct((rows, hidden), BF),
            jax.ShapeDtypeStruct((rows, hidden), BF),
            jax.ShapeDtypeStruct((words, width), BF),
        ),
        grid_spec=pltpu.PrefetchScalarGridSpec(
            num_scalar_prefetch=2,
            grid=(rows // BLOCK,),
            in_specs=[
                rows_spec(width),
                rows_spec(GROUP),
                full(inverse.shape),
                pl.BlockSpec((width, SMALL), lambda i, *_: (0, 4 * width // SMALL)),
                full(weights.shape),
            ],
            out_specs=(rows_spec(hidden), rows_spec(hidden), full((words, width))),
            scratch_shapes=[pltpu.VMEM((SMALL, width), F32)]
            + [pltpu.VMEM((words + GROUP, GROUP), F32)] * (width // GROUP),
        ),
        compiler_params=pltpu.CompilerParams(vmem_limit_bytes=48 * MIB),
        cost_estimate=pl.CostEstimate(
            flops=rows * width * width * 16, bytes_accessed=rows * width * 20, transcendentals=rows * 1024
        ),
    )(blocks, first, after, hot, inverse, small_of, weights)


@live_steps
def char_ffn_back_kernel(
    langs,
    blocks,
    first,
    after,
    hot,
    act,
    slope,
    inverse,
    upstream,
    small,
    weights,
    grad_to_word,
    grad_after,
    grads,
    sums_out,
    small_rows,
    grad_expand,
    grad_reduce,
    sums,
    up_rows,
    *spread_up,
):
    i = pl.program_id(0)
    width = after.shape[1]
    hidden = FOLD * width
    words = upstream.shape[0]

    @pl.when(i == 0)
    def _():
        small_rows[...] = small[...].astype(F32).T
        for k, part in enumerate(spread_up):
            cols = slice(k * GROUP, (k + 1) * GROUP)
            part[:words, :] = upstream[:, cols].astype(F32) * inverse[...]
            part[words:, :] = jnp.zeros((GROUP, GROUP), F32)
        grad_expand[...] = jnp.zeros_like(grad_expand)
        grad_reduce[...] = jnp.zeros_like(grad_reduce)
        sums[...] = jnp.zeros_like(sums)

    for g in range(SPLIT):
        here = slice(g * GROUP, (g + 1) * GROUP)
        for k, part in enumerate(spread_up):
            words_here = part[pl.ds(first[i * SPLIT + g], GROUP), :].astype(BF)
            up_rows[here, k * GROUP : (k + 1) * GROUP] = dot(hot[here, :], words_here).astype(BF)
    up = up_rows[...]
    unit, spread = norm_parts(after[...])
    gain = small_rows[langs + 2 : langs + 3, :]
    normed = (unit * gain + small_rows[langs + 3 : langs + 4, :]).astype(BF)
    grad_normed = jnp.zeros((BLOCK, width), F32)
    for j in range(FOLD):
        cols = slice(j * width, (j + 1) * width)
        grad_act = dot_t(up, weights[:, hidden + j * width : hidden + (j + 1) * width])
        grad_pre = grad_act * slope[:, cols].astype(F32)
        sums[8 * j : 8 * j + 8, :] += fold_rows(grad_pre)
        grad_pre = grad_pre.astype(BF)
        grad_normed = grad_normed + dot_t(grad_pre, weights[:, cols])
        grad_expand[:, cols] += t_dot(normed, grad_pre)
        grad_reduce[:, cols] += t_dot(up, act[:, cols])
    up_wide = up.astype(F32)
    sums[32:40, :] += fold_rows(grad_normed * unit)
    sums[40:48, :] += fold_rows(grad_normed)
    sums[48:56, :] += fold_rows(up_wide)
    grad_after[...] = up_wide + norm_back(unit, spread, grad_normed * gain)

    @pl.when(i == blocks[0] - 1)
    def _():
        grads[:, :hidden] = grad_expand[...].astype(BF)
        for j in range(FOLD):
            grads[:, hidden + j * width : hidden + (j + 1) * width] = (
                grad_reduce[:, j * width : (j + 1) * width].T.astype(BF)
            )
        grads[:, 2 * hidden :] = grad_to_word[...]
        sums_out[...] = sums[...]


def char_ffn_back(
    langs, blocks, first, after, hot, act, slope, inverse, upstream, small_of, weights, grad_to_word
):
    rows, width = after.shape
    words = inverse.shape[0]
    hidden = FOLD * width
    return pl.pallas_call(
        functools.partial(char_ffn_back_kernel, langs),
        out_shape=(
            jax.ShapeDtypeStruct((rows, width), F32),
            jax.ShapeDtypeStruct(weights.shape, BF),
            jax.ShapeDtypeStruct((64, width), F32),
        ),
        grid_spec=pltpu.PrefetchScalarGridSpec(
            num_scalar_prefetch=2,
            grid=(rows // BLOCK,),
            in_specs=[
                rows_spec(width),
                rows_spec(GROUP),
                rows_spec(hidden),
                rows_spec(hidden),
                full(inverse.shape),
                full(upstream.shape),
                pl.BlockSpec((width, SMALL), lambda i, *_: (0, 4 * width // SMALL)),
                full(weights.shape),
                full(grad_to_word.shape),
            ],
            out_specs=(rows_spec(width), full(weights.shape), full((64, width))),
            scratch_shapes=[
                pltpu.VMEM((SMALL, width), F32),
                pltpu.VMEM((width, hidden), F32),
                pltpu.VMEM((width, hidden), F32),
                pltpu.VMEM((64, width), F32),
                pltpu.VMEM((BLOCK, width), BF),
            ]
            + [pltpu.VMEM((words + GROUP, GROUP), F32)] * (width // GROUP),
        ),
        compiler_params=pltpu.CompilerParams(vmem_limit_bytes=48 * MIB),
        cost_estimate=pl.CostEstimate(
            flops=rows * width * width * 32, bytes_accessed=rows * width * 20, transcendentals=0
        ),
    )(blocks, first, after, hot, act, slope, inverse, upstream, small_of, weights, grad_to_word)


@live_steps
def char_attend_back_kernel(
    langs,
    blocks,
    rows_of,
    ids,
    packed,
    qkv,
    soft,
    mixed,
    grad_after,
    weights,
    sums_in,
    grads,
    *refs,
):
    i = pl.program_id(0)
    width = packed.shape[1]
    grad_start = refs[: width // GROUP]
    small_rows, grad_in, grad_out, sums, small_grads, grad_mixed, grad_qkv = refs[width // GROUP :]

    @pl.when(i == 0)
    def _():
        small_rows[...] = weights[:, 4 * width :].astype(F32).T
        grad_in[...] = jnp.zeros_like(grad_in)
        grad_out[...] = jnp.zeros_like(grad_out)
        sums[...] = jnp.zeros_like(sums)
        small_grads[...] = jnp.zeros_like(small_grads)

    start = with_language(i, rows_of, ids, packed, small_rows)
    unit, spread = norm_parts(start)
    gain = small_rows[langs : langs + 1, :]
    normed = (unit * gain + small_rows[langs + 1 : langs + 2, :]).astype(BF)
    after_low = grad_after[...].astype(BF)
    grad_out[...] += t_dot(mixed[...], after_low)
    grad_mixed[...] = dot_t(after_low, weights[:, 3 * width : 4 * width]).astype(BF)
    masks = head_masks(width, CHEADS)
    for g in range(SPLIT):
        here = slice(g * GROUP, (g + 1) * GROUP)
        low = grad_mixed[here, :]
        queries = qkv[here, :width]
        keys = stack_heads(qkv[here, width : 2 * width], masks)
        values = stack_heads(qkv[here, 2 * width :], masks)
        grad_soft = dot_t(low, values)
        parts = []
        grad_keys = jnp.zeros((GROUP, width), F32)
        grad_values = jnp.zeros((GROUP, width), F32)
        for h in range(CHEADS):
            cols = slice(h * GROUP, (h + 1) * GROUP)
            weight = soft[here, cols]
            wide = weight.astype(F32)
            one = grad_soft[:, cols]
            one = wide * (one - jnp.sum(wide * one, -1, keepdims=True))
            one = one.astype(BF)
            parts.append(one)
            grad_keys = grad_keys + t_dot(one, queries * masks[h])
            grad_values = grad_values + t_dot(weight, low * masks[h])
        grad_queries = dot(jnp.concatenate(parts, 1), keys)
        grad_qkv[here, :width] = (grad_queries * SCALE).astype(BF)
        grad_qkv[here, width : 2 * width] = (grad_keys * SCALE).astype(BF)
        grad_qkv[here, 2 * width :] = grad_values.astype(BF)
    grad_in[...] += t_dot(normed, grad_qkv[...])
    grad_normed = dot_t(grad_qkv[...], weights[:, : 3 * width])
    sums[0:8, :] += fold_rows(grad_normed * unit)
    sums[8:16, :] += fold_rows(grad_normed)
    result = grad_after[...] + norm_back(unit, spread, grad_normed * gain)
    for k, part in enumerate(grad_start):
        part[...] = result[:, k * GROUP : (k + 1) * GROUP]
    for g in range(SPLIT):
        line = pl.ds(ids[rows_of[i * SPLIT + g]], 1)
        part = jnp.sum(result[g * GROUP : (g + 1) * GROUP, :], 0, keepdims=True)
        small_grads[line, :] = small_grads[line, :] + part

    @pl.when(i == blocks[0] - 1)
    def _():
        def put(at, block):
            small_grads[langs + at : langs + at + 1, :] = jnp.sum(block, 0, keepdims=True)

        put(0, sums[0:8, :])
        put(1, sums[8:16, :])
        put(2, sums_in[32:40, :])
        put(3, sums_in[40:48, :])
        put(4, sums_in[48:56, :])
        for j in range(FOLD):
            put(5 + j, sums_in[8 * j : 8 * j + 8, :])
        grads[:, : 3 * width] = grad_in[...].astype(BF)
        grads[:, 3 * width : 4 * width] = grad_out[...].astype(BF)
        grads[:, 4 * width :] = small_grads[...].T.astype(BF)


def char_attend_back(langs, blocks, rows_of, ids, packed, qkv, soft, mixed, grad_after, weights, sums):
    rows, width = packed.shape
    return pl.pallas_call(
        functools.partial(char_attend_back_kernel, langs),
        out_shape=(
            jax.ShapeDtypeStruct(weights.shape, BF),
        )
        + (jax.ShapeDtypeStruct((rows + GROUP, GROUP), F32),) * (width // GROUP),
        grid_spec=pltpu.PrefetchScalarGridSpec(
            num_scalar_prefetch=3,
            grid=(rows // BLOCK,),
            in_specs=[
                rows_spec(width),
                rows_spec(3 * width),
                rows_spec(CHEADS * GROUP),
                rows_spec(width),
                rows_spec(width),
                full(weights.shape),
                full(sums.shape),
            ],
            out_specs=(full(weights.shape),) + (rows_spec(GROUP),) * (width // GROUP),
            scratch_shapes=[
                pltpu.VMEM((SMALL, width), F32),
                pltpu.VMEM((width, 3 * width), F32),
                pltpu.VMEM((width, width), F32),
                pltpu.VMEM((16, width), F32),
                pltpu.VMEM((SMALL, width), F32),
                pltpu.VMEM((BLOCK, width), BF),
                pltpu.VMEM((BLOCK, 3 * width), BF),
            ],
        ),
        compiler_params=pltpu.CompilerParams(vmem_limit_bytes=48 * MIB),
        cost_estimate=pl.CostEstimate(
            flops=rows * width * width * 24, bytes_accessed=rows * width * 20, transcendentals=0
        ),
    )(blocks, rows_of, ids, packed, qkv, soft, mixed, grad_after, weights, sums)


def word_kernel(
    place,
    pooled,
    to_word,
    weights,
    cotangent,
    words_out,
    grad_after_out,
    grad_query_out,
    grad_pair_out,
    normed_out,
    word_in_out,
    grads,
    sums_out,
    small_rows,
    word_all,
    normed_all,
    pair,
    query,
    blocked,
    soft_near,
    soft_far,
    mixed,
    after,
    unit_two,
    normed_two,
    up_low,
    total,
    grad_normed,
):
    member = place[0]
    length = place[1]
    all_words, _ = pooled.shape
    width = to_word.shape[1]
    own_words = cotangent.shape[0]
    local = own_words // 2
    half = all_words // 2
    hidden = FOLD * width
    reach = (half, all_words)
    at_in, at_out, at_expand, at_reduce = 0, 3 * width, 4 * width, 4 * width + hidden
    small_rows[...] = weights[:, 4 * width + 2 * hidden :].astype(F32).T

    def embed(t, carry):
        here = pl.ds(pl.multiple_of(t * local, local), local)
        value = dot(pooled[here, :], to_word[...]) + small_rows[5:6, :]
        word_all[here, :] = value
        unit, _ = norm_parts(value)
        normed = (unit * small_rows[0:1, :] + small_rows[1:2, :]).astype(BF)
        normed_all[here, :] = normed
        pair[here, :] = dot(normed, weights[:, width : 3 * width]).astype(BF)
        return carry

    lax.fori_loop(0, all_words // local, embed, 0)
    origin = []
    for t in range(2):
        base = pl.multiple_of(member * local + t * half, local)
        origin.append(base)
        here = slice(t * local, (t + 1) * local)
        word_in_out[here, :] = word_all[pl.ds(base, local), :]
        normed_out[here, :] = normed_all[pl.ds(base, local), :]
    query[...] = dot(normed_out[...], weights[:, :width]).astype(BF)
    masks = head_masks(GROUP, 2)
    softs = (soft_near, soft_far)

    for t in range(2):
        here = slice(t * local, (t + 1) * local)
        keys_seen = reach[t]
        seen = lax.broadcasted_iota(jnp.int32, (local, keys_seen), 1)
        asks = lax.broadcasted_iota(jnp.int32, (local, keys_seen), 0) + origin[t]
        blocked[:, :keys_seen] = jnp.where((seen <= asks) & (seen < length), 0.0, MASKED)

        def attend(p, carry):
            lanes = pl.ds(pl.multiple_of(p * GROUP, GROUP), GROUP)
            after_lanes = pl.ds(pl.multiple_of(width + p * GROUP, GROUP), GROUP)
            asking = query[here, lanes]
            keys = pair[:keys_seen, lanes]
            values = pair[:keys_seen, after_lanes]
            out = jnp.zeros((local, GROUP), F32)
            for h in range(2):
                scores = dot_t(asking * masks[h], keys) * SCALE + blocked[:, :keys_seen]
                scores = jnp.exp(scores - jnp.max(scores, -1, keepdims=True))
                soft = (scores * (1.0 / jnp.sum(scores, -1, keepdims=True))).astype(BF)
                softs[t][2 * p + h] = soft
                out = out + dot(soft, values * masks[h])
            mixed[here, lanes] = out.astype(BF)
            return carry

        lax.fori_loop(0, WHEADS // 2, attend, 0)

    value = word_in_out[...] + dot(mixed[...], weights[:, at_out : at_out + width])
    after[...] = value
    unit, spread = norm_parts(value)
    unit_two[...] = unit
    normed_two[...] = (unit * small_rows[2:3, :] + small_rows[3:4, :]).astype(BF)
    row = lax.broadcasted_iota(jnp.int32, (own_words, 1), 0)
    index = jnp.where(row < local, origin[0] + row, origin[1] + row - local)
    valid = index < length
    up_low[...] = jnp.where(valid, cotangent[...].astype(F32), 0.0).astype(BF)
    total[...] = jnp.zeros_like(total)
    grad_normed[...] = jnp.zeros_like(grad_normed)

    def feed(j, carry):
        expand = weights[:, pl.ds(pl.multiple_of(at_expand + j * width, GROUP), width)]
        shrink = weights[:, pl.ds(pl.multiple_of(at_reduce + j * width, GROUP), width)]
        pre = dot(normed_two[...], expand) + small_rows[pl.ds(6 + j, 1), :]
        act, slope = gelu_both(pre)
        act = act.astype(BF)
        total[...] += dot(act, shrink)
        grad_pre = dot_t(up_low[...], shrink) * slope
        sums_out[pl.ds(6 + j, 1), :] = jnp.sum(grad_pre, 0, keepdims=True)
        grad_pre = grad_pre.astype(BF)
        grad_normed[...] += dot_t(grad_pre, expand)
        cols = pl.multiple_of(j * width, GROUP)
        grads[:, pl.ds(cols, width)] = t_dot(normed_two[...], grad_pre).astype(BF)
        grads[:, pl.ds(pl.multiple_of(hidden + j * width, GROUP), width)] = t_dot(
            act, up_low[...]
        ).astype(BF)
        return carry

    lax.fori_loop(0, FOLD, feed, 0)
    words_out[...] = jnp.where(valid, after[...] + (total[...] + small_rows[4:5, :]), 0.0)
    upstream = up_low[...].astype(F32)
    incoming = grad_normed[...]
    sums_out[2:3, :] = jnp.sum(incoming * unit_two[...], 0, keepdims=True)
    sums_out[3:4, :] = jnp.sum(incoming, 0, keepdims=True)
    sums_out[4:5, :] = jnp.sum(upstream, 0, keepdims=True)
    grad_after = upstream + norm_back(unit_two[...], spread, incoming * small_rows[2:3, :])
    grad_after_out[...] = grad_after
    grad_low = grad_after.astype(BF)
    grads[:, 2 * hidden :] = t_dot(mixed[...], grad_low).astype(BF)
    mixed[...] = dot_t(grad_low, weights[:, at_out : at_out + width]).astype(BF)

    def attend_back(p, carry):
        lanes = pl.ds(pl.multiple_of(p * GROUP, GROUP), GROUP)
        after_lanes = pl.ds(pl.multiple_of(width + p * GROUP, GROUP), GROUP)
        grad_keys, grad_values = [], []
        for t in range(2):
            here = slice(t * local, (t + 1) * local)
            keys_seen = reach[t]
            asking = query[here, lanes]
            keys = pair[:keys_seen, lanes]
            values = pair[:keys_seen, after_lanes]
            incoming = mixed[here, lanes]
            grad_query = jnp.zeros((local, GROUP), F32)
            grad_key = jnp.zeros((keys_seen, GROUP), F32)
            grad_value = jnp.zeros((keys_seen, GROUP), F32)
            for h in range(2):
                soft = softs[t][2 * p + h]
                wide = soft.astype(F32)
                one = dot_t(incoming * masks[h], values)
                one = wide * (one - jnp.sum(wide * one, -1, keepdims=True))
                one = one.astype(BF)
                grad_query = grad_query + dot(one, keys * masks[h])
                grad_key = grad_key + t_dot(one, asking * masks[h])
                grad_value = grad_value + t_dot(soft, incoming * masks[h])
            grad_query_out[here, lanes] = (grad_query * SCALE).astype(BF)
            grad_keys.append(grad_key)
            grad_values.append(grad_value)
        for parts, at, factor in ((grad_keys, lanes, SCALE), (grad_values, after_lanes, 1.0)):
            grad_pair_out[:half, at] = ((parts[0] + parts[1][:half]) * factor).astype(BF)
            grad_pair_out[half:, at] = (parts[1][half:] * factor).astype(BF)
        return carry

    lax.fori_loop(0, WHEADS // 2, attend_back, 0)


def word_part(place, pooled, to_word, weights, cotangent):
    all_words, _ = pooled.shape
    width = to_word.shape[1]
    own = cotangent.shape[0]
    local = own // 2
    hidden = FOLD * width
    vmem = pl.BlockSpec(memory_space=pltpu.VMEM)
    return pl.pallas_call(
        word_kernel,
        out_shape=(
            jax.ShapeDtypeStruct((own, width), F32),
            jax.ShapeDtypeStruct((own, width), F32),
            jax.ShapeDtypeStruct((own, width), BF),
            jax.ShapeDtypeStruct((all_words, 2 * width), BF),
            jax.ShapeDtypeStruct((own, width), BF),
            jax.ShapeDtypeStruct((own, width), F32),
            jax.ShapeDtypeStruct((width, 2 * hidden + width), BF),
            jax.ShapeDtypeStruct((16, width), F32),
        ),
        in_specs=[pl.BlockSpec(memory_space=pltpu.SMEM), vmem, vmem, vmem, vmem],
        out_specs=(vmem,) * 8,
        scratch_shapes=[
            pltpu.VMEM((SMALL, width), F32),
            pltpu.VMEM((all_words, width), F32),
            pltpu.VMEM((all_words, width), BF),
            pltpu.VMEM((all_words, 2 * width), BF),
            pltpu.VMEM((own, width), BF),
            pltpu.VMEM((local, all_words), F32),
            pltpu.VMEM((WHEADS, local, all_words // 2), BF),
            pltpu.VMEM((WHEADS, local, all_words), BF),
            pltpu.VMEM((own, width), BF),
            pltpu.VMEM((own, width), F32),
            pltpu.VMEM((own, width), F32),
            pltpu.VMEM((own, width), BF),
            pltpu.VMEM((own, width), BF),
            pltpu.VMEM((own, width), F32),
            pltpu.VMEM((own, width), F32),
        ],
        compiler_params=pltpu.CompilerParams(vmem_limit_bytes=56 * MIB),
        cost_estimate=pl.CostEstimate(
            flops=own * width * width * 60, bytes_accessed=20 * MIB, transcendentals=own * 8192
        ),
    )(place, pooled, to_word, weights, cotangent)


def word_end_kernel(
    pooled,
    to_word,
    weights,
    small,
    grad_query,
    grad_pair,
    normed,
    word_in,
    grad_after,
    sums,
    grad_pooled,
    grad_to_word,
    grads,
    small_rows,
    small_grads,
    incoming,
):
    width = to_word.shape[1]
    small_rows[...] = small[...].astype(F32).T
    incoming[:, :width] = grad_query[...]
    incoming[:, width:] = grad_pair[...].astype(BF)
    grads[:, : 3 * width] = t_dot(normed[...], incoming[...]).astype(BF)
    grad_normed = dot_t(incoming[...], weights[...])
    unit, spread = norm_parts(word_in[...])
    small_grads[...] = jnp.zeros_like(small_grads)
    small_grads[0:1, :] = jnp.sum(grad_normed * unit, 0, keepdims=True)
    small_grads[1:2, :] = jnp.sum(grad_normed, 0, keepdims=True)
    small_grads[2:5, :] = sums[2:5, :]
    small_grads[6:10, :] = sums[6:10, :]
    value = grad_after[...] + norm_back(unit, spread, grad_normed * small_rows[0:1, :])
    small_grads[5:6, :] = jnp.sum(value, 0, keepdims=True)
    low = value.astype(BF)
    grad_to_word[...] = t_dot(pooled[...], low).astype(BF)
    grad_pooled[...] = dot_t(low, to_word[...]).astype(BF)
    grads[:, 3 * width :] = small_grads[...].T.astype(BF)


def word_end(pooled, to_word, weights, grad_query, grad_pair, normed, word_in, grad_after, sums):
    own, narrow = pooled.shape
    width = to_word.shape[1]
    columns = weights.shape[1]
    return pl.pallas_call(
        word_end_kernel,
        grid=(1,),
        out_shape=(
            jax.ShapeDtypeStruct((own, narrow), BF),
            jax.ShapeDtypeStruct((narrow, width), BF),
            jax.ShapeDtypeStruct((width, 3 * width + SMALL), BF),
        ),
        in_specs=[
            full(pooled.shape),
            full(to_word.shape),
            pl.BlockSpec((width, 3 * width), lambda i: (0, 0)),
            pl.BlockSpec((width, SMALL), lambda i: (0, columns // SMALL - 1)),
            full(grad_query.shape),
            full(grad_pair.shape),
            full(normed.shape),
            full(word_in.shape),
            full(grad_after.shape),
            full(sums.shape),
        ],
        out_specs=(full((own, narrow)), full((narrow, width)), full((width, 3 * width + SMALL))),
        scratch_shapes=[
            pltpu.VMEM((SMALL, width), F32),
            pltpu.VMEM((SMALL, width), F32),
            pltpu.VMEM((own, 3 * width), BF),
        ],
        compiler_params=pltpu.CompilerParams(vmem_limit_bytes=48 * MIB),
        cost_estimate=pl.CostEstimate(
            flops=own * width * width * 14, bytes_accessed=10 * MIB, transcendentals=0
        ),
    )(pooled, to_word, weights, weights, grad_query, grad_pair, normed, word_in, grad_after, sums)


def swap(values, axis, bit):
    count = lax.axis_size(axis)
    return lax.ppermute(values, axis, [(k, k ^ bit) for k in range(count)])


def bit_of(axis, bit):
    return lax.rem(lax.div(lax.axis_index(axis), bit), 2)


def bits_down(axis):
    count = lax.axis_size(axis)
    return [1 << k for k in reversed(range(count.bit_length() - 1))]


def ordered(mine, other, axis, bit, at):
    swapped = bit_of(axis, bit) == 1
    low = jnp.where(swapped, other, mine)
    high = jnp.where(swapped, mine, other)
    return jnp.stack([low, high], at)


def gather(shard):
    value = shard
    for axis in ("dp", "fsdp"):
        for bit in bits_down(axis):
            value = ordered(value, swap(value, axis, bit), axis, bit, value.ndim - 2)
    return value.reshape(-1, shard.shape[-1])


def scatter(value):
    steps = [(axis, bit) for axis in ("dp", "fsdp") for bit in bits_down(axis)]
    rows, columns = value.shape
    value = value.reshape([2] * len(steps) + [rows >> len(steps), columns])
    for axis, bit in reversed(steps):
        mine = bit_of(axis, bit)
        at = value.ndim - 3
        kept = lax.dynamic_index_in_dim(value, mine, at, keepdims=False)
        sent = lax.dynamic_index_in_dim(value, 1 - mine, at, keepdims=False)
        value = kept.astype(F32) + swap(sent, axis, bit).astype(F32)
        if value.ndim > 2:
            value = value.astype(BF)
    return value


def split_hidden(shard):
    rows, hidden = shard.shape
    return shard.reshape(rows, hidden // FOLD, FOLD).swapaxes(1, 2).reshape(rows, hidden)


def join_hidden(shard):
    rows, hidden = shard.shape
    return shard.reshape(rows, FOLD, hidden // FOLD).swapaxes(1, 2).reshape(rows, hidden)


def beside(columns):
    rows = columns[0].shape[0]
    small = jnp.concatenate(columns, 1)
    return jnp.pad(small, ((0, 0), (0, SMALL - small.shape[1])))


def body(
    char_inputs,
    language_ids,
    char_counts,
    row_lengths,
    cotangent,
    language_table,
    char_gain_one,
    char_bias_one,
    char_inward,
    char_outward,
    char_gain_two,
    char_bias_two,
    char_expand,
    char_expand_bias,
    char_reduce,
    char_reduce_bias,
    char_to_word,
    char_to_word_bias,
    word_gain_one,
    word_bias_one,
    word_inward,
    word_outward,
    word_gain_two,
    word_bias_two,
    word_expand,
    word_expand_bias,
    word_reduce,
    word_reduce_bias,
):
    rows, local, slots, width = char_inputs.shape
    words = rows * local
    langs = language_table.shape[0]
    wide = word_inward.shape[1] // 3
    share = lax.axis_size("fsdp")
    members = share // rows
    member = lax.rem(lax.axis_index("fsdp"), members)
    top = members
    my_row = bit_of("fsdp", top)

    def one(vector, like):
        return vector.reshape(like.shape[0], -1)

    attend_shard = jnp.concatenate(
        [
            char_inward,
            char_outward,
            beside(
                [language_table.T]
                + [
                    one(v, char_inward)
                    for v in (
                        char_gain_one,
                        char_bias_one,
                        char_gain_two,
                        char_bias_two,
                        char_reduce_bias,
                        char_expand_bias,
                    )
                ]
            ),
        ],
        1,
    )
    feed_shard = jnp.concatenate(
        [split_hidden(char_expand), one(char_reduce, char_inward), char_to_word], 1
    )
    word_shard = jnp.concatenate(
        [
            word_inward,
            word_outward,
            split_hidden(word_expand),
            one(word_reduce, word_inward),
            beside(
                [
                    one(v, word_inward)
                    for v in (
                        word_gain_one,
                        word_bias_one,
                        word_gain_two,
                        word_bias_two,
                        word_reduce_bias,
                        char_to_word_bias,
                        word_expand_bias,
                    )
                ]
            ),
        ],
        1,
    )
    attend_full = gather(attend_shard)
    feed_full = gather(feed_shard)
    word_full = lax.all_gather(word_shard, ("dp", "fsdp"), axis=0, tiled=True)
    to_word = feed_full[:, 2 * FOLD * width :]

    def pick(values, which):
        return lax.dynamic_index_in_dim(values, which, 0, keepdims=False)

    def to_rows(values):
        other = swap(pick(values, 1 - my_row), "fsdp", top)
        return ordered(pick(values, my_row), other, "fsdp", top, 0)

    cotangent_own = to_rows(cotangent)
    counts = char_counts.reshape(words)
    inverse = 1.0 / counts.astype(F32).reshape(words, 1)
    packed, bias, hot, offs, first, rows_of, blocks = pack(
        counts, char_inputs.reshape(words, slots, width), local
    )
    qkv, soft, mixed, after = char_attend(langs, blocks, rows_of, language_ids, packed, bias, attend_full)
    act, slope, pooled = char_ffn(langs, blocks, first, after, hot, inverse, attend_full, feed_full)

    pooled_own = to_rows(pooled.reshape(rows, local, width))
    pooled_all = pooled_own[:, None]
    for bit in [b for b in bits_down("fsdp") if b < members]:
        both = ordered(pooled_all, swap(pooled_all, "fsdp", bit), "fsdp", bit, 2)
        pooled_all = both.reshape(rows, -1, local, width)
    place = jnp.stack([member, pick(row_lengths, my_row)])
    (
        words_own,
        word_after_grad,
        query_grad,
        pair_grad,
        word_normed,
        word_in,
        word_grads,
        word_sums,
    ) = word_part(
        place,
        pooled_all.reshape(-1, width),
        to_word,
        word_full,
        cotangent_own.reshape(words, wide),
    )
    word_shares = scatter(word_grads)
    words_out = to_rows(words_own.reshape(rows, local, wide))
    pair_own = pair_grad.reshape(rows, members, local, 2 * wide)
    for bit in [b for b in bits_down("fsdp") if b < members]:
        halves = pair_own.reshape(rows, 2, -1, local, 2 * wide)
        mine = bit_of("fsdp", bit)
        kept = lax.dynamic_index_in_dim(halves, mine, 1, keepdims=False)
        sent = lax.dynamic_index_in_dim(halves, 1 - mine, 1, keepdims=False)
        pair_own = (kept.astype(F32) + swap(sent, "fsdp", bit).astype(F32)).astype(BF)
    pooled_grad, to_word_grad, inward_grads = word_end(
        pooled_own.reshape(words, width),
        to_word,
        word_full,
        query_grad,
        pair_own.reshape(words, 2 * wide),
        word_normed,
        word_in,
        word_after_grad,
        word_sums,
    )
    inward_shares = scatter(inward_grads)
    char_up = to_rows(pooled_grad.reshape(rows, local, width)).reshape(words, width)
    after_grad, feed_grads, char_sums = char_ffn_back(
        langs,
        blocks,
        first,
        after,
        hot,
        act,
        slope,
        inverse,
        char_up,
        attend_full,
        feed_full,
        to_word_grad,
    )
    feed_shares = scatter(feed_grads)
    attend_grads, *start_grad = char_attend_back(
        langs, blocks, rows_of, language_ids, packed, qkv, soft, mixed, after_grad, attend_full, char_sums
    )
    attend_shares = scatter(attend_grads)
    char_input_grad = unpack(offs, counts, start_grad, words, slots).reshape(char_inputs.shape)

    small = attend_shares[:, 4 * width :]
    word_small = inward_shares[:, 3 * wide :]
    hidden = FOLD * width
    wide_hidden = FOLD * wide

    def column(values, at, count=1):
        return values[:, at : at + count].reshape(-1)

    return (
        words_out,
        char_input_grad,
        small[:, :langs].T,
        column(small, langs),
        column(small, langs + 1),
        attend_shares[:, : 3 * width],
        attend_shares[:, 3 * width : 4 * width],
        column(small, langs + 2),
        column(small, langs + 3),
        join_hidden(feed_shares[:, :hidden]),
        column(small, langs + 5, FOLD),
        feed_shares[:, hidden : 2 * hidden].reshape(char_reduce.shape),
        column(small, langs + 4),
        feed_shares[:, 2 * hidden :],
        column(word_small, 5),
        column(word_small, 0),
        column(word_small, 1),
        inward_shares[:, : 3 * wide],
        word_shares[:, 2 * wide_hidden :],
        column(word_small, 2),
        column(word_small, 3),
        join_hidden(word_shares[:, :wide_hidden]),
        column(word_small, 6, FOLD),
        word_shares[:, wide_hidden : 2 * wide_hidden].reshape(word_reduce.shape),
        column(word_small, 4),
    )


def solution(mesh):
    both = ("dp", "fsdp")
    vector, matrix = P(both), P(both, None)
    weights = (
        (P(None, both), vector, vector, matrix, matrix, vector, vector)
        + (matrix, vector, matrix, vector, matrix, vector)
        + (vector, vector, matrix, matrix, vector, vector, matrix, vector, matrix, vector)
    )
    in_specs = (
        P("dp", "fsdp", None, None),
        P("dp"),
        P("dp", "fsdp"),
        P("dp"),
        P("dp", "fsdp", None),
    ) + weights
    out_specs = (P("dp", "fsdp", None), P("dp", "fsdp", None, None)) + weights
    return jax.shard_map(body, mesh=mesh, in_specs=in_specs, out_specs=out_specs, check_vma=False)
```

```python
import functools

import jax
import jax.numpy as jnp
from jax import lax
from jax.experimental import pallas as pl
from jax.experimental.pallas import tpu as pltpu
from jax.sharding import PartitionSpec as P

BF = jnp.bfloat16
F32 = jnp.float32
EPS = 1e-05
MASKED = -1e30
CHEADS = 4
WHEADS = 8
HEAD = 64
SCALE = HEAD ** (-0.5)
GROUP = 128
GROUP_BITS = 7
BLOCK = 1024
SPLIT = BLOCK // GROUP
FOLD = 4
SMALL = 128
GELU_A = 0.7978845608028654
GELU_B = 0.044715
MIB = 1024 * 1024
MEMBER, ROW, LENGTH, CORE, NEAR, FAR = range(6)


def columns_of(width):
    small = 4 * width
    expand = small + SMALL
    return small, expand, expand + FOLD * width, expand + 2 * FOLD * width


def dot(a, b):
    return jnp.dot(a, b, preferred_element_type=F32)


def dot_t(a, b):
    return lax.dot_general(a, b, (((1,), (1,)), ((), ())), preferred_element_type=F32)


def t_dot(a, b):
    return dot(a.T, b)


def norm_parts(hidden):
    centred = hidden - jnp.mean(hidden, -1, keepdims=True)
    spread = lax.rsqrt(jnp.mean(centred * centred, -1, keepdims=True) + EPS)
    return centred * spread, spread


def norm_back(unit, spread, gained):
    return (
        gained
        - jnp.mean(gained, -1, keepdims=True)
        - unit * jnp.mean(gained * unit, -1, keepdims=True)
    ) * spread


def gelu_both(pre):
    square = pre * pre
    turn = jnp.tanh(pre * (GELU_A + (GELU_A * GELU_B) * square))
    half = 0.5 + 0.5 * turn
    slope = half + pre * half * (1.0 - turn) * (GELU_A + (3.0 * GELU_A * GELU_B) * square)
    return pre * half, slope


def fold_rows(values):
    rows, width = values.shape
    return jnp.sum(values.reshape(rows // 8, 8, width), 0)


def head_masks(width, heads):
    lanes = lax.broadcasted_iota(jnp.int32, (1, width), 1) // HEAD
    return [(lanes == h).astype(F32).astype(BF) for h in range(heads)]


def run_blocks(step, begin, end, inputs, outputs):
    def one(*refs):
        step(begin + pl.program_id(0), *refs)

    def spec(ref):
        return pl.BlockSpec((BLOCK, ref.shape[1]), lambda i: (begin + i, 0))

    pltpu.emit_pipeline(
        one,
        grid=(end - begin,),
        in_specs=[spec(ref) for ref in inputs],
        out_specs=[spec(ref) for ref in outputs],
    )(*inputs, *outputs)


def streamed(kernel, scalars, streams, fixed, stream_outs, fixed_outs, scratch, cost, aliases=None):
    hbm = pl.BlockSpec(memory_space=pltpu.HBM)
    return pl.pallas_call(
        kernel,
        out_shape=tuple(jax.ShapeDtypeStruct(*out) for out in tuple(stream_outs) + tuple(fixed_outs)),
        grid_spec=pltpu.PrefetchScalarGridSpec(
            num_scalar_prefetch=len(scalars),
            grid=(1,),
            in_specs=[hbm] * len(streams) + [full(one.shape) for one in fixed],
            out_specs=(hbm,) * len(stream_outs) + tuple(full(shape) for shape, _ in fixed_outs),
            scratch_shapes=[pltpu.VMEM(*one) for one in scratch],
        ),
        input_output_aliases=aliases or {},
        compiler_params=pltpu.CompilerParams(vmem_limit_bytes=60 * MIB),
        cost_estimate=cost,
    )(*scalars, *streams, *fixed)


def full(shape):
    return pl.BlockSpec(shape, lambda *_: (0,) * len(shape))


def offsets_kernel(per_row, counts, offs, first, rows_of, blocks):
    words = counts.shape[0]

    def clear(g, carry):
        first[g] = 0
        rows_of[g] = 0
        return carry

    lax.fori_loop(0, first.shape[0], clear, 0, unroll=True)
    spare = first.shape[0] - 1

    def place(row, w, at):
        live = counts[w]
        inside = at & (GROUP - 1)
        at = jnp.where(inside + live > GROUP, at - inside + GROUP, at)
        group = jnp.where((at & (GROUP - 1)) == 0, at >> GROUP_BITS, spare)
        first[group] = w
        rows_of[group] = row
        offs[w] = at
        return at + live

    at = 0
    for row in range(words // per_row):
        at = lax.fori_loop(row * per_row, (row + 1) * per_row, functools.partial(place, row), at, unroll=8)
        at = ((at + (GROUP - 1)) >> GROUP_BITS) << GROUP_BITS
    blocks[0] = lax.div(at + (BLOCK - 1), BLOCK)


def group_count(words, slots, per_row):
    groups = (words * slots) // (GROUP - slots + 1) + 1 + words // per_row
    return -(-groups // SPLIT) * SPLIT


def offsets(counts, slots, per_row):
    words = counts.shape[0]
    groups = group_count(words, slots, per_row)
    smem = pl.BlockSpec(memory_space=pltpu.SMEM)
    sizes = (words, groups + 1, groups + 1, 1)
    return pl.pallas_call(
        functools.partial(offsets_kernel, per_row),
        out_shape=tuple(jax.ShapeDtypeStruct((size,), jnp.int32) for size in sizes),
        in_specs=[smem],
        out_specs=(smem,) * 4,
        cost_estimate=pl.CostEstimate(flops=words * 4000, bytes_accessed=12 * MIB, transcendentals=0),
    )(counts)


def pack_kernel(counts, offs, first, blocks, chars, packed_all, bias_all, hot_all, tags, *wide):
    words, slots, width = chars.shape
    slot = lax.broadcasted_iota(jnp.int32, (slots, GROUP), 0)

    def clear_rows(k, carry):
        there = pl.ds(pl.multiple_of(k * GROUP, GROUP), GROUP)
        for part in wide:
            part[there, :] = jnp.zeros((GROUP, GROUP), F32)
        tags[there, :] = jnp.full((GROUP, GROUP), -1.0, F32)
        return carry

    lax.fori_loop(0, blocks[0] * SPLIT, clear_rows, 0)

    def place(w, carry):
        at = offs[w]
        for k, part in enumerate(wide):
            part[pl.ds(at, slots), :] = chars[w, :, k * GROUP : (k + 1) * GROUP].astype(F32)
        tags[pl.ds(at, slots), :] = jnp.where(slot < counts[w], w.astype(F32), -1.0)
        return carry

    lax.fori_loop(0, words, place, 0, unroll=8)
    lane = lax.broadcasted_iota(jnp.int32, (GROUP, GROUP), 1).astype(F32)

    def step(i, packed, bias, hot):
        for g in range(SPLIT):
            here = slice(g * GROUP, (g + 1) * GROUP)
            there = pl.ds(pl.multiple_of((i * SPLIT + g) * GROUP, GROUP), GROUP)
            tag = tags[there, :]
            bias[here, :] = jnp.where(tag == tag.T, 0.0, MASKED).astype(BF)
            hot[here, :] = (tag - first[i * SPLIT + g].astype(F32) == lane).astype(F32).astype(BF)
            for k, part in enumerate(wide):
                packed[here, k * GROUP : (k + 1) * GROUP] = part[there, :].astype(BF)

    run_blocks(step, 0, blocks[0], (), (packed_all, bias_all, hot_all))


def pack(counts, offs, first, blocks, chars, per_row):
    words, slots, width = chars.shape
    rows = group_count(words, slots, per_row) * GROUP
    return streamed(
        pack_kernel,
        (counts, offs, first, blocks),
        (),
        (chars,),
        (((rows, width), BF), ((rows, GROUP), BF), ((rows, GROUP), BF)),
        (),
        (((rows + GROUP, GROUP), F32),) * (1 + width // GROUP),
        pl.CostEstimate(flops=rows * width * 4, bytes_accessed=rows * width * 10, transcendentals=0),
    )


def unpack_kernel(begin, offs, counts, *refs):
    out = refs[-1]
    slots, width = out.shape[1:]
    packed = refs[: width // GROUP]
    here = begin + pl.program_id(0) * out.shape[0]
    slot = lax.broadcasted_iota(jnp.int32, (slots, GROUP), 0)

    def take(k, carry):
        w = here + k
        for j, part in enumerate(packed):
            rows = part[pl.ds(offs[w], slots), :]
            out[k, :, j * GROUP : (j + 1) * GROUP] = jnp.where(slot < counts[w], rows, 0.0)
        return carry

    lax.fori_loop(0, out.shape[0], take, 0, unroll=8)


def unpack(offs, counts, packed, slots, before=None):
    words = counts.shape[0]
    width = len(packed) * GROUP
    step = words // 8
    begin = 0 if before is None else 4
    extra = [] if before is None else [before]
    return pl.pallas_call(
        functools.partial(unpack_kernel, begin * step),
        out_shape=jax.ShapeDtypeStruct((words, slots, width), F32),
        grid_spec=pltpu.PrefetchScalarGridSpec(
            num_scalar_prefetch=2,
            grid=(4,),
            in_specs=[full(part.shape) for part in packed] + [pl.BlockSpec(memory_space=pltpu.HBM)] * len(extra),
            out_specs=pl.BlockSpec((step, slots, width), lambda i, *_: (begin + i, 0, 0)),
        ),
        input_output_aliases={2 + len(packed): 0} if extra else {},
        compiler_params=pltpu.CompilerParams(vmem_limit_bytes=60 * MIB),
        cost_estimate=pl.CostEstimate(
            flops=words * slots * width, bytes_accessed=words * slots * width * 4, transcendentals=0
        ),
    )(offs, counts, *packed, *extra)


def with_language(i, rows_of, ids, packed, small_rows):
    parts = []
    for g in range(SPLIT):
        row = small_rows[pl.ds(ids[rows_of[i * SPLIT + g]], 1), :]
        parts.append(packed[g * GROUP : (g + 1) * GROUP, :].astype(F32) + row)
    return jnp.concatenate(parts, 0)


def both_heads(values, lower):
    wide = values.astype(F32)
    return jnp.concatenate([jnp.where(lower, wide, 0.0), jnp.where(lower, 0.0, wide)], 0).astype(BF)


def pick_heads(stacked, lower):
    rows = stacked.shape[0] // 2
    return jnp.where(lower, stacked[:rows], stacked[rows:])


def char_attend_kernel(
    langs,
    blocks,
    rows_of,
    ids,
    packed_all,
    bias_all,
    weights,
    qkv_all,
    soft_all,
    mixed_all,
    after_all,
    small_rows,
):
    width = packed_all.shape[1]
    small_rows[...] = weights[:, 4 * width : 4 * width + SMALL].astype(F32).T

    def step(i, packed, bias, qkv_out, soft_out, mixed_out, after_out):
        start = with_language(i, rows_of, ids, packed, small_rows)
        unit, _ = norm_parts(start)
        normed = (unit * small_rows[langs : langs + 1, :] + small_rows[langs + 1 : langs + 2, :]).astype(BF)
        qkv_out[...] = dot(normed, weights[:, : 3 * width]).astype(BF)
        lower = lax.broadcasted_iota(jnp.int32, (GROUP, GROUP), 1) < HEAD
        places = [(slice(g * GROUP, (g + 1) * GROUP), t) for g in range(SPLIT) for t in range(CHEADS // 2)]
        scores = []
        for here, t in places:
            tile = slice(t * GROUP, (t + 1) * GROUP)
            keys = both_heads(qkv_out[here, width + t * GROUP : width + (t + 1) * GROUP], lower)
            scores.append(dot_t(keys, qkv_out[here, tile]))
        softs = []
        for (here, t), score in zip(places, scores):
            blocked = bias[here, :].astype(F32)
            for h in range(2):
                one = score[h * GROUP : (h + 1) * GROUP] * SCALE + blocked
                one = jnp.exp(one - jnp.max(one, 0, keepdims=True))
                one = (one * (1.0 / jnp.sum(one, 0, keepdims=True))).astype(BF)
                soft_out[here, (2 * t + h) * GROUP : (2 * t + h + 1) * GROUP] = one
                softs.append(one)
        for k, (here, t) in enumerate(places):
            values = qkv_out[here, 2 * width + t * GROUP : 2 * width + (t + 1) * GROUP]
            mixed = dot(jnp.concatenate([softs[2 * k].T, softs[2 * k + 1].T], 0), values)
            mixed_out[here, t * GROUP : (t + 1) * GROUP] = pick_heads(mixed, lower).astype(BF)
        after_out[...] = start + dot(mixed_out[...], weights[:, 3 * width : 4 * width])

    run_blocks(step, 0, blocks[0], (packed_all, bias_all), (qkv_all, soft_all, mixed_all, after_all))


def char_attend(langs, blocks, rows_of, ids, packed, bias, weights):
    rows, width = packed.shape
    return streamed(
        functools.partial(char_attend_kernel, langs),
        (blocks, rows_of, ids),
        (packed, bias),
        (weights,),
        (
            ((rows, 3 * width), BF),
            ((rows, CHEADS * GROUP), BF),
            ((rows, width), BF),
            ((rows, width), F32),
        ),
        (),
        (((SMALL, width), F32),),
        pl.CostEstimate(
            flops=rows * width * width * 12, bytes_accessed=rows * width * 12, transcendentals=rows * 512
        ),
    )


def char_ffn_kernel(
    langs,
    blocks,
    first,
    place,
    after_all,
    hot_all,
    inverse,
    weights,
    act_all,
    slope_all,
    kept_out,
    sent_out,
    small_rows,
    *total,
):
    width = after_all.shape[1]
    at_small, at_expand, at_reduce, _ = columns_of(width)
    small_rows[...] = weights[:, at_small : at_small + SMALL].astype(F32).T
    for part in total:
        part[...] = jnp.zeros_like(part)

    def step(i, after, hot, act_out, slope_out):
        unit, _ = norm_parts(after[...])
        normed = (unit * small_rows[langs + 2 : langs + 3, :] + small_rows[langs + 3 : langs + 4, :]).astype(BF)
        out = after[...] + small_rows[langs + 4 : langs + 5, :]
        pres = [dot(normed, weights[:, at_expand + j * width : at_expand + (j + 1) * width]) for j in range(FOLD)]
        acts = []
        for j, pre in enumerate(pres):
            cols = slice(j * width, (j + 1) * width)
            act, slope = gelu_both(pre + small_rows[langs + 5 + j : langs + 6 + j, :])
            act = act.astype(BF)
            act_out[:, cols] = act
            slope_out[:, cols] = slope.astype(BF)
            acts.append(act)
        for j, act in enumerate(acts):
            out = out + dot(act, weights[:, at_reduce + j * width : at_reduce + (j + 1) * width])
        out = out.astype(BF)
        for g in range(SPLIT):
            here = slice(g * GROUP, (g + 1) * GROUP)
            words = pl.ds(first[i * SPLIT + g], GROUP)
            found = t_dot(hot[here, :], out[here, :])
            for k, part in enumerate(total):
                part[words, :] = part[words, :] + found[:, k * GROUP : (k + 1) * GROUP]

    run_blocks(step, 0, blocks[0], (after_all, hot_all), (act_all, slope_all))
    local = kept_out.shape[0]
    for out_ref, row in ((kept_out, place[ROW]), (sent_out, 1 - place[ROW])):
        there = pl.ds(pl.multiple_of(row * local, local), local)
        for k, part in enumerate(total):
            out_ref[:, k * GROUP : (k + 1) * GROUP] = (part[there, :] * inverse[there, :]).astype(BF)


def char_ffn(langs, blocks, first, place, after, hot, inverse, weights):
    rows, width = after.shape
    words = inverse.shape[0]
    hidden = FOLD * width
    return streamed(
        functools.partial(char_ffn_kernel, langs),
        (blocks, first, place),
        (after, hot),
        (inverse, weights),
        (((rows, hidden), BF), ((rows, hidden), BF)),
        (((words // 2, width), BF), ((words // 2, width), BF)),
        (((SMALL, width), F32),) + (((words + GROUP, GROUP), F32),) * (width // GROUP),
        pl.CostEstimate(
            flops=rows * width * width * 16, bytes_accessed=rows * width * 20, transcendentals=rows * 1024
        ),
    )


def sorted_rows(core, counts, rows, cuts=1, which=0):
    far, near = counts
    each = rows // (2 * far * near)
    some = each // cuts
    low = near // 2
    line = lax.broadcasted_iota(jnp.int32, (rows // (2 * cuts), rows), 0)
    inner = lax.rem(line, some)
    part = lax.div(line, some)
    at_far, at_near = lax.rem(part, far), lax.div(part, far)
    device = ((at_far * 2 + lax.div(at_near, low)) * low + lax.rem(at_near, low)) * 2 + core
    source = device * each + which * some + inner
    return (source == lax.broadcasted_iota(jnp.int32, source.shape, 1)).astype(F32).astype(BF)


def folding(back):
    size = FOLD * HEAD
    unit = lax.broadcasted_iota(jnp.int32, (size, size), 1 if back else 0)
    held = lax.broadcasted_iota(jnp.int32, (size, size), 0 if back else 1)
    return (held == (unit & (FOLD - 1)) * HEAD + lax.div(unit, FOLD)).astype(F32).astype(BF)


def unfold_into(out, folded, width):
    size = FOLD * HEAD
    matrix = folding(True)
    for m in range(width // HEAD):
        near = [folded[:, j * width + m * HEAD : j * width + (m + 1) * HEAD] for j in range(FOLD)]
        out[:, m * size : (m + 1) * size] = dot(jnp.concatenate(near, 1), matrix).astype(BF)


def char_ffn_back_kernel(
    settings,
    blocks,
    first,
    place,
    after_all,
    hot_all,
    act_all,
    slope_all,
    inverse,
    up_kept,
    up_sent,
    weights,
    grad_to_word,
    riding_kept,
    riding_sent,
    grad_after_all,
    kept_out,
    sent_out,
    sums,
    small_rows,
    grad_expand,
    grad_reduce,
    up_rows,
    grads,
    *spread_up,
):
    langs, counts = settings
    width = after_all.shape[1]
    hidden = FOLD * width
    local = up_kept.shape[0]
    at_small, at_expand, at_reduce, _ = columns_of(width)
    small_rows[...] = weights[:, at_small : at_small + SMALL].astype(F32).T
    for up_in, row in ((up_kept, place[ROW]), (up_sent, 1 - place[ROW])):
        there = pl.ds(pl.multiple_of(row * local, local), local)
        for k, part in enumerate(spread_up):
            cols = slice(k * GROUP, (k + 1) * GROUP)
            part[there, :] = up_in[:, cols].astype(F32) * inverse[there, :]
    for part in spread_up:
        part[2 * local :, :] = jnp.zeros((GROUP, GROUP), F32)
    grad_expand[...] = jnp.zeros_like(grad_expand)
    grad_reduce[...] = jnp.zeros_like(grad_reduce)
    sums[...] = jnp.zeros_like(sums)

    def step(i, after, hot, act, slope, grad_after):
        for g in range(SPLIT):
            here = slice(g * GROUP, (g + 1) * GROUP)
            for k, part in enumerate(spread_up):
                words_here = part[pl.ds(first[i * SPLIT + g], GROUP), :].astype(BF)
                up_rows[here, k * GROUP : (k + 1) * GROUP] = dot(hot[here, :], words_here).astype(BF)
        up = up_rows[...]
        unit, spread = norm_parts(after[...])
        gain = small_rows[langs + 2 : langs + 3, :]
        normed = (unit * gain + small_rows[langs + 3 : langs + 4, :]).astype(BF)
        grad_normed = jnp.zeros((BLOCK, width), F32)
        parts = [slice(j * width, (j + 1) * width) for j in range(FOLD)]
        grad_acts = [
            dot_t(up, weights[:, at_reduce + j * width : at_reduce + (j + 1) * width]) for j in range(FOLD)
        ]
        grad_pres = []
        for j, cols in enumerate(parts):
            grad_pre = grad_acts[j] * slope[:, cols].astype(F32)
            sums[8 * j : 8 * j + 8, :] += fold_rows(grad_pre)
            grad_pres.append(grad_pre.astype(BF))
        for j, grad_pre in enumerate(grad_pres):
            grad_normed = grad_normed + dot_t(
                grad_pre, weights[:, at_expand + j * width : at_expand + (j + 1) * width]
            )
        turned = normed.T
        for cols, grad_pre in zip(parts, grad_pres):
            grad_expand[:, cols] += dot(turned, grad_pre)
        turned = up.T
        for cols in parts:
            grad_reduce[:, cols] += dot(turned, act[:, cols])
        up_wide = up.astype(F32)
        sums[32:40, :] += fold_rows(grad_normed * unit)
        sums[40:48, :] += fold_rows(grad_normed)
        sums[48:56, :] += fold_rows(up_wide)
        grad_after[...] = up_wide + norm_back(unit, spread, grad_normed * gain)

    run_blocks(step, 0, blocks[0], (after_all, hot_all, act_all, slope_all), (grad_after_all,))
    unfold_into(grads.at[:, :hidden], grad_expand[...].astype(BF), width)
    for j in range(FOLD):
        grads[:, hidden + j * width : hidden + (j + 1) * width] = (
            grad_reduce[:, j * width : (j + 1) * width].T.astype(BF)
        )
    grads[:, 2 * hidden :] = grad_to_word[...]
    own = grads.shape[1]
    for out_ref, riding, core in (
        (kept_out, riding_kept, place[CORE]),
        (sent_out, riding_sent, 1 - place[CORE]),
    ):
        out_ref[:, :own] = dot(sorted_rows(core, counts, width), grads[...]).astype(BF)
        out_ref[:, own:] = riding[...]


def char_ffn_back(
    settings,
    blocks,
    first,
    place,
    after,
    hot,
    act,
    slope,
    inverse,
    up_kept,
    up_sent,
    weights,
    grad_to_word,
    riding,
):
    rows, width = after.shape
    words = inverse.shape[0]
    hidden = FOLD * width
    columns = 2 * hidden + grad_to_word.shape[1]
    return streamed(
        functools.partial(char_ffn_back_kernel, settings),
        (blocks, first, place),
        (after, hot, act, slope),
        (inverse, up_kept, up_sent, weights, grad_to_word, *riding),
        (((rows, width), F32),),
        (((width // 2, columns + riding[0].shape[1]), BF),) * 2 + (((64, width), F32),),
        (
            ((SMALL, width), F32),
            ((width, hidden), F32),
            ((width, hidden), F32),
            ((BLOCK, width), BF),
            ((width, columns), BF),
        )
        + (((words + GROUP, GROUP), F32),) * (width // GROUP),
        pl.CostEstimate(
            flops=rows * width * width * 32, bytes_accessed=rows * width * 20, transcendentals=0
        ),
    )


def char_attend_back_kernel(settings, blocks, rows_of, ids, place, *refs):
    langs, counts, is_second = settings
    packed_all, qkv_all, soft_all, mixed_all, grad_after_all = refs[:5]
    width = packed_all.shape[1]
    halves = width // GROUP
    refs = refs[5 + (halves if is_second else 0) :]
    weights, sums_in, refs = refs[0], refs[1], refs[2:]
    if is_second:
        grad_in_before, lines_before, refs = refs[0], refs[1], refs[2:]
    start_all, refs = refs[:halves], refs[halves:]
    if is_second:
        kept_out, sent_out, small_rows, grad_mixed, grad_qkv, grad_in, lines, grads = refs
        grad_in[...] = grad_in_before[...]
        lines[...] = lines_before[...]
    else:
        grad_in, lines, small_rows, grad_mixed, grad_qkv = refs
        grad_in[...] = jnp.zeros_like(grad_in)
        lines[...] = jnp.zeros_like(lines)
    half = (blocks[0] + 1) >> 1
    begin, end = (half, blocks[0]) if is_second else (0, half)
    small_rows[...] = weights[:, 4 * width : 4 * width + SMALL].astype(F32).T

    def step(i, packed, qkv, soft, mixed, grad_after, *grad_start):
        start = with_language(i, rows_of, ids, packed, small_rows)
        unit, spread = norm_parts(start)
        gain = small_rows[langs : langs + 1, :]
        normed = (unit * gain + small_rows[langs + 1 : langs + 2, :]).astype(BF)
        after_low = grad_after[...].astype(BF)
        grad_in[:, 3 * width :] += t_dot(mixed[...], after_low)
        grad_mixed[...] = dot_t(after_low, weights[:, 3 * width : 4 * width]).astype(BF)
        lower = lax.broadcasted_iota(jnp.int32, (GROUP, GROUP), 1) < HEAD
        places = [(slice(g * GROUP, (g + 1) * GROUP), t) for g in range(SPLIT) for t in range(CHEADS // 2)]

        def tile_of(values, which, k):
            here, t = places[k]
            return values[here, which * width + t * GROUP : which * width + (t + 1) * GROUP]

        every = range(len(places))
        lows = [both_heads(tile_of(grad_mixed, 0, k), lower) for k in every]
        grad_softs = [dot_t(tile_of(qkv, 2, k), lows[k]) for k in every]
        weights_of = [soft[here, 2 * t * GROUP : (2 * t + 2) * GROUP] for here, t in places]
        ones = []
        for weight, grad_soft in zip(weights_of, grad_softs):
            wide = weight.astype(F32)
            ones.append((wide * (grad_soft - jnp.sum(wide * grad_soft, 0, keepdims=True))).astype(BF))
        for k, (here, t) in enumerate(places):
            value = dot(weights_of[k], lows[k])
            grad_qkv[here, 2 * width + t * GROUP : 2 * width + (t + 1) * GROUP] = value.astype(BF)
        for k, (here, t) in enumerate(places):
            value = dot(ones[k], both_heads(tile_of(qkv, 0, k), lower))
            grad_qkv[here, width + t * GROUP : width + (t + 1) * GROUP] = (value * SCALE).astype(BF)
        for k, (here, t) in enumerate(places):
            turned = jnp.concatenate([ones[k][:, :GROUP].T, ones[k][:, GROUP:].T], 1)
            value = dot(turned, both_heads(tile_of(qkv, 1, k), lower))
            grad_qkv[here, t * GROUP : (t + 1) * GROUP] = (value * SCALE).astype(BF)
        grad_in[:, : 3 * width] += t_dot(normed, grad_qkv[...])
        grad_normed = dot_t(grad_qkv[...], weights[:, : 3 * width])
        lines[SMALL : SMALL + 8, :] += fold_rows(grad_normed * unit)
        lines[SMALL + 8 :, :] += fold_rows(grad_normed)
        result = grad_after[...] + norm_back(unit, spread, grad_normed * gain)
        for k, part in enumerate(grad_start):
            part[...] = result[:, k * GROUP : (k + 1) * GROUP]
        for g in range(SPLIT):
            line = pl.ds(ids[rows_of[i * SPLIT + g]], 1)
            part = jnp.sum(result[g * GROUP : (g + 1) * GROUP, :], 0, keepdims=True)
            lines[line, :] = lines[line, :] + part

    run_blocks(step, begin, end, (packed_all, qkv_all, soft_all, mixed_all, grad_after_all), start_all)
    if is_second:

        def put(at, block):
            lines[langs + at : langs + at + 1, :] = jnp.sum(block, 0, keepdims=True)

        put(0, lines[SMALL : SMALL + 8, :])
        put(1, lines[SMALL + 8 :, :])
        put(2, sums_in[32:40, :])
        put(3, sums_in[40:48, :])
        put(4, sums_in[48:56, :])
        for j in range(FOLD):
            put(5 + j, sums_in[8 * j : 8 * j + 8, :])
        grads[:, : 4 * width] = grad_in[...].astype(BF)
        grads[:, 4 * width :] = lines[:SMALL, :].T.astype(BF)
        kept_out[...] = dot(sorted_rows(place[CORE], counts, width), grads[...]).astype(BF)
        sent_out[...] = dot(sorted_rows(1 - place[CORE], counts, width), grads[...]).astype(BF)


def char_attend_back(
    settings, blocks, rows_of, ids, place, packed, qkv, soft, mixed, grad_after, weights, sums, before=None
):
    rows, width = packed.shape
    columns = 4 * width + SMALL
    halves = width // GROUP
    is_second = before is not None
    streams = (packed, qkv, soft, mixed, grad_after)
    fixed = (weights, sums)
    grad_in = ((width, 4 * width), F32)
    lines = ((SMALL + 16, width), F32)
    scratch = (
        ((SMALL, width), F32),
        ((BLOCK, width), BF),
        ((BLOCK, 3 * width), BF),
    )
    aliases = {}
    fixed_outs = (grad_in, lines)
    if is_second:
        aliases = {4 + len(streams) + k: k for k in range(halves)}
        streams += tuple(before[:halves])
        fixed += tuple(before[halves:])
        scratch += (grad_in, lines, ((width, columns), BF))
        fixed_outs = (((width // 2, columns), BF),) * 2
    return streamed(
        functools.partial(char_attend_back_kernel, settings + (is_second,)),
        (blocks, rows_of, ids, place),
        streams,
        fixed,
        (((rows + GROUP, GROUP), F32),) * halves,
        fixed_outs,
        scratch,
        pl.CostEstimate(
            flops=rows * width * width * 12, bytes_accessed=rows * width * 10, transcendentals=0
        ),
        aliases,
    )


def word_kernel(
    counts,
    members,
    place,
    char_weights,
    weights,
    cotangent,
    cotangent_other,
    *refs,
):
    pieces, refs = refs[: 2 * members], refs[2 * members :]
    words_both, words_sent, grad_after_out, grad_query_out, normed_out, word_in_out = refs[:6]
    kept_out, sent_out, sums_out = refs[6:9]
    pair_outs, refs = refs[9 : 9 + members], refs[9 + members :]
    (
        small_rows,
        pooled,
        word_all,
        normed_all,
        pair,
        query,
        blocked,
        soft_near,
        soft_far,
        mixed,
        after,
        unit_two,
        normed_two,
        up_low,
        total,
        grad_normed,
        grads,
        natural,
        grad_pair,
    ) = refs
    member = place[MEMBER]
    my_row = place[ROW]
    length = place[LENGTH]
    all_words, narrow = pooled.shape
    width = up_low.shape[1]
    at_to_word = columns_of(narrow)[3]
    own_words = up_low.shape[0]
    local = own_words // 2
    half = all_words // 2
    hidden = FOLD * width
    reach = (half, all_words)
    at_out, at_expand, at_reduce = 3 * width, 4 * width, 4 * width + hidden
    small_rows[...] = weights[:, 4 * width + 2 * hidden :].astype(F32).T

    def rows_at(index):
        return pl.ds(pl.multiple_of(index * local, local), local)

    for m in range(members):
        there = jnp.bitwise_xor(member, m)
        pooled[rows_at(my_row * members + there), :] = pieces[2 * m][...]
        pooled[rows_at((1 - my_row) * members + there), :] = pieces[2 * m + 1][...]

    def embed(t, carry):
        here = pl.ds(pl.multiple_of(t * local, local), local)
        value = dot(pooled[here, :], char_weights[:, at_to_word:]) + small_rows[5:6, :]
        word_all[here, :] = value
        unit, _ = norm_parts(value)
        normed = (unit * small_rows[0:1, :] + small_rows[1:2, :]).astype(BF)
        normed_all[here, :] = normed
        pair[here, :] = dot(normed, weights[:, width : 3 * width]).astype(BF)
        return carry

    lax.fori_loop(0, all_words // local, embed, 0)
    origin = []
    for t in range(2):
        base = member * local + t * half
        origin.append(base)
        here = slice(t * local, (t + 1) * local)
        word_in_out[here, :] = word_all[rows_at(member + t * members), :]
        normed_out[here, :] = normed_all[rows_at(member + t * members), :]
    query[...] = dot(normed_out[...], weights[:, :width]).astype(BF)
    masks = head_masks(GROUP, 2)
    softs = (soft_near, soft_far)

    for t in range(2):
        seen = lax.broadcasted_iota(jnp.int32, (local, reach[t]), 1)
        asks = lax.broadcasted_iota(jnp.int32, (local, reach[t]), 0) + origin[t]
        blocked[t * local : (t + 1) * local, : reach[t]] = jnp.where((seen <= asks) & (seen < length), 0.0, MASKED)
    chains = [(slice(t * local, (t + 1) * local), t, h) for t in range(2) for h in range(2)]

    def attend(p, carry):
        lanes = pl.ds(pl.multiple_of(p * GROUP, GROUP), GROUP)
        after_lanes = pl.ds(pl.multiple_of(width + p * GROUP, GROUP), GROUP)
        scores = [dot_t(query[here, lanes] * masks[h], pair[: reach[t], lanes]) for here, t, h in chains]
        weights_of = []
        for (here, t, h), score in zip(chains, scores):
            score = score * SCALE + blocked[here, : reach[t]]
            score = jnp.exp(score - jnp.max(score, -1, keepdims=True))
            soft = (score * (1.0 / jnp.sum(score, -1, keepdims=True))).astype(BF)
            softs[t][2 * p + h] = soft
            weights_of.append(soft)
        outs = [
            dot(soft, pair[: reach[t], after_lanes] * masks[h])
            for (_, t, h), soft in zip(chains, weights_of)
        ]
        for t in range(2):
            mixed[t * local : (t + 1) * local, lanes] = (outs[2 * t] + outs[2 * t + 1]).astype(BF)
        return carry

    lax.fori_loop(0, WHEADS // 2, attend, 0)
    value = word_in_out[...] + dot(mixed[...], weights[:, at_out : at_out + width])
    after[...] = value
    unit, spread = norm_parts(value)
    unit_two[...] = unit
    normed_two[...] = (unit * small_rows[2:3, :] + small_rows[3:4, :]).astype(BF)
    row = lax.broadcasted_iota(jnp.int32, (own_words, 1), 0)
    index = jnp.where(row < local, origin[0] + row, origin[1] + row - local)
    valid = index < length
    up_low[rows_at(my_row), :] = cotangent[my_row]
    up_low[rows_at(1 - my_row), :] = cotangent_other[...]
    up_low[...] = jnp.where(valid, up_low[...].astype(F32), 0.0).astype(BF)
    total[...] = jnp.zeros_like(total)
    grad_normed[...] = jnp.zeros_like(grad_normed)

    def feed(j, carry):
        expand = weights[:, pl.ds(pl.multiple_of(at_expand + j * width, GROUP), width)]
        shrink = weights[:, pl.ds(pl.multiple_of(at_reduce + j * width, GROUP), width)]
        pre = dot(normed_two[...], expand) + small_rows[pl.ds(6 + j, 1), :]
        act, slope = gelu_both(pre)
        act = act.astype(BF)
        total[...] += dot(act, shrink)
        grad_pre = dot_t(up_low[...], shrink) * slope
        sums_out[pl.ds(6 + j, 1), :] = jnp.sum(grad_pre, 0, keepdims=True)
        grad_pre = grad_pre.astype(BF)
        grad_normed[...] += dot_t(grad_pre, expand)
        cols = pl.multiple_of(j * width, GROUP)
        grads[:, pl.ds(cols, width)] = t_dot(normed_two[...], grad_pre).astype(BF)
        grads[:, pl.ds(pl.multiple_of(hidden + j * width, GROUP), width)] = t_dot(
            act, up_low[...]
        ).astype(BF)
        return carry

    lax.fori_loop(0, FOLD, feed, 0)
    total[...] = jnp.where(valid, after[...] + (total[...] + small_rows[4:5, :]), 0.0)
    for t in range(2):
        words_both[t] = total[t * local : (t + 1) * local, :]
    words_sent[...] = total[rows_at(1 - my_row), :]
    upstream = up_low[...].astype(F32)
    incoming = grad_normed[...]
    sums_out[2:3, :] = jnp.sum(incoming * unit_two[...], 0, keepdims=True)
    sums_out[3:4, :] = jnp.sum(incoming, 0, keepdims=True)
    sums_out[4:5, :] = jnp.sum(upstream, 0, keepdims=True)
    grad_after = upstream + norm_back(unit_two[...], spread, incoming * small_rows[2:3, :])
    grad_after_out[...] = grad_after
    grad_low = grad_after.astype(BF)
    grads[:, 2 * hidden :] = t_dot(mixed[...], grad_low).astype(BF)
    mixed[...] = dot_t(grad_low, weights[:, at_out : at_out + width]).astype(BF)
    unfold_into(natural, grads[:, :hidden], width)
    for out_ref, core in ((kept_out, place[CORE]), (sent_out, 1 - place[CORE])):
        chosen = sorted_rows(core, counts, width)
        out_ref[:, :hidden] = dot(chosen, natural[...]).astype(BF)
        out_ref[:, hidden:] = dot(chosen, grads[:, hidden:]).astype(BF)

    def attend_back(p, carry):
        lanes = pl.ds(pl.multiple_of(p * GROUP, GROUP), GROUP)
        after_lanes = pl.ds(pl.multiple_of(width + p * GROUP, GROUP), GROUP)
        lows = [mixed[here, lanes] * masks[h] for here, t, h in chains]
        ones = [dot_t(low, pair[: reach[t], after_lanes]) for low, (_, t, h) in zip(lows, chains)]
        weights_of = [softs[t][2 * p + h] for _, t, h in chains]
        grads_of = []
        for one, soft in zip(ones, weights_of):
            wide = soft.astype(F32)
            grads_of.append((wide * (one - jnp.sum(wide * one, -1, keepdims=True))).astype(BF))
        grad_values = [dot(soft.T, low) for soft, low in zip(weights_of, lows)]
        grad_keys = [
            dot(one.T, query[here, lanes] * masks[h]) for one, (here, t, h) in zip(grads_of, chains)
        ]
        grad_queries = [
            dot(one, pair[: reach[t], lanes] * masks[h]) for one, (_, t, h) in zip(grads_of, chains)
        ]
        grad_values = [grad_values[2 * t] + grad_values[2 * t + 1] for t in range(2)]
        grad_keys = [grad_keys[2 * t] + grad_keys[2 * t + 1] for t in range(2)]
        for t in range(2):
            grad_query = grad_queries[2 * t] + grad_queries[2 * t + 1]
            grad_query_out[t * local : (t + 1) * local, lanes] = (grad_query * SCALE).astype(BF)
        for parts, at, factor in ((grad_keys, lanes, SCALE), (grad_values, after_lanes, 1.0)):
            grad_pair[:half, at] = ((parts[0] + parts[1][:half]) * factor).astype(BF)
            grad_pair[half:, at] = (parts[1][half:] * factor).astype(BF)
        return carry

    lax.fori_loop(0, WHEADS // 2, attend_back, 0)
    for m in range(members):
        there = jnp.bitwise_xor(member, m)
        for t in range(2):
            pair_outs[m][t * local : (t + 1) * local, :] = grad_pair[rows_at(t * members + there), :]


def word_part(counts, place, pieces, char_weights, weights, cotangent, cotangent_other):
    members = len(pieces) // 2
    local, narrow = pieces[0].shape
    all_words = local * len(pieces)
    width = cotangent.shape[2]
    own = 2 * local
    hidden = FOLD * width
    vmem = pl.BlockSpec(memory_space=pltpu.VMEM)
    share = jax.ShapeDtypeStruct((width // 2, 2 * hidden + width), BF)
    out_shape = (
        jax.ShapeDtypeStruct((2, local, width), F32),
        jax.ShapeDtypeStruct((local, width), F32),
        jax.ShapeDtypeStruct((own, width), F32),
        jax.ShapeDtypeStruct((own, width), BF),
        jax.ShapeDtypeStruct((own, width), BF),
        jax.ShapeDtypeStruct((own, width), F32),
        share,
        share,
        jax.ShapeDtypeStruct((16, width), F32),
    ) + (jax.ShapeDtypeStruct((own, 2 * width), BF),) * members
    return pl.pallas_call(
        functools.partial(word_kernel, counts, members),
        out_shape=out_shape,
        in_specs=[pl.BlockSpec(memory_space=pltpu.SMEM)] + [vmem] * (4 + len(pieces)),
        out_specs=(vmem,) * len(out_shape),
        scratch_shapes=[
            pltpu.VMEM((SMALL, width), F32),
            pltpu.VMEM((all_words, narrow), BF),
            pltpu.VMEM((all_words, width), F32),
            pltpu.VMEM((all_words, width), BF),
            pltpu.VMEM((all_words, 2 * width), BF),
            pltpu.VMEM((own, width), BF),
            pltpu.VMEM((own, all_words), F32),
            pltpu.VMEM((WHEADS, local, all_words // 2), BF),
            pltpu.VMEM((WHEADS, local, all_words), BF),
            pltpu.VMEM((own, width), BF),
            pltpu.VMEM((own, width), F32),
            pltpu.VMEM((own, width), F32),
            pltpu.VMEM((own, width), BF),
            pltpu.VMEM((own, width), BF),
            pltpu.VMEM((own, width), F32),
            pltpu.VMEM((own, width), F32),
            pltpu.VMEM((width, 2 * hidden + width), BF),
            pltpu.VMEM((width, hidden), BF),
            pltpu.VMEM((all_words, 2 * width), BF),
        ],
        compiler_params=pltpu.CompilerParams(vmem_limit_bytes=60 * MIB),
        cost_estimate=pl.CostEstimate(
            flops=own * width * width * 60, bytes_accessed=20 * MIB, transcendentals=own * 8192
        ),
    )(place, char_weights, weights, cotangent, cotangent_other, *pieces)


def word_end_kernel(
    counts,
    place,
    pooled_kept,
    pooled_other,
    char_weights,
    weights,
    small,
    grad_query,
    normed,
    word_in,
    grad_after,
    sums,
    *refs,
):
    pairs, refs = refs[:-8], refs[-8:]
    up_kept, up_sent, grad_to_word, kept_out, sent_out, small_rows, small_grads, incoming = refs
    width = grad_query.shape[1]
    local, narrow = pooled_kept.shape
    to_word = char_weights[:, columns_of(narrow)[3] :]
    small_rows[...] = small[...].astype(F32).T
    incoming[:, :width] = grad_query[...]
    pair = pairs[0][...].astype(F32)
    for other in pairs[1:]:
        pair = pair + other[...].astype(F32)
    incoming[:, width:] = pair.astype(BF)
    grad_normed = dot_t(incoming[...], weights[...])
    unit, spread = norm_parts(word_in[...])
    small_grads[...] = jnp.zeros_like(small_grads)
    small_grads[0:1, :] = jnp.sum(grad_normed * unit, 0, keepdims=True)
    small_grads[1:2, :] = jnp.sum(grad_normed, 0, keepdims=True)
    small_grads[2:5, :] = sums[2:5, :]
    small_grads[6:10, :] = sums[6:10, :]
    value = grad_after[...] + norm_back(unit, spread, grad_normed * small_rows[0:1, :])
    small_grads[5:6, :] = jnp.sum(value, 0, keepdims=True)
    low = value.astype(BF)
    back = dot_t(low, to_word).astype(BF)
    first_half = place[ROW] == 0
    up_kept[...] = jnp.where(first_half, back[:local].astype(F32), back[local:].astype(F32)).astype(BF)
    up_sent[...] = jnp.where(first_half, back[local:].astype(F32), back[:local].astype(F32)).astype(BF)
    low_kept = jnp.where(first_half, value[:local], value[local:]).astype(BF)
    low_other = jnp.where(first_half, value[local:], value[:local]).astype(BF)
    grad_to_word[...] = (t_dot(pooled_kept[...], low_kept) + t_dot(pooled_other[...], low_other)).astype(BF)
    inward = t_dot(normed[...], incoming[...]).astype(BF)
    small_turned = small_grads[...].T.astype(BF)
    columns = 3 * width + SMALL
    for out_ref, core in ((kept_out, place[CORE]), (sent_out, 1 - place[CORE])):
        for k in range(width // narrow):
            chosen = sorted_rows(core, counts, width, width // narrow, k)
            out_ref[:, k * columns : k * columns + 3 * width] = dot(chosen, inward).astype(BF)
            out_ref[:, k * columns + 3 * width : (k + 1) * columns] = dot(chosen, small_turned).astype(BF)


def word_end(
    counts,
    place,
    pooled_kept,
    pooled_other,
    char_weights,
    weights,
    grad_query,
    normed,
    word_in,
    grad_after,
    sums,
    pairs,
):
    local, narrow = pooled_kept.shape
    own, width = grad_query.shape
    columns = weights.shape[1]
    share = (narrow // 2, (3 * width + SMALL) * (width // narrow))
    outs = ((local, narrow), (local, narrow), (narrow, width), share, share)
    operands = (grad_query, normed, word_in, grad_after, sums) + tuple(pairs)
    return pl.pallas_call(
        functools.partial(word_end_kernel, counts),
        out_shape=tuple(jax.ShapeDtypeStruct(shape, BF) for shape in outs),
        grid_spec=pltpu.PrefetchScalarGridSpec(
            num_scalar_prefetch=1,
            grid=(1,),
            in_specs=[
                full(pooled_kept.shape),
                full(pooled_other.shape),
                full(char_weights.shape),
                pl.BlockSpec((width, 3 * width), lambda i, *_: (0, 0)),
                pl.BlockSpec((width, SMALL), lambda i, *_: (0, columns // SMALL - 1)),
            ]
            + [full(operand.shape) for operand in operands],
            out_specs=tuple(full(shape) for shape in outs),
            scratch_shapes=[
                pltpu.VMEM((SMALL, width), F32),
                pltpu.VMEM((SMALL, width), F32),
                pltpu.VMEM((own, 3 * width), BF),
            ],
        ),
        compiler_params=pltpu.CompilerParams(vmem_limit_bytes=60 * MIB),
        cost_estimate=pl.CostEstimate(
            flops=own * width * width * 14, bytes_accessed=10 * MIB, transcendentals=0
        ),
    )(place, pooled_kept, pooled_other, char_weights, weights, weights, *operands)


def column(vector, rows):
    each = vector.shape[0] // rows
    wide = vector[...].astype(F32).reshape(1, rows * each)
    line = lax.broadcasted_iota(jnp.int32, (rows, rows * each), 0)
    lane = lax.broadcasted_iota(jnp.int32, (rows, rows * each), 1)
    return [
        jnp.sum(jnp.where(line * each + j == lane, wide, 0.0), 1, keepdims=True) for j in range(each)
    ]


def columns_beside(rows, vectors, at):
    lane = lax.broadcasted_iota(jnp.int32, (rows, SMALL), 1)
    block = jnp.zeros((rows, SMALL), F32)
    for vector in vectors:
        for one in column(vector, rows):
            block = block + jnp.where(lane == at, one, 0.0)
            at += 1
    return block


def fold_into(out, at, weights, width):
    size = FOLD * HEAD
    matrix = folding(False)
    for m in range(width // HEAD):
        block = dot(weights[:, m * size : (m + 1) * size], matrix).astype(BF)
        for j in range(FOLD):
            there = at + j * width + m * HEAD
            out[:, there : there + HEAD] = block[:, j * HEAD : (j + 1) * HEAD]


def fold_shard(weights):
    tall = weights.shape[0]
    rows = tall // FOLD
    line = lax.broadcasted_iota(jnp.int32, (rows, tall), 0)
    lane = lax.broadcasted_iota(jnp.int32, (rows, tall), 1)
    return [
        dot((lane == FOLD * line + j).astype(F32).astype(BF), weights[...]).astype(BF) for j in range(FOLD)
    ]


def char_shard_kernel(table, inward, outward, expand, reduced, to_word, *refs):
    vectors, out = refs[:-1], refs[-1]
    rows, langs = table.shape
    width = outward.shape[1]
    at_small, at_expand, at_reduce, at_to_word = columns_of(width)
    out[:, : 3 * width] = inward[...]
    out[:, 3 * width : 4 * width] = outward[...]
    line = lax.broadcasted_iota(jnp.int32, (langs, SMALL), 0)
    lane = lax.broadcasted_iota(jnp.int32, (langs, SMALL), 1)
    spread = (line == lane).astype(F32).astype(BF)
    small = dot(table[...], spread) + columns_beside(rows, vectors, langs)
    out[:, at_small:at_expand] = small.astype(BF)
    fold_into(out, at_expand, expand, width)
    for j, part in enumerate(fold_shard(reduced)):
        out[:, at_reduce + j * width : at_reduce + (j + 1) * width] = part
    out[:, at_to_word:] = to_word[...]


def char_shard(table, inward, outward, expand, reduced, to_word, vectors):
    rows, width = outward.shape
    vmem = pl.BlockSpec(memory_space=pltpu.VMEM)
    return pl.pallas_call(
        char_shard_kernel,
        out_shape=jax.ShapeDtypeStruct((rows, columns_of(width)[3] + to_word.shape[1]), BF),
        in_specs=[vmem] * (6 + len(vectors)),
        out_specs=vmem,
    )(table, inward, outward, expand, reduced, to_word, *vectors)


def word_shard_kernel(inward, outward, expand, reduced, *refs):
    vectors, out = refs[:-1], refs[-1]
    rows, width = outward.shape
    out[:, : 3 * width] = inward[...]
    out[:, 3 * width : 4 * width] = outward[...]
    fold_into(out, 4 * width, expand, width)
    for j, part in enumerate(fold_shard(reduced)):
        out[:, (8 + j) * width : (9 + j) * width] = part
    out[:, 12 * width :] = columns_beside(rows, vectors, 0).astype(BF)


def word_shard(inward, outward, expand, reduced, vectors):
    rows, width = outward.shape
    vmem = pl.BlockSpec(memory_space=pltpu.VMEM)
    return pl.pallas_call(
        word_shard_kernel,
        out_shape=jax.ShapeDtypeStruct((rows, 12 * width + SMALL), BF),
        in_specs=[vmem] * (4 + len(vectors)),
        out_specs=vmem,
    )(inward, outward, expand, reduced, *vectors)


def assemble_kernel(masks, index, *refs):
    pieces, out = refs[:-1], refs[-1]
    me = index[0]
    size = pieces[0].shape[0]
    for k, piece in enumerate(pieces):
        for t in range(size):
            out[jnp.bitwise_xor(me, masks[k * size + t])] = piece[t]


def assemble(masks, index, pieces):
    size, rows, columns = pieces[0].shape
    vmem = pl.BlockSpec(memory_space=pltpu.VMEM)
    out = pl.pallas_call(
        functools.partial(assemble_kernel, tuple(masks)),
        out_shape=jax.ShapeDtypeStruct((size * len(pieces), rows, columns), BF),
        in_specs=[pl.BlockSpec(memory_space=pltpu.SMEM)] + [vmem] * len(pieces),
        out_specs=vmem,
        cost_estimate=pl.CostEstimate(
            flops=0, bytes_accessed=4 * size * len(pieces) * rows * columns, transcendentals=0
        ),
    )(index, *pieces)
    return out.reshape(-1, columns)


def add_and_cut_kernel(layout, which, place, *refs):
    groups, parts = layout
    at = 0
    ins = []
    for count in groups:
        ins.append(refs[at : at + count])
        at += count
    me = place[which]
    for arrived in ins:
        total = arrived[0][...].astype(F32)
        for one in arrived[1:]:
            total = total + one[...].astype(F32)
        total = total.astype(BF)
        rows = total.shape[0]
        each = rows // parts
        line = lax.broadcasted_iota(jnp.int32, (each, rows), 0)
        lane = lax.broadcasted_iota(jnp.int32, (each, rows), 1)
        for m in range(parts):
            chosen = (lane == jnp.bitwise_xor(me, m) * each + line).astype(F32).astype(BF)
            refs[at][...] = dot(chosen, total).astype(BF)
            at += 1


def add_and_cut(arrivals, parts, which, place):
    vmem = pl.BlockSpec(memory_space=pltpu.VMEM)
    flat = [one for arrived in arrivals for one in arrived]
    shapes = []
    for arrived in arrivals:
        rows, columns = arrived[0].shape
        shapes += [jax.ShapeDtypeStruct((rows // parts, columns), BF)] * parts
    outs = pl.pallas_call(
        functools.partial(add_and_cut_kernel, (tuple(len(a) for a in arrivals), parts), which),
        out_shape=tuple(shapes),
        in_specs=[pl.BlockSpec(memory_space=pltpu.SMEM)] + [vmem] * len(flat),
        out_specs=(vmem,) * len(shapes),
        compiler_params=pltpu.CompilerParams(vmem_limit_bytes=60 * MIB),
        cost_estimate=pl.CostEstimate(
            flops=0, bytes_accessed=sum(4 * one.size for one in flat), transcendentals=0
        ),
    )(place, *flat)
    return [outs[k * parts : (k + 1) * parts] for k in range(len(arrivals))]


def add_up(arrived):
    total = arrived[0].astype(F32)
    for one in arrived[1:]:
        total = total + one.astype(F32)
    return total


def tie(values, after):
    return lax.optimization_barrier((values, after))[0]


def body(
    char_inputs,
    language_ids,
    char_counts,
    row_lengths,
    cotangent,
    language_table,
    char_gain_one,
    char_bias_one,
    char_inward,
    char_outward,
    char_gain_two,
    char_bias_two,
    char_expand,
    char_expand_bias,
    char_reduce,
    char_reduce_bias,
    char_to_word,
    char_to_word_bias,
    word_gain_one,
    word_bias_one,
    word_inward,
    word_outward,
    word_gain_two,
    word_bias_two,
    word_expand,
    word_expand_bias,
    word_reduce,
    word_reduce_bias,
):
    rows, local, slots, width = char_inputs.shape
    words = rows * local
    langs = language_table.shape[0]
    wide = word_inward.shape[1] // 3
    deep, share = lax.axis_size("dp"), lax.axis_size("fsdp")
    devices = deep * share
    members = share // rows
    axes = ("dp", "fsdp")
    at_deep, at_share = lax.axis_index("dp"), lax.axis_index("fsdp")

    def swap(values, mask):
        return lax.ppermute(values, axes, [(k, k ^ mask) for k in range(devices)])

    far, low = deep // 2, share // 2
    near = 2 * low
    far_masks = [m * 2 * share for m in range(far)]
    near_masks = [(m // low) * share + (m % low) * 2 for m in range(near)]
    core_masks = [0, 1]
    counts_of = (far, near)
    top = members
    my_row = at_share // members
    place = jnp.stack(
        [
            at_share % members,
            my_row,
            lax.dynamic_index_in_dim(row_lengths, my_row, 0, keepdims=False),
            at_share % 2,
            (at_deep % 2) * low + at_share // 2,
            at_deep // 2,
        ]
    )
    index = (at_deep * share + at_share).reshape(1)

    def swaps(values, masks):
        return [values] + [swap(values, m) for m in masks[1:]]

    def together(pieces, rows):
        return jnp.stack(pieces).reshape(-1, rows, pieces[0].shape[-1])

    order = [c | n | f for c in core_masks for n in near_masks for f in far_masks]

    char_piece = char_shard(
        language_table.T,
        char_inward,
        char_outward,
        char_expand,
        char_reduce,
        char_to_word,
        (char_gain_one, char_bias_one, char_gain_two, char_bias_two, char_reduce_bias, char_expand_bias),
    )
    each = char_piece.shape[0]
    counts = tie(char_counts.reshape(words), char_piece)
    offs, first, rows_of, blocks = offsets(counts, slots, local)
    char_pieces = tie(swaps(char_piece, far_masks), offs)
    char_piece = together(char_pieces, each)
    packed, bias, hot = pack(
        tie(counts, char_piece), offs, first, blocks, char_inputs.reshape(words, slots, width), local
    )
    char_piece = together(swaps(char_piece, near_masks), each)
    char_full = assemble(order, index, swaps(tie(char_piece, packed), core_masks))
    word_full = lax.all_gather(
        word_shard(
            word_inward,
            word_outward,
            word_expand,
            word_reduce,
            (
                word_gain_one,
                word_bias_one,
                word_gain_two,
                word_bias_two,
                word_reduce_bias,
                char_to_word_bias,
                word_expand_bias,
            ),
        ),
        axes,
        axis=0,
        tiled=True,
    )
    cotangent_other = swap(lax.dynamic_index_in_dim(cotangent, 1 - my_row, 0, keepdims=False), top)

    inverse = 1.0 / counts.astype(F32).reshape(words, 1)
    qkv, soft, mixed, after = char_attend(langs, blocks, rows_of, language_ids, packed, bias, char_full)
    act, slope, pooled_kept, pooled_sent = char_ffn(
        langs, blocks, first, place, after, hot, inverse, char_full
    )
    pooled_other = swap(pooled_sent, top)
    pieces = []
    for m in range(members):
        pieces += [swap(pooled_kept, m), swap(pooled_other, m)] if m else [pooled_kept, pooled_other]
    words_both, words_sent, word_after_grad, query_grad, word_normed, word_in, *others = word_part(
        counts_of, place, pieces, char_full, word_full, cotangent, cotangent_other
    )
    word_kept, word_sent, word_sums, *pair_grads = others
    word_arrived = [word_kept, swap(word_sent, 1)]
    pairs = [pair_grads[0]] + [swap(pair_grads[m], m) for m in range(1, members)]
    up_kept, up_sent, to_word_grad, inward_kept, inward_sent = word_end(
        counts_of,
        place,
        pooled_kept,
        pooled_other,
        char_full,
        word_full,
        query_grad,
        word_normed,
        word_in,
        word_after_grad,
        word_sums,
        pairs,
    )
    up_other = swap(up_sent, top)

    def phase(parts, masks):
        return [[own[0]] + [swap(own[m], masks[m]) for m in range(1, len(masks))] for own in parts]

    word_parts = add_and_cut([word_arrived], near, NEAR, place)
    up_kept = tie(up_kept, word_parts)
    after_grad, feed_kept, feed_sent, char_sums = char_ffn_back(
        (langs, counts_of),
        blocks,
        first,
        place,
        after,
        hot,
        act,
        slope,
        inverse,
        up_kept,
        up_other,
        char_full,
        to_word_grad,
        (inward_kept, inward_sent),
    )
    word_parts = add_and_cut(tie(phase(word_parts, near_masks), feed_kept), far, FAR, place)
    feed_sent = tie(feed_sent, word_parts)
    late_parts = add_and_cut([[feed_kept, swap(feed_sent, 1)]], near, NEAR, place)
    after_grad = tie(after_grad, (word_parts, late_parts))
    operands = (packed, qkv, soft, mixed, after_grad, char_full, char_sums)
    before = char_attend_back((langs, counts_of), blocks, rows_of, language_ids, place, *operands)
    arrived_words, arrived_late, before = lax.optimization_barrier(
        (phase(word_parts, far_masks), phase(late_parts, near_masks), before)
    )
    word_shares = add_up(arrived_words[0])
    late_parts = add_and_cut(arrived_late, far, FAR, place)
    words_sent, before = lax.optimization_barrier((words_sent, tie(before, (word_shares, late_parts))))
    *start_grad, attend_kept, attend_sent = char_attend_back(
        (langs, counts_of), blocks, rows_of, language_ids, place, *operands, before=before
    )
    arrived_late, words_other, attend_kept, attend_sent = lax.optimization_barrier(
        (phase(late_parts, far_masks), swap(words_sent, top), attend_kept, attend_sent)
    )
    late_shares = add_up(arrived_late[0])
    words_out = lax.dynamic_update_index_in_dim(words_both, words_other, 1 - my_row, 0)
    feed_columns = 2 * FOLD * width + wide
    feed_shares = late_shares[:, :feed_columns]
    inward_shares = late_shares[:, feed_columns:].reshape(late_shares.shape[0], wide // width, -1)
    inward_shares = inward_shares.swapaxes(0, 1).reshape(word_inward.shape[0], -1)
    word_small = inward_shares[:, 3 * wide :]
    hidden = FOLD * width
    wide_hidden = FOLD * wide

    def column_of(values, at, count=1):
        return values[:, at : at + count].reshape(-1)

    earlier = (
        words_out,
        feed_shares[:, :hidden],
        feed_shares[:, hidden : 2 * hidden].reshape(char_reduce.shape),
        feed_shares[:, 2 * hidden :],
        column_of(word_small, 5),
        column_of(word_small, 0),
        column_of(word_small, 1),
        inward_shares[:, : 3 * wide],
        word_shares[:, 2 * wide_hidden :],
        column_of(word_small, 2),
        column_of(word_small, 3),
        word_shares[:, :wide_hidden],
        column_of(word_small, 6, FOLD),
        word_shares[:, wide_hidden : 2 * wide_hidden].reshape(word_reduce.shape),
        column_of(word_small, 4),
    )
    arrived, earlier = lax.optimization_barrier(([attend_kept, swap(attend_sent, 1)], earlier))
    attend_parts = add_and_cut([arrived], near, NEAR, place)
    char_input_grad = unpack(offs, counts, tie(start_grad, attend_parts), slots)
    arrived, char_input_grad = lax.optimization_barrier((phase(attend_parts, near_masks), char_input_grad))
    attend_parts = add_and_cut(arrived, far, FAR, place)
    char_input_grad = unpack(offs, counts, tie(start_grad, attend_parts), slots, char_input_grad)
    arrived, char_input_grad = lax.optimization_barrier((phase(attend_parts, far_masks), char_input_grad))
    attend_shares = add_up(arrived[0])
    small = attend_shares[:, 4 * width :]
    (
        words_out,
        grad_expand,
        grad_reduce,
        grad_to_word,
        grad_to_word_bias,
        *grads_word,
    ) = earlier
    return (
        words_out,
        char_input_grad.reshape(char_inputs.shape),
        small[:, :langs].T,
        column_of(small, langs),
        column_of(small, langs + 1),
        attend_shares[:, : 3 * width],
        attend_shares[:, 3 * width : 4 * width],
        column_of(small, langs + 2),
        column_of(small, langs + 3),
        grad_expand,
        column_of(small, langs + 5, FOLD),
        grad_reduce,
        column_of(small, langs + 4),
        grad_to_word,
        grad_to_word_bias,
        *grads_word,
    )


def solution(mesh):
    both = ("dp", "fsdp")
    vector, matrix = P(both), P(both, None)
    weights = (
        (P(None, both), vector, vector, matrix, matrix, vector, vector)
        + (matrix, vector, matrix, vector, matrix, vector)
        + (vector, vector, matrix, matrix, vector, vector, matrix, vector, matrix, vector)
    )
    in_specs = (
        P("dp", "fsdp", None, None),
        P("dp"),
        P("dp", "fsdp"),
        P("dp"),
        P("dp", "fsdp", None),
    ) + weights
    out_specs = (P("dp", "fsdp", None), P("dp", "fsdp", None, None)) + weights
    return jax.shard_map(body, mesh=mesh, in_specs=in_specs, out_specs=out_specs, check_vma=False)
```

```python
import functools

import jax
import jax.numpy as jnp
from jax import lax
from jax.experimental import pallas as pl
from jax.experimental.pallas import tpu as pltpu
from jax.sharding import PartitionSpec as P

BF = jnp.bfloat16
F32 = jnp.float32
EPS = 1e-05
MASKED = -1e30
CHEADS = 4
WHEADS = 8
HEAD = 64
SCALE = HEAD ** (-0.5)
GROUP = 128
GROUP_BITS = 7
BLOCK = 1024
SPLIT = BLOCK // GROUP
FOLD = 4
SMALL = 128
GELU_A = 0.7978845608028654
GELU_B = 0.044715
MIB = 1024 * 1024
VMEM_LIMIT = 63 * MIB
MEMBER, ROW, LENGTH, CORE, NEAR, FAR = range(6)


def columns_of(width, wide):
    hidden = FOLD * width
    return 4 * width, 4 * width + hidden, 4 * width + 2 * hidden, 4 * width + 2 * hidden + wide


def columns(array, width, start):
    return array, pl.BlockSpec((array.shape[0], width), lambda *_: (0, start // width))


def dot(a, b):
    return jnp.dot(a, b, preferred_element_type=F32)


def dot_t(a, b):
    return lax.dot_general(a, b, (((1,), (1,)), ((), ())), preferred_element_type=F32)


def t_dot(a, b):
    return dot(a.T, b)


def norm_parts(hidden):
    centred = hidden - jnp.mean(hidden, -1, keepdims=True)
    spread = lax.rsqrt(jnp.mean(centred * centred, -1, keepdims=True) + EPS)
    return centred * spread, spread


def norm_back(unit, spread, gained):
    return (
        gained
        - jnp.mean(gained, -1, keepdims=True)
        - unit * jnp.mean(gained * unit, -1, keepdims=True)
    ) * spread


def gelu_both(pre):
    square = pre * pre
    turn = jnp.tanh(pre * (GELU_A + (GELU_A * GELU_B) * square))
    half = 0.5 + 0.5 * turn
    slope = half + pre * half * (1.0 - turn) * (GELU_A + (3.0 * GELU_A * GELU_B) * square)
    return pre * half, slope


def fold_rows(values):
    rows, width = values.shape
    return jnp.sum(values.reshape(rows // 8, 8, width), 0)


def head_masks(width, heads):
    lanes = lax.broadcasted_iota(jnp.int32, (1, width), 1) // HEAD
    return [(lanes == h).astype(F32).astype(BF) for h in range(heads)]


def run_blocks(step, begin, end, inputs, outputs):
    def one(*refs):
        step(begin + pl.program_id(0), *refs)

    def spec(ref):
        return pl.BlockSpec((BLOCK, ref.shape[1]), lambda i: (begin + i, 0))

    pltpu.emit_pipeline(
        one,
        grid=(end - begin,),
        in_specs=[spec(ref) for ref in inputs],
        out_specs=[spec(ref) for ref in outputs],
    )(*inputs, *outputs)


def streamed(kernel, scalars, streams, fixed, stream_outs, fixed_outs, scratch, cost, aliases=None):
    hbm = pl.BlockSpec(memory_space=pltpu.HBM)
    fixed = [one if isinstance(one, tuple) else (one, full(one.shape)) for one in fixed]
    return pl.pallas_call(
        kernel,
        out_shape=tuple(jax.ShapeDtypeStruct(*out) for out in tuple(stream_outs) + tuple(fixed_outs)),
        grid_spec=pltpu.PrefetchScalarGridSpec(
            num_scalar_prefetch=len(scalars),
            grid=(1,),
            in_specs=[hbm] * len(streams) + [spec for _, spec in fixed],
            out_specs=(hbm,) * len(stream_outs) + tuple(full(shape) for shape, _ in fixed_outs),
            scratch_shapes=[pltpu.VMEM(*one) if isinstance(one, tuple) else one for one in scratch],
        ),
        input_output_aliases=aliases or {},
        compiler_params=pltpu.CompilerParams(vmem_limit_bytes=VMEM_LIMIT),
        cost_estimate=cost,
    )(*scalars, *streams, *(one for one, _ in fixed))


def full(shape):
    return pl.BlockSpec(shape, lambda *_: (0,) * len(shape))


def offsets_kernel(layout, counts, lengths, index, offs, first, rows_of, blocks, place_out):
    share, members = layout
    rows, per_row = counts.shape
    deep, part = lax.div(index[0], share), lax.rem(index[0], share)
    my_row = lax.div(part, members)
    place_out[MEMBER] = lax.rem(part, members)
    place_out[ROW] = my_row
    place_out[LENGTH] = lengths[my_row]
    place_out[CORE] = lax.rem(part, 2)
    place_out[NEAR] = lax.rem(deep, 2) * (share // 2) + lax.div(part, 2)
    place_out[FAR] = lax.div(deep, 2)

    def clear(g, carry):
        first[g] = 0
        rows_of[g] = 0
        return carry

    lax.fori_loop(0, first.shape[0], clear, 0, unroll=True)
    spare = first.shape[0] - 1

    def place(row, k, at):
        live = counts[row, k]
        w = row * per_row + k
        inside = at & (GROUP - 1)
        at = jnp.where(inside + live > GROUP, at - inside + GROUP, at)
        group = jnp.where((at & (GROUP - 1)) == 0, at >> GROUP_BITS, spare)
        first[group] = w
        rows_of[group] = row
        offs[w] = at
        return at + live

    at = 0
    for row in range(rows):
        at = lax.fori_loop(0, per_row, functools.partial(place, row), at, unroll=8)
        at = ((at + (GROUP - 1)) >> GROUP_BITS) << GROUP_BITS
    blocks[0] = lax.div(at + (BLOCK - 1), BLOCK)


def group_count(words, slots, per_row):
    groups = (words * slots) // (GROUP - slots + 1) + 1 + words // per_row
    return -(-groups // SPLIT) * SPLIT


def offsets(layout, counts, lengths, index, slots):
    rows, per_row = counts.shape
    words = rows * per_row
    groups = group_count(words, slots, per_row)
    smem = pl.BlockSpec(memory_space=pltpu.SMEM)
    sizes = (words, groups + 1, groups + 1, 1, 6)
    return pl.pallas_call(
        functools.partial(offsets_kernel, layout),
        out_shape=tuple(jax.ShapeDtypeStruct((size,), jnp.int32) for size in sizes),
        in_specs=[smem] * 3,
        out_specs=(smem,) * 5,
        cost_estimate=pl.CostEstimate(flops=words * 4000, bytes_accessed=12 * MIB, transcendentals=0),
    )(counts, lengths, index)


def pack_kernel(
    counts, offs, first, blocks, chars, packed_all, bias_all, hot_all, tags, *wide
):
    slots = chars.shape[1]
    rows, per_row = counts.shape
    slot = lax.broadcasted_iota(jnp.int32, (slots, GROUP), 0)

    def clear_rows(k, carry):
        there = pl.ds(pl.multiple_of(k * GROUP, GROUP), GROUP)
        for part in wide:
            part[there, :] = jnp.zeros((GROUP, GROUP), F32)
        tags[there, :] = jnp.full((GROUP, GROUP), -1.0, F32)
        return carry

    lax.fori_loop(0, blocks[0] * SPLIT, clear_rows, 0)

    def put(row, n, carry):
        w = row * per_row + n
        at = offs[w]
        for k, part in enumerate(wide):
            part[pl.ds(at, slots), :] = chars[w, :, k * GROUP : (k + 1) * GROUP].astype(F32)
        tags[pl.ds(at, slots), :] = jnp.where(slot < counts[row, n], w.astype(F32), -1.0)
        return carry

    for row in range(rows):
        lax.fori_loop(0, per_row, functools.partial(put, row), 0, unroll=8)
    lane = lax.broadcasted_iota(jnp.int32, (GROUP, GROUP), 1).astype(F32)

    def step(i, packed, bias, hot):
        for g in range(SPLIT):
            here = slice(g * GROUP, (g + 1) * GROUP)
            there = pl.ds(pl.multiple_of((i * SPLIT + g) * GROUP, GROUP), GROUP)
            tag = tags[there, :]
            bias[here, :] = jnp.where(tag == tag.T, 0.0, MASKED).astype(BF)
            hot[here, :] = (tag - first[i * SPLIT + g].astype(F32) == lane).astype(F32).astype(BF)
            for k, part in enumerate(wide):
                packed[here, k * GROUP : (k + 1) * GROUP] = part[there, :].astype(BF)

    run_blocks(step, 0, blocks[0], (), (packed_all, bias_all, hot_all))


def pack(counts, offs, first, blocks, chars):
    words, slots, width = chars.shape
    rows = group_count(words, slots, counts.shape[1]) * GROUP
    return streamed(
        pack_kernel,
        (counts, offs, first, blocks),
        (),
        (chars,),
        (((rows, width), BF), ((rows, GROUP), BF), ((rows, GROUP), BF)),
        (),
        (((rows + GROUP, GROUP), F32),) * (1 + width // GROUP),
        pl.CostEstimate(flops=rows * width * 4, bytes_accessed=rows * width * 10, transcendentals=0),
    )


def unpack_kernel(row, halves, offs, counts, *refs):
    packed = refs[:halves]
    out, held, arrived = refs[-2 - halves], refs[-1 - halves : -1], refs[-1]
    slots = out.shape[1]
    count = counts.shape[1]
    begin = row * count
    here = pl.program_id(0) * out.shape[0]
    slot = lax.broadcasted_iota(jnp.int32, (slots, GROUP), 0)

    @pl.when(pl.program_id(0) == 0)
    def _():
        low = lax.div(offs[begin], BLOCK)
        high = lax.div(offs[begin + count - 1] + (slots + BLOCK - 1), BLOCK)

        def copy(k, j):
            there = pl.ds(pl.multiple_of(k * BLOCK, BLOCK), BLOCK)
            return pltpu.make_async_copy(packed[j].at[there, :], held[j].at[there, :], arrived.at[j, k])

        def fetch(k, carry):
            for j in range(halves):
                copy(k, j).start()
            return carry

        def await_one(k, carry):
            for j in range(halves):
                copy(k, j).wait()
            return carry

        lax.fori_loop(low, high, fetch, 0)
        lax.fori_loop(low, high, await_one, 0)

    def take(k, carry):
        n = here + k
        for j, part in enumerate(held):
            rows = part[pl.ds(offs[begin + n], slots), :]
            out[k, :, j * GROUP : (j + 1) * GROUP] = jnp.where(slot < counts[row, n], rows, 0.0)
        return carry

    lax.fori_loop(0, out.shape[0], take, 0, unroll=8)


def unpack(offs, counts, packed, slots, before=None):
    words = counts.size
    halves = len(packed)
    width = halves * GROUP
    step = words // 8
    row = 0 if before is None else 1
    extra = [] if before is None else [before]
    hbm = pl.BlockSpec(memory_space=pltpu.HBM)
    return pl.pallas_call(
        functools.partial(unpack_kernel, row, halves),
        out_shape=jax.ShapeDtypeStruct((words, slots, width), F32),
        grid_spec=pltpu.PrefetchScalarGridSpec(
            num_scalar_prefetch=2,
            grid=(4,),
            in_specs=[hbm] * (halves + len(extra)),
            out_specs=pl.BlockSpec((step, slots, width), lambda i, *_: (4 * row + i, 0, 0)),
            scratch_shapes=[pltpu.VMEM(part.shape, F32) for part in packed]
            + [pltpu.SemaphoreType.DMA((halves, packed[0].shape[0] // BLOCK))],
        ),
        input_output_aliases={2 + halves: 0} if extra else {},
        compiler_params=pltpu.CompilerParams(vmem_limit_bytes=VMEM_LIMIT),
        cost_estimate=pl.CostEstimate(
            flops=words * slots * width, bytes_accessed=words * slots * width * 4, transcendentals=0
        ),
    )(offs, counts, *packed, *extra)


def with_language(i, rows_of, ids, packed, small_rows):
    parts = []
    for g in range(SPLIT):
        row = small_rows[pl.ds(ids[rows_of[i * SPLIT + g]], 1), :]
        parts.append(packed[g * GROUP : (g + 1) * GROUP, :].astype(F32) + row)
    return jnp.concatenate(parts, 0)


def both_heads(values, lower):
    wide = values.astype(F32)
    return jnp.concatenate([jnp.where(lower, wide, 0.0), jnp.where(lower, 0.0, wide)], 0).astype(BF)


def pick_heads(stacked, lower):
    rows = stacked.shape[0] // 2
    return jnp.where(lower, stacked[:rows], stacked[rows:])


def char_attend_kernel(
    langs,
    blocks,
    rows_of,
    ids,
    place,
    packed_all,
    bias_all,
    cotangent,
    weights,
    small,
    qkv_all,
    soft_all,
    mixed_all,
    after_all,
    cotangent_out,
    small_rows,
    sent,
):
    copy = pltpu.make_async_copy(cotangent.at[1 - place[ROW]], cotangent_out, sent)
    copy.start()
    width = packed_all.shape[1]
    small_rows[...] = small[...].astype(F32).T

    def step(i, packed, bias, qkv_out, soft_out, mixed_out, after_out):
        start = with_language(i, rows_of, ids, packed, small_rows)
        unit, _ = norm_parts(start)
        normed = (unit * small_rows[langs : langs + 1, :] + small_rows[langs + 1 : langs + 2, :]).astype(BF)
        qkv_out[...] = dot(normed, weights[:, : 3 * width]).astype(BF)
        lower = lax.broadcasted_iota(jnp.int32, (GROUP, GROUP), 1) < HEAD
        places = [(slice(g * GROUP, (g + 1) * GROUP), t) for g in range(SPLIT) for t in range(CHEADS // 2)]
        scores = []
        for here, t in places:
            tile = slice(t * GROUP, (t + 1) * GROUP)
            keys = both_heads(qkv_out[here, width + t * GROUP : width + (t + 1) * GROUP], lower)
            scores.append(dot_t(keys, qkv_out[here, tile]))
        softs = []
        for (here, t), score in zip(places, scores):
            blocked = bias[here, :].astype(F32)
            for h in range(2):
                one = score[h * GROUP : (h + 1) * GROUP] * SCALE + blocked
                one = jnp.exp(one - jnp.max(one, 0, keepdims=True))
                one = (one * (1.0 / jnp.sum(one, 0, keepdims=True))).astype(BF)
                soft_out[here, (2 * t + h) * GROUP : (2 * t + h + 1) * GROUP] = one
                softs.append(one)
        for k, (here, t) in enumerate(places):
            values = qkv_out[here, 2 * width + t * GROUP : 2 * width + (t + 1) * GROUP]
            mixed = dot(jnp.concatenate([softs[2 * k].T, softs[2 * k + 1].T], 0), values)
            mixed_out[here, t * GROUP : (t + 1) * GROUP] = pick_heads(mixed, lower).astype(BF)
        after_out[...] = start + dot(mixed_out[...], weights[:, 3 * width : 4 * width])

    run_blocks(step, 0, blocks[0], (packed_all, bias_all), (qkv_all, soft_all, mixed_all, after_all))
    copy.wait()


def char_attend(langs, blocks, rows_of, ids, place, packed, bias, weights, cotangent):
    rows, width = packed.shape
    at_small = weights.shape[1] - SMALL
    return streamed(
        functools.partial(char_attend_kernel, langs),
        (blocks, rows_of, ids, place),
        (packed, bias, cotangent),
        (columns(weights, 4 * width, 0), columns(weights, SMALL, at_small)),
        (
            ((rows, 3 * width), BF),
            ((rows, CHEADS * GROUP), BF),
            ((rows, width), BF),
            ((rows, width), F32),
            (cotangent.shape[1:], BF),
        ),
        (),
        (((SMALL, width), F32), pltpu.SemaphoreType.DMA),
        pl.CostEstimate(
            flops=rows * width * width * 12, bytes_accessed=rows * width * 12, transcendentals=rows * 512
        ),
    )


def char_ffn_kernel(
    langs,
    blocks,
    first,
    place,
    after_all,
    hot_all,
    inverse,
    expand,
    reduced,
    small,
    act_all,
    slope_all,
    kept_out,
    sent_out,
    small_rows,
    *total,
):
    width = after_all.shape[1]
    small_rows[...] = small[...].astype(F32).T
    for part in total:
        part[...] = jnp.zeros_like(part)

    def step(i, after, hot, act_out, slope_out):
        unit, _ = norm_parts(after[...])
        normed = (unit * small_rows[langs + 2 : langs + 3, :] + small_rows[langs + 3 : langs + 4, :]).astype(BF)
        out = after[...] + small_rows[langs + 4 : langs + 5, :]
        pres = [dot(normed, expand[:, j * width : (j + 1) * width]) for j in range(FOLD)]
        acts = []
        for j, pre in enumerate(pres):
            cols = slice(j * width, (j + 1) * width)
            act, slope = gelu_both(pre + small_rows[langs + 5 + j : langs + 6 + j, :])
            act = act.astype(BF)
            act_out[:, cols] = act
            slope_out[:, cols] = slope.astype(BF)
            acts.append(act)
        for j, act in enumerate(acts):
            out = out + dot(act, reduced[:, j * width : (j + 1) * width])
        out = out.astype(BF)
        for g in range(SPLIT):
            here = slice(g * GROUP, (g + 1) * GROUP)
            words = pl.ds(first[i * SPLIT + g], GROUP)
            found = t_dot(hot[here, :], out[here, :])
            for k, part in enumerate(total):
                part[words, :] = part[words, :] + found[:, k * GROUP : (k + 1) * GROUP]

    run_blocks(step, 0, blocks[0], (after_all, hot_all), (act_all, slope_all))
    local = kept_out.shape[0]
    for out_ref, row in ((kept_out, place[ROW]), (sent_out, 1 - place[ROW])):
        there = pl.ds(pl.multiple_of(row * local, local), local)
        for k, part in enumerate(total):
            out_ref[:, k * GROUP : (k + 1) * GROUP] = (part[there, :] * inverse[there, :]).astype(BF)


def feed_columns(weights, width):
    hidden = FOLD * width
    return (
        columns(weights, hidden, 4 * width),
        columns(weights, hidden, 4 * width + hidden),
        columns(weights, SMALL, weights.shape[1] - SMALL),
    )


def char_ffn(langs, blocks, first, place, after, hot, inverse, weights):
    rows, width = after.shape
    words = inverse.shape[0]
    hidden = FOLD * width
    return streamed(
        functools.partial(char_ffn_kernel, langs),
        (blocks, first, place),
        (after, hot),
        (inverse, *feed_columns(weights, width)),
        (((rows, hidden), BF), ((rows, hidden), BF)),
        (((words // 2, width), BF), ((words // 2, width), BF)),
        (((SMALL, width), F32),) + (((words + GROUP, GROUP), F32),) * (width // GROUP),
        pl.CostEstimate(
            flops=rows * width * width * 16, bytes_accessed=rows * width * 20, transcendentals=rows * 1024
        ),
    )


def sorted_rows(core, counts, rows, cuts=1, which=0):
    far, near = counts
    each = rows // (2 * far * near)
    some = each // cuts
    low = near // 2
    line = lax.broadcasted_iota(jnp.int32, (rows // (2 * cuts), rows), 0)
    inner = lax.rem(line, some)
    part = lax.div(line, some)
    at_far, at_near = lax.rem(part, far), lax.div(part, far)
    device = ((at_far * 2 + lax.div(at_near, low)) * low + lax.rem(at_near, low)) * 2 + core
    source = device * each + which * some + inner
    return (source == lax.broadcasted_iota(jnp.int32, source.shape, 1)).astype(F32).astype(BF)


def folding(back):
    size = FOLD * HEAD
    unit = lax.broadcasted_iota(jnp.int32, (size, size), 1 if back else 0)
    held = lax.broadcasted_iota(jnp.int32, (size, size), 0 if back else 1)
    return (held == (unit & (FOLD - 1)) * HEAD + lax.div(unit, FOLD)).astype(F32).astype(BF)


def unfold_into(out, folded, width):
    size = FOLD * HEAD
    matrix = folding(True)
    for m in range(width // HEAD):
        near = [folded[:, j * width + m * HEAD : j * width + (m + 1) * HEAD] for j in range(FOLD)]
        out[:, m * size : (m + 1) * size] = dot(jnp.concatenate(near, 1), matrix).astype(BF)


def char_ffn_back_kernel(
    settings,
    blocks,
    first,
    place,
    after_all,
    hot_all,
    act_all,
    slope_all,
    inverse,
    up_kept,
    up_sent,
    expand,
    reduced,
    small,
    grad_to_word,
    riding_kept,
    riding_sent,
    grad_after_all,
    kept_out,
    sent_out,
    sums,
    small_rows,
    grad_expand,
    grad_reduce,
    up_rows,
    grads,
    *spread_up,
):
    langs, counts = settings
    width = after_all.shape[1]
    hidden = FOLD * width
    local = up_kept.shape[0]
    small_rows[...] = small[...].astype(F32).T
    for up_in, row in ((up_kept, place[ROW]), (up_sent, 1 - place[ROW])):
        there = pl.ds(pl.multiple_of(row * local, local), local)
        for k, part in enumerate(spread_up):
            cols = slice(k * GROUP, (k + 1) * GROUP)
            part[there, :] = up_in[:, cols].astype(F32) * inverse[there, :]
    for part in spread_up:
        part[2 * local :, :] = jnp.zeros((GROUP, GROUP), F32)
    grad_expand[...] = jnp.zeros_like(grad_expand)
    grad_reduce[...] = jnp.zeros_like(grad_reduce)
    sums[...] = jnp.zeros_like(sums)

    def step(i, after, hot, act, slope, grad_after):
        for g in range(SPLIT):
            here = slice(g * GROUP, (g + 1) * GROUP)
            for k, part in enumerate(spread_up):
                words_here = part[pl.ds(first[i * SPLIT + g], GROUP), :].astype(BF)
                up_rows[here, k * GROUP : (k + 1) * GROUP] = dot(hot[here, :], words_here).astype(BF)
        up = up_rows[...]
        unit, spread = norm_parts(after[...])
        gain = small_rows[langs + 2 : langs + 3, :]
        normed = (unit * gain + small_rows[langs + 3 : langs + 4, :]).astype(BF)
        grad_normed = jnp.zeros((BLOCK, width), F32)
        parts = [slice(j * width, (j + 1) * width) for j in range(FOLD)]
        grad_acts = [
            dot_t(up, reduced[:, j * width : (j + 1) * width]) for j in range(FOLD)
        ]
        grad_pres = []
        for j, cols in enumerate(parts):
            grad_pre = grad_acts[j] * slope[:, cols].astype(F32)
            sums[8 * j : 8 * j + 8, :] += fold_rows(grad_pre)
            grad_pres.append(grad_pre.astype(BF))
        for j, grad_pre in enumerate(grad_pres):
            grad_normed = grad_normed + dot_t(grad_pre, expand[:, j * width : (j + 1) * width])
        turned = normed.T
        for cols, grad_pre in zip(parts, grad_pres):
            grad_expand[:, cols] += dot(turned, grad_pre)
        turned = up.T
        for cols in parts:
            grad_reduce[:, cols] += dot(turned, act[:, cols])
        up_wide = up.astype(F32)
        sums[32:40, :] += fold_rows(grad_normed * unit)
        sums[40:48, :] += fold_rows(grad_normed)
        sums[48:56, :] += fold_rows(up_wide)
        grad_after[...] = up_wide + norm_back(unit, spread, grad_normed * gain)

    run_blocks(step, 0, blocks[0], (after_all, hot_all, act_all, slope_all), (grad_after_all,))
    unfold_into(grads.at[:, :hidden], grad_expand[...].astype(BF), width)
    for j in range(FOLD):
        grads[:, hidden + j * width : hidden + (j + 1) * width] = (
            grad_reduce[:, j * width : (j + 1) * width].T.astype(BF)
        )
    grads[:, 2 * hidden :] = grad_to_word[...]
    own = grads.shape[1]
    for out_ref, riding, core in (
        (kept_out, riding_kept, place[CORE]),
        (sent_out, riding_sent, 1 - place[CORE]),
    ):
        out_ref[:, :own] = dot(sorted_rows(core, counts, width), grads[...]).astype(BF)
        out_ref[:, own:] = riding[...]


def char_ffn_back(
    settings,
    blocks,
    first,
    place,
    after,
    hot,
    act,
    slope,
    inverse,
    up_kept,
    up_sent,
    weights,
    grad_to_word,
    riding,
):
    rows, width = after.shape
    words = inverse.shape[0]
    hidden = FOLD * width
    span = 2 * hidden + grad_to_word.shape[1]
    return streamed(
        functools.partial(char_ffn_back_kernel, settings),
        (blocks, first, place),
        (after, hot, act, slope),
        (inverse, up_kept, up_sent, *feed_columns(weights, width), grad_to_word, *riding),
        (((rows, width), F32),),
        (((width // 2, span + riding[0].shape[1]), BF),) * 2 + (((64, width), F32),),
        (
            ((SMALL, width), F32),
            ((width, hidden), F32),
            ((width, hidden), F32),
            ((BLOCK, width), BF),
            ((width, span), BF),
        )
        + (((words + GROUP, GROUP), F32),) * (width // GROUP),
        pl.CostEstimate(
            flops=rows * width * width * 32, bytes_accessed=rows * width * 20, transcendentals=0
        ),
    )


def char_attend_back_kernel(settings, blocks, rows_of, ids, place, *refs):
    langs, counts = settings
    streams, refs = refs[:5], refs[5:]
    width = streams[0].shape[1]
    halves = width // GROUP
    (weights, small, sums_in), refs = refs[:3], refs[3:]
    start_all, refs = refs[:halves], refs[halves:]
    kept_out, sent_out, small_rows, grad_mixed, grad_qkv, grad_in, lines, grads = refs
    grad_in[...] = jnp.zeros_like(grad_in)
    lines[...] = jnp.zeros_like(lines)
    small_rows[...] = small[...].astype(F32).T

    def step(i, packed, qkv, soft, mixed, grad_after, *grad_start):
        start = with_language(i, rows_of, ids, packed, small_rows)
        unit, spread = norm_parts(start)
        gain = small_rows[langs : langs + 1, :]
        normed = (unit * gain + small_rows[langs + 1 : langs + 2, :]).astype(BF)
        after_low = grad_after[...].astype(BF)
        grad_in[:, 3 * width :] += t_dot(mixed[...], after_low)
        grad_mixed[...] = dot_t(after_low, weights[:, 3 * width : 4 * width]).astype(BF)
        lower = lax.broadcasted_iota(jnp.int32, (GROUP, GROUP), 1) < HEAD
        places = [(slice(g * GROUP, (g + 1) * GROUP), t) for g in range(SPLIT) for t in range(CHEADS // 2)]

        def tile_of(values, which, k):
            here, t = places[k]
            return values[here, which * width + t * GROUP : which * width + (t + 1) * GROUP]

        every = range(len(places))
        lows = [both_heads(tile_of(grad_mixed, 0, k), lower) for k in every]
        grad_softs = [dot_t(tile_of(qkv, 2, k), lows[k]) for k in every]
        weights_of = [soft[here, 2 * t * GROUP : (2 * t + 2) * GROUP] for here, t in places]
        ones = []
        for weight, grad_soft in zip(weights_of, grad_softs):
            wide = weight.astype(F32)
            ones.append((wide * (grad_soft - jnp.sum(wide * grad_soft, 0, keepdims=True))).astype(BF))
        for k, (here, t) in enumerate(places):
            value = dot(weights_of[k], lows[k])
            grad_qkv[here, 2 * width + t * GROUP : 2 * width + (t + 1) * GROUP] = value.astype(BF)
        for k, (here, t) in enumerate(places):
            value = dot(ones[k], both_heads(tile_of(qkv, 0, k), lower))
            grad_qkv[here, width + t * GROUP : width + (t + 1) * GROUP] = (value * SCALE).astype(BF)
        for k, (here, t) in enumerate(places):
            turned = jnp.concatenate([ones[k][:, :GROUP].T, ones[k][:, GROUP:].T], 1)
            value = dot(turned, both_heads(tile_of(qkv, 1, k), lower))
            grad_qkv[here, t * GROUP : (t + 1) * GROUP] = (value * SCALE).astype(BF)
        grad_in[:, : 3 * width] += t_dot(normed, grad_qkv[...])
        grad_normed = dot_t(grad_qkv[...], weights[:, : 3 * width])
        lines[SMALL : SMALL + 8, :] += fold_rows(grad_normed * unit)
        lines[SMALL + 8 :, :] += fold_rows(grad_normed)
        result = grad_after[...] + norm_back(unit, spread, grad_normed * gain)
        for k, part in enumerate(grad_start):
            part[...] = result[:, k * GROUP : (k + 1) * GROUP]
        for g in range(SPLIT):
            line = pl.ds(ids[rows_of[i * SPLIT + g]], 1)
            part = jnp.sum(result[g * GROUP : (g + 1) * GROUP, :], 0, keepdims=True)
            lines[line, :] = lines[line, :] + part

    run_blocks(step, 0, blocks[0], streams, start_all)

    def put(at, block):
        lines[langs + at : langs + at + 1, :] = jnp.sum(block, 0, keepdims=True)

    put(0, lines[SMALL : SMALL + 8, :])
    put(1, lines[SMALL + 8 :, :])
    put(2, sums_in[32:40, :])
    put(3, sums_in[40:48, :])
    put(4, sums_in[48:56, :])
    for j in range(FOLD):
        put(5 + j, sums_in[8 * j : 8 * j + 8, :])
    grads[:, : 4 * width] = grad_in[...].astype(BF)
    grads[:, 4 * width :] = lines[:SMALL, :].T.astype(BF)
    kept_out[...] = dot(sorted_rows(place[CORE], counts, width), grads[...]).astype(BF)
    sent_out[...] = dot(sorted_rows(1 - place[CORE], counts, width), grads[...]).astype(BF)


def char_attend_back(
    settings, blocks, rows_of, ids, place, packed, qkv, soft, mixed, grad_after, weights, sums
):
    rows, width = packed.shape
    span = 4 * width + SMALL
    return streamed(
        functools.partial(char_attend_back_kernel, settings),
        (blocks, rows_of, ids, place),
        (packed, qkv, soft, mixed, grad_after),
        (columns(weights, 4 * width, 0), columns(weights, SMALL, weights.shape[1] - SMALL), sums),
        (((rows + BLOCK, GROUP), F32),) * (width // GROUP),
        (((width // 2, span), BF),) * 2,
        (
            ((SMALL, width), F32),
            ((BLOCK, width), BF),
            ((BLOCK, 3 * width), BF),
            ((width, 4 * width), F32),
            ((SMALL + 16, width), F32),
            ((width, span), BF),
        ),
        pl.CostEstimate(
            flops=rows * width * width * 24, bytes_accessed=rows * width * 20, transcendentals=0
        ),
    )


def word_kernel(
    counts,
    members,
    place,
    char_weights,
    weights_all,
    cotangent,
    cotangent_other,
    *refs,
):
    pieces, refs = refs[: 2 * members], refs[2 * members :]
    away, refs = refs[:7], refs[7:]
    grad_query_out, sums_out = refs[:2]
    pair_outs, refs = refs[2 : 2 + members], refs[2 + members :]
    words_both, words_sent, grad_after_out, normed_out, word_in_out, kept_out, sent_out = refs[:7]
    sent_sem, weights, to_word, held_sem = refs[7:11]
    refs = refs[11:]
    (
        small_rows,
        pooled,
        word_all,
        normed_all,
        pair,
        query,
        blocked,
        soft_near,
        soft_far,
        mixed,
        after,
        unit_two,
        normed_two,
        up_low,
        total,
        grad_normed,
        grads,
        natural,
        grad_pair,
    ) = refs
    member = place[MEMBER]
    my_row = place[ROW]
    length = place[LENGTH]
    all_words, narrow = pooled.shape
    width = up_low.shape[1]
    own_words = up_low.shape[0]
    local = own_words // 2
    half = all_words // 2
    hidden = FOLD * width
    reach = (half, all_words)
    at_out, at_expand, at_reduce = 3 * width, 4 * width, 4 * width + hidden
    at_small = at_reduce + hidden
    at_to_word = columns_of(narrow, width)[2]

    def fetch(k, start, stop):
        return pltpu.make_async_copy(
            weights_all.at[:, start:stop], weights.at[:, start:stop], held_sem.at[k]
        )

    early = (
        pltpu.make_async_copy(char_weights.at[:, at_to_word : at_to_word + width], to_word, held_sem.at[0]),
        fetch(1, at_small, at_small + SMALL),
        fetch(2, 0, at_out),
    )
    late = (fetch(3, at_out, at_expand), fetch(4, at_expand, at_small))
    for copy in early + late:
        copy.start()
    leaving = [
        pltpu.make_async_copy(here, there, sent_sem.at[k])
        for k, (here, there) in enumerate(
            zip((words_both, words_sent, grad_after_out, normed_out, word_in_out, kept_out, sent_out), away)
        )
    ]
    for copy in early:
        copy.wait()
    small_rows[...] = weights[:, at_small:].astype(F32).T

    def rows_at(index):
        return pl.ds(pl.multiple_of(index * local, local), local)

    for m in range(members):
        there = jnp.bitwise_xor(member, m)
        pooled[rows_at(my_row * members + there), :] = pieces[2 * m][...]
        pooled[rows_at((1 - my_row) * members + there), :] = pieces[2 * m + 1][...]

    def embed(t, carry):
        here = pl.ds(pl.multiple_of(t * local, local), local)
        value = dot(pooled[here, :], to_word[...]) + small_rows[5:6, :]
        word_all[here, :] = value
        unit, _ = norm_parts(value)
        normed = (unit * small_rows[0:1, :] + small_rows[1:2, :]).astype(BF)
        normed_all[here, :] = normed
        pair[here, :] = dot(normed, weights[:, width : 3 * width]).astype(BF)
        return carry

    lax.fori_loop(0, all_words // local, embed, 0, unroll=4)
    origin = []
    for t in range(2):
        base = member * local + t * half
        origin.append(base)
        here = slice(t * local, (t + 1) * local)
        word_in_out[here, :] = word_all[rows_at(member + t * members), :]
        normed_out[here, :] = normed_all[rows_at(member + t * members), :]
    leaving[3].start()
    leaving[4].start()
    query[...] = dot(normed_out[...], weights[:, :width]).astype(BF)
    masks = head_masks(GROUP, 2)
    softs = (soft_near, soft_far)

    for t in range(2):
        seen = lax.broadcasted_iota(jnp.int32, (local, reach[t]), 1)
        asks = lax.broadcasted_iota(jnp.int32, (local, reach[t]), 0) + origin[t]
        blocked[t * local : (t + 1) * local, : reach[t]] = jnp.where((seen <= asks) & (seen < length), 0.0, MASKED)
    chains = [(slice(t * local, (t + 1) * local), t, h) for t in range(2) for h in range(2)]

    def attend(p, carry):
        lanes = pl.ds(pl.multiple_of(p * GROUP, GROUP), GROUP)
        after_lanes = pl.ds(pl.multiple_of(width + p * GROUP, GROUP), GROUP)
        scores = [dot_t(query[here, lanes] * masks[h], pair[: reach[t], lanes]) for here, t, h in chains]
        weights_of = []
        for (here, t, h), score in zip(chains, scores):
            score = score * SCALE + blocked[here, : reach[t]]
            score = jnp.exp(score - jnp.max(score, -1, keepdims=True))
            soft = (score * (1.0 / jnp.sum(score, -1, keepdims=True))).astype(BF)
            softs[t][2 * p + h] = soft
            weights_of.append(soft)
        outs = [
            dot(soft, pair[: reach[t], after_lanes] * masks[h])
            for (_, t, h), soft in zip(chains, weights_of)
        ]
        for t in range(2):
            mixed[t * local : (t + 1) * local, lanes] = (outs[2 * t] + outs[2 * t + 1]).astype(BF)
        return carry

    lax.fori_loop(0, WHEADS // 2, attend, 0, unroll=4)
    for copy in late:
        copy.wait()
    value = word_in_out[...] + dot(mixed[...], weights[:, at_out : at_out + width])
    after[...] = value
    unit, spread = norm_parts(value)
    unit_two[...] = unit
    normed_two[...] = (unit * small_rows[2:3, :] + small_rows[3:4, :]).astype(BF)
    row = lax.broadcasted_iota(jnp.int32, (own_words, 1), 0)
    index = jnp.where(row < local, origin[0] + row, origin[1] + row - local)
    valid = index < length
    up_low[rows_at(my_row), :] = cotangent[my_row]
    up_low[rows_at(1 - my_row), :] = cotangent_other[...]
    up_low[...] = jnp.where(valid, up_low[...].astype(F32), 0.0).astype(BF)
    total[...] = jnp.zeros_like(total)
    grad_normed[...] = jnp.zeros_like(grad_normed)

    def feed(j, carry):
        expand = weights[:, pl.ds(pl.multiple_of(at_expand + j * width, GROUP), width)]
        shrink = weights[:, pl.ds(pl.multiple_of(at_reduce + j * width, GROUP), width)]
        pre = dot(normed_two[...], expand) + small_rows[pl.ds(6 + j, 1), :]
        act, slope = gelu_both(pre)
        act = act.astype(BF)
        total[...] += dot(act, shrink)
        grad_pre = dot_t(up_low[...], shrink) * slope
        sums_out[pl.ds(6 + j, 1), :] = jnp.sum(grad_pre, 0, keepdims=True)
        grad_pre = grad_pre.astype(BF)
        grad_normed[...] += dot_t(grad_pre, expand)
        cols = pl.multiple_of(j * width, GROUP)
        grads[:, pl.ds(cols, width)] = t_dot(normed_two[...], grad_pre).astype(BF)
        grads[:, pl.ds(pl.multiple_of(hidden + j * width, GROUP), width)] = t_dot(
            act, up_low[...]
        ).astype(BF)
        return carry

    lax.fori_loop(0, FOLD, feed, 0, unroll=4)
    total[...] = jnp.where(valid, after[...] + (total[...] + small_rows[4:5, :]), 0.0)
    for t in range(2):
        words_both[t] = total[t * local : (t + 1) * local, :]
    words_sent[...] = total[rows_at(1 - my_row), :]
    leaving[0].start()
    leaving[1].start()
    upstream = up_low[...].astype(F32)
    incoming = grad_normed[...]
    sums_out[2:3, :] = jnp.sum(incoming * unit_two[...], 0, keepdims=True)
    sums_out[3:4, :] = jnp.sum(incoming, 0, keepdims=True)
    sums_out[4:5, :] = jnp.sum(upstream, 0, keepdims=True)
    grad_after = upstream + norm_back(unit_two[...], spread, incoming * small_rows[2:3, :])
    grad_after_out[...] = grad_after
    leaving[2].start()
    grad_low = grad_after.astype(BF)
    grads[:, 2 * hidden :] = t_dot(mixed[...], grad_low).astype(BF)
    mixed[...] = dot_t(grad_low, weights[:, at_out : at_out + width]).astype(BF)
    unfold_into(natural, grads[:, :hidden], width)
    for out_ref, core in ((kept_out, place[CORE]), (sent_out, 1 - place[CORE])):
        chosen = sorted_rows(core, counts, width)
        out_ref[:, :hidden] = dot(chosen, natural[...]).astype(BF)
        out_ref[:, hidden:] = dot(chosen, grads[:, hidden:]).astype(BF)
    leaving[5].start()
    leaving[6].start()

    def attend_back(p, carry):
        lanes = pl.ds(pl.multiple_of(p * GROUP, GROUP), GROUP)
        after_lanes = pl.ds(pl.multiple_of(width + p * GROUP, GROUP), GROUP)
        lows = [mixed[here, lanes] * masks[h] for here, t, h in chains]
        ones = [dot_t(low, pair[: reach[t], after_lanes]) for low, (_, t, h) in zip(lows, chains)]
        weights_of = [softs[t][2 * p + h] for _, t, h in chains]
        grads_of = []
        for one, soft in zip(ones, weights_of):
            wide = soft.astype(F32)
            grads_of.append((wide * (one - jnp.sum(wide * one, -1, keepdims=True))).astype(BF))
        grad_values = [dot(soft.T, low) for soft, low in zip(weights_of, lows)]
        grad_keys = [
            dot(one.T, query[here, lanes] * masks[h]) for one, (here, t, h) in zip(grads_of, chains)
        ]
        grad_queries = [
            dot(one, pair[: reach[t], lanes] * masks[h]) for one, (_, t, h) in zip(grads_of, chains)
        ]
        grad_values = [grad_values[2 * t] + grad_values[2 * t + 1] for t in range(2)]
        grad_keys = [grad_keys[2 * t] + grad_keys[2 * t + 1] for t in range(2)]
        for t in range(2):
            grad_query = grad_queries[2 * t] + grad_queries[2 * t + 1]
            grad_query_out[t * local : (t + 1) * local, lanes] = (grad_query * SCALE).astype(BF)
        for parts, at, factor in ((grad_keys, lanes, SCALE), (grad_values, after_lanes, 1.0)):
            grad_pair[:half, at] = ((parts[0] + parts[1][:half]) * factor).astype(BF)
            grad_pair[half:, at] = (parts[1][half:] * factor).astype(BF)
        return carry

    lax.fori_loop(0, WHEADS // 2, attend_back, 0)
    for m in range(members):
        there = jnp.bitwise_xor(member, m)
        for t in range(2):
            pair_outs[m][t * local : (t + 1) * local, :] = grad_pair[rows_at(t * members + there), :]
    for copy in leaving:
        copy.wait()


def word_part(counts, place, pieces, char_weights, weights, cotangent, cotangent_other):
    members = len(pieces) // 2
    local, narrow = pieces[0].shape
    all_words = local * len(pieces)
    width = cotangent.shape[2]
    own = 2 * local
    hidden = FOLD * width
    vmem = pl.BlockSpec(memory_space=pltpu.VMEM)
    hbm = pl.BlockSpec(memory_space=pltpu.HBM)
    share = ((width // 2, 2 * hidden + width), BF)
    away = (
        ((2, local, width), F32),
        ((local, width), F32),
        ((own, width), F32),
        ((own, width), BF),
        ((own, width), F32),
        share,
        share,
    )
    stay = (((own, width), BF), ((16, width), F32)) + (((own, 2 * width), BF),) * members
    return pl.pallas_call(
        functools.partial(word_kernel, counts, members),
        out_shape=tuple(jax.ShapeDtypeStruct(*out) for out in away + stay),
        in_specs=[pl.BlockSpec(memory_space=pltpu.SMEM), hbm, hbm] + [vmem] * (2 + len(pieces)),
        out_specs=(hbm,) * len(away) + (vmem,) * len(stay),
        scratch_shapes=[pltpu.VMEM(*out) for out in away]
        + [
            pltpu.SemaphoreType.DMA((len(away),)),
            pltpu.VMEM(weights.shape, BF),
            pltpu.VMEM((narrow, width), BF),
            pltpu.SemaphoreType.DMA((5,)),
            pltpu.VMEM((SMALL, width), F32),
            pltpu.VMEM((all_words, narrow), BF),
            pltpu.VMEM((all_words, width), F32),
            pltpu.VMEM((all_words, width), BF),
            pltpu.VMEM((all_words, 2 * width), BF),
            pltpu.VMEM((own, width), BF),
            pltpu.VMEM((own, all_words), F32),
            pltpu.VMEM((WHEADS, local, all_words // 2), BF),
            pltpu.VMEM((WHEADS, local, all_words), BF),
            pltpu.VMEM((own, width), BF),
            pltpu.VMEM((own, width), F32),
            pltpu.VMEM((own, width), F32),
            pltpu.VMEM((own, width), BF),
            pltpu.VMEM((own, width), BF),
            pltpu.VMEM((own, width), F32),
            pltpu.VMEM((own, width), F32),
            pltpu.VMEM((width, 2 * hidden + width), BF),
            pltpu.VMEM((width, hidden), BF),
            pltpu.VMEM((all_words, 2 * width), BF),
        ],
        compiler_params=pltpu.CompilerParams(vmem_limit_bytes=VMEM_LIMIT),
        cost_estimate=pl.CostEstimate(
            flops=own * width * width * 60, bytes_accessed=20 * MIB, transcendentals=own * 8192
        ),
    )(place, char_weights, weights, cotangent, cotangent_other, *pieces)


def word_end_kernel(
    counts,
    place,
    pooled_kept,
    pooled_other,
    to_word_ref,
    weights,
    small,
    grad_query,
    normed,
    word_in,
    grad_after,
    sums,
    *refs,
):
    pairs, refs = refs[:-8], refs[-8:]
    up_kept, up_sent, grad_to_word, kept_out, sent_out, small_rows, small_grads, incoming = refs
    width = grad_query.shape[1]
    local, narrow = pooled_kept.shape
    to_word = to_word_ref[...]
    small_rows[...] = small[...].astype(F32).T
    incoming[:, :width] = grad_query[...]
    pair = pairs[0][...].astype(F32)
    for other in pairs[1:]:
        pair = pair + other[...].astype(F32)
    incoming[:, width:] = pair.astype(BF)
    grad_normed = dot_t(incoming[...], weights[...])
    unit, spread = norm_parts(word_in[...])
    small_grads[...] = jnp.zeros_like(small_grads)
    small_grads[0:1, :] = jnp.sum(grad_normed * unit, 0, keepdims=True)
    small_grads[1:2, :] = jnp.sum(grad_normed, 0, keepdims=True)
    small_grads[2:5, :] = sums[2:5, :]
    small_grads[6:10, :] = sums[6:10, :]
    value = grad_after[...] + norm_back(unit, spread, grad_normed * small_rows[0:1, :])
    small_grads[5:6, :] = jnp.sum(value, 0, keepdims=True)
    low = value.astype(BF)
    back = dot_t(low, to_word).astype(BF)
    first_half = place[ROW] == 0
    up_kept[...] = jnp.where(first_half, back[:local].astype(F32), back[local:].astype(F32)).astype(BF)
    up_sent[...] = jnp.where(first_half, back[local:].astype(F32), back[:local].astype(F32)).astype(BF)
    low_kept = jnp.where(first_half, value[:local], value[local:]).astype(BF)
    low_other = jnp.where(first_half, value[local:], value[:local]).astype(BF)
    grad_to_word[...] = (t_dot(pooled_kept[...], low_kept) + t_dot(pooled_other[...], low_other)).astype(BF)
    inward = t_dot(normed[...], incoming[...]).astype(BF)
    small_turned = small_grads[...].T.astype(BF)
    span = 3 * width + SMALL
    for out_ref, core in ((kept_out, place[CORE]), (sent_out, 1 - place[CORE])):
        for k in range(width // narrow):
            chosen = sorted_rows(core, counts, width, width // narrow, k)
            out_ref[:, k * span : k * span + 3 * width] = dot(chosen, inward).astype(BF)
            out_ref[:, k * span + 3 * width : (k + 1) * span] = dot(chosen, small_turned).astype(BF)


def word_end(
    counts,
    place,
    pooled_kept,
    pooled_other,
    char_weights,
    weights,
    grad_query,
    normed,
    word_in,
    grad_after,
    sums,
    pairs,
):
    local, narrow = pooled_kept.shape
    own, width = grad_query.shape
    last = weights.shape[1] // SMALL - 1
    share = (narrow // 2, (3 * width + SMALL) * (width // narrow))
    outs = ((local, narrow), (local, narrow), (narrow, width), share, share)
    operands = (grad_query, normed, word_in, grad_after, sums) + tuple(pairs)
    return pl.pallas_call(
        functools.partial(word_end_kernel, counts),
        out_shape=tuple(jax.ShapeDtypeStruct(shape, BF) for shape in outs),
        grid_spec=pltpu.PrefetchScalarGridSpec(
            num_scalar_prefetch=1,
            grid=(1,),
            in_specs=[
                full(pooled_kept.shape),
                full(pooled_other.shape),
                columns(char_weights, width, columns_of(narrow, width)[2])[1],
                pl.BlockSpec((width, 3 * width), lambda i, *_: (0, 0)),
                pl.BlockSpec((width, SMALL), lambda i, *_: (0, last)),
            ]
            + [full(operand.shape) for operand in operands],
            out_specs=tuple(full(shape) for shape in outs),
            scratch_shapes=[
                pltpu.VMEM((SMALL, width), F32),
                pltpu.VMEM((SMALL, width), F32),
                pltpu.VMEM((own, 3 * width), BF),
            ],
        ),
        compiler_params=pltpu.CompilerParams(vmem_limit_bytes=VMEM_LIMIT),
        cost_estimate=pl.CostEstimate(
            flops=own * width * width * 14, bytes_accessed=10 * MIB, transcendentals=0
        ),
    )(place, pooled_kept, pooled_other, char_weights, weights, weights, *operands)


def column(vector, rows):
    each = vector.shape[0] // rows
    wide = vector[...].astype(F32).reshape(1, rows * each)
    line = lax.broadcasted_iota(jnp.int32, (rows, rows * each), 0)
    lane = lax.broadcasted_iota(jnp.int32, (rows, rows * each), 1)
    return [
        jnp.sum(jnp.where(line * each + j == lane, wide, 0.0), 1, keepdims=True) for j in range(each)
    ]


def columns_beside(rows, vectors, at):
    lane = lax.broadcasted_iota(jnp.int32, (rows, SMALL), 1)
    block = jnp.zeros((rows, SMALL), F32)
    for vector in vectors:
        for one in column(vector, rows):
            block = block + jnp.where(lane == at, one, 0.0)
            at += 1
    return block


def fold_into(out, at, weights, width):
    size = FOLD * HEAD
    matrix = folding(False)
    for m in range(width // HEAD):
        block = dot(weights[:, m * size : (m + 1) * size], matrix).astype(BF)
        for j in range(FOLD):
            there = at + j * width + m * HEAD
            out[:, there : there + HEAD] = block[:, j * HEAD : (j + 1) * HEAD]


def fold_shard(weights):
    tall = weights.shape[0]
    rows = tall // FOLD
    line = lax.broadcasted_iota(jnp.int32, (rows, tall), 0)
    lane = lax.broadcasted_iota(jnp.int32, (rows, tall), 1)
    return [
        dot((lane == FOLD * line + j).astype(F32).astype(BF), weights[...]).astype(BF) for j in range(FOLD)
    ]


def char_shard_kernel(table, inward, outward, expand, reduced, to_word, *refs):
    vectors, out = refs[:-1], refs[-1]
    rows, langs = table.shape
    width = outward.shape[1]
    at_expand, at_reduce, at_to_word, at_small = columns_of(width, to_word.shape[1])
    out[:, : 3 * width] = inward[...]
    out[:, 3 * width : 4 * width] = outward[...]
    line = lax.broadcasted_iota(jnp.int32, (langs, SMALL), 0)
    lane = lax.broadcasted_iota(jnp.int32, (langs, SMALL), 1)
    spread = (line == lane).astype(F32).astype(BF)
    small = dot(table[...], spread) + columns_beside(rows, vectors, langs)
    out[:, at_small:] = small.astype(BF)
    fold_into(out, at_expand, expand, width)
    for j, part in enumerate(fold_shard(reduced)):
        out[:, at_reduce + j * width : at_reduce + (j + 1) * width] = part
    out[:, at_to_word:at_small] = to_word[...]


def char_shard(table, inward, outward, expand, reduced, to_word, vectors):
    rows, width = outward.shape
    vmem = pl.BlockSpec(memory_space=pltpu.VMEM)
    return pl.pallas_call(
        char_shard_kernel,
        out_shape=jax.ShapeDtypeStruct((rows, columns_of(width, to_word.shape[1])[3] + SMALL), BF),
        in_specs=[vmem] * (6 + len(vectors)),
        out_specs=vmem,
    )(table, inward, outward, expand, reduced, to_word, *vectors)


def word_shard_kernel(inward, outward, expand, reduced, *refs):
    vectors, out = refs[:-1], refs[-1]
    rows, width = outward.shape
    out[:, : 3 * width] = inward[...]
    out[:, 3 * width : 4 * width] = outward[...]
    fold_into(out, 4 * width, expand, width)
    for j, part in enumerate(fold_shard(reduced)):
        out[:, (8 + j) * width : (9 + j) * width] = part
    out[:, 12 * width :] = columns_beside(rows, vectors, 0).astype(BF)


def word_shard(inward, outward, expand, reduced, vectors):
    rows, width = outward.shape
    vmem = pl.BlockSpec(memory_space=pltpu.VMEM)
    return pl.pallas_call(
        word_shard_kernel,
        out_shape=jax.ShapeDtypeStruct((rows, 12 * width + SMALL), BF),
        in_specs=[vmem] * (4 + len(vectors)),
        out_specs=vmem,
    )(inward, outward, expand, reduced, *vectors)


def assemble_kernel(masks, index, *refs):
    pieces, out = refs[:-1], refs[-1]
    me = index[0]
    size = pieces[0].shape[0]
    for k, piece in enumerate(pieces):
        for t in range(size):
            out[jnp.bitwise_xor(me, masks[k * size + t])] = piece[t]


def assemble(masks, index, pieces):
    size, rows, columns = pieces[0].shape
    vmem = pl.BlockSpec(memory_space=pltpu.VMEM)
    out = pl.pallas_call(
        functools.partial(assemble_kernel, tuple(masks)),
        out_shape=jax.ShapeDtypeStruct((size * len(pieces), rows, columns), BF),
        in_specs=[pl.BlockSpec(memory_space=pltpu.SMEM)] + [vmem] * len(pieces),
        out_specs=vmem,
        compiler_params=pltpu.CompilerParams(vmem_limit_bytes=VMEM_LIMIT),
        cost_estimate=pl.CostEstimate(
            flops=0, bytes_accessed=4 * size * len(pieces) * rows * columns, transcendentals=0
        ),
    )(index, *pieces)
    return out.reshape(-1, columns)


def add_and_cut_kernel(which, arrivals, place, *refs):
    arrived, outs = refs[:arrivals], refs[arrivals:]
    total = arrived[0][...].astype(F32)
    for one in arrived[1:]:
        total = total + one[...].astype(F32)
    total = total.astype(BF)
    rows = total.shape[0]
    each = rows // len(outs)
    line = lax.broadcasted_iota(jnp.int32, (each, rows), 0)
    lane = lax.broadcasted_iota(jnp.int32, (each, rows), 1)
    for m, out in enumerate(outs):
        chosen = (lane == jnp.bitwise_xor(place[which], m) * each + line).astype(F32).astype(BF)
        out[...] = dot(chosen, total).astype(BF)


def add_and_cut(arrived, parts, which, place):
    rows, columns = arrived[0].shape

    vmem = pl.BlockSpec(memory_space=pltpu.VMEM)
    return pl.pallas_call(
        functools.partial(add_and_cut_kernel, which, len(arrived)),
        out_shape=(jax.ShapeDtypeStruct((rows // parts, columns), BF),) * parts,
        in_specs=[pl.BlockSpec(memory_space=pltpu.SMEM)] + [vmem] * len(arrived),
        out_specs=(vmem,) * parts,
        compiler_params=pltpu.CompilerParams(vmem_limit_bytes=VMEM_LIMIT),
        cost_estimate=pl.CostEstimate(
            flops=0, bytes_accessed=sum(4 * one.size for one in arrived), transcendentals=0
        ),
    )(place, *arrived)


def unfold_rows(folded, rows, out):
    width = out.shape[1]
    line = lax.broadcasted_iota(jnp.int32, (FOLD * rows, rows), 0)
    lane = lax.broadcasted_iota(jnp.int32, (FOLD * rows, rows), 1)
    total = jnp.zeros(out.shape, F32)
    for j in range(FOLD):
        chosen = (line == FOLD * lane + j).astype(F32)
        total = total + lax.dot_general(
            chosen,
            folded[:, j * width : (j + 1) * width],
            (((1,), (0,)), ((), ())),
            precision=lax.Precision.HIGHEST,
            preferred_element_type=F32,
        )
    out[...] = total


def finish_kernel(plan, count, *refs):
    arrived, outs = refs[:count], refs[count:]
    total = arrived[0][...].astype(F32)
    for one in arrived[1:]:
        total = total + one[...].astype(F32)
    rows = total.shape[0]
    for (kind, start, stop), out in zip(plan, outs):
        if kind == "folded":
            unfold_rows(total[:, start:stop], rows, out)
        elif kind == "plain":
            out[...] = total[:, start:stop]
        elif kind == "halves":
            height, width = out.shape
            pieces = height // rows
            stride = (stop - start) // pieces
            for k in range(pieces):
                out[k * rows : (k + 1) * rows, :] = total[:, start + k * stride : start + k * stride + width]
        else:
            pieces = stop[0]
            height = rows * pieces
            each = out.shape[0] // height
            value = jnp.zeros((1, out.shape[0]), F32)
            for k in range(pieces):
                block = total[:, start + k * stop[1] : start + k * stop[1] + SMALL]
                line = lax.broadcasted_iota(jnp.int32, (rows, out.shape[0]), 0) + k * rows
                lane = lax.broadcasted_iota(jnp.int32, (rows, out.shape[0]), 1)
                for j in range(each):
                    at = stop[2] + j
                    found = jnp.where(lane == line * each + j, block[:, at : at + 1], 0.0)
                    value = value + jnp.sum(found, 0, keepdims=True)
            out[...] = value.reshape(out.shape[0])


def finish(arrived, plan):
    vmem = pl.BlockSpec(memory_space=pltpu.VMEM)
    return pl.pallas_call(
        functools.partial(finish_kernel, tuple(one[:3] for one in plan), len(arrived)),
        out_shape=tuple(jax.ShapeDtypeStruct(shape, F32) for _, _, _, shape in plan),
        in_specs=[vmem] * len(arrived),
        out_specs=(vmem,) * len(plan),
        compiler_params=pltpu.CompilerParams(vmem_limit_bytes=VMEM_LIMIT),
    )(*arrived)


def tie(values, after):
    return lax.optimization_barrier((values, after))[0]


def body(
    char_inputs,
    language_ids,
    char_counts,
    row_lengths,
    cotangent,
    language_table,
    char_gain_one,
    char_bias_one,
    char_inward,
    char_outward,
    char_gain_two,
    char_bias_two,
    char_expand,
    char_expand_bias,
    char_reduce,
    char_reduce_bias,
    char_to_word,
    char_to_word_bias,
    word_gain_one,
    word_bias_one,
    word_inward,
    word_outward,
    word_gain_two,
    word_bias_two,
    word_expand,
    word_expand_bias,
    word_reduce,
    word_reduce_bias,
):
    rows, local, slots, width = char_inputs.shape
    words = rows * local
    langs = language_table.shape[0]
    wide = word_inward.shape[1] // 3
    deep, share = lax.axis_size("dp"), lax.axis_size("fsdp")
    devices = deep * share
    members = share // rows
    axes = ("dp", "fsdp")
    at_deep, at_share = lax.axis_index("dp"), lax.axis_index("fsdp")

    def swap(values, mask):
        return lax.ppermute(values, axes, [(k, k ^ mask) for k in range(devices)])

    far, low = deep // 2, share // 2
    near = 2 * low
    far_masks = [m * 2 * share for m in range(far)]
    near_masks = [(m // low) * share + (m % low) * 2 for m in range(near)]
    core_masks = [0, 1]
    counts_of = (far, near)
    top = members
    my_row = at_share // members
    index = (at_deep * share + at_share).reshape(1)

    def swaps(values, masks):
        return [values] + [swap(values, m) for m in masks[1:]]

    def together(pieces, rows):
        return jnp.stack(pieces).reshape(-1, rows, pieces[0].shape[-1])

    order = [c | n | f for c in core_masks for n in near_masks for f in far_masks]

    char_piece = char_shard(
        language_table.T,
        char_inward,
        char_outward,
        char_expand,
        char_reduce,
        char_to_word,
        (char_gain_one, char_bias_one, char_gain_two, char_bias_two, char_reduce_bias, char_expand_bias),
    )
    each = char_piece.shape[0]
    counts = tie(char_counts, char_piece)
    offs, first, rows_of, blocks, place = offsets((share, members), counts, row_lengths, index, slots)
    char_piece = together(tie(swaps(char_piece, far_masks), offs), each)
    packed, bias, hot = pack(
        tie(counts, char_piece), offs, first, blocks, char_inputs.reshape(words, slots, width)
    )
    char_piece = together(swaps(char_piece, near_masks), each)
    char_full = assemble(order, index, swaps(tie(char_piece, packed), core_masks))
    word_full = lax.all_gather(
        word_shard(
            word_inward,
            word_outward,
            word_expand,
            word_reduce,
            (
                word_gain_one,
                word_bias_one,
                word_gain_two,
                word_bias_two,
                word_reduce_bias,
                char_to_word_bias,
                word_expand_bias,
            ),
        ),
        axes,
        axis=0,
        tiled=True,
    )

    inverse = 1.0 / char_counts.astype(F32).reshape(words, 1)
    qkv, soft, mixed, after, cotangent_sent = char_attend(
        langs, blocks, rows_of, language_ids, place, packed, bias, char_full, cotangent
    )
    cotangent_other = swap(cotangent_sent, top)
    act, slope, pooled_kept, pooled_sent = char_ffn(
        langs, blocks, first, place, after, hot, inverse, char_full
    )
    cotangent_other, pooled_kept, pooled_sent = lax.optimization_barrier(
        (cotangent_other, pooled_kept, pooled_sent)
    )
    pooled_other = swap(pooled_sent, top)
    pieces = []
    for m in range(members):
        pieces += [swap(pooled_kept, m), swap(pooled_other, m)] if m else [pooled_kept, pooled_other]
    words_both, words_sent, word_after_grad, word_normed, word_in, word_kept, word_sent, *others = word_part(
        counts_of, place, pieces, char_full, word_full, cotangent, cotangent_other
    )
    query_grad, word_sums, *pair_grads = others
    pairs = [pair_grads[0]] + [swap(pair_grads[m], m) for m in range(1, members)]
    word_sent, words_sent, pairs = lax.optimization_barrier((word_sent, words_sent, pairs))
    words_other = swap(words_sent, top)
    word_arrived = [word_kept, swap(word_sent, 1)]
    up_kept, up_sent, to_word_grad, inward_kept, inward_sent = word_end(
        counts_of,
        place,
        pooled_kept,
        pooled_other,
        char_full,
        word_full,
        query_grad,
        word_normed,
        word_in,
        word_after_grad,
        word_sums,
        pairs,
    )
    up_other = swap(up_sent, top)

    def phase(parts, masks):
        return [parts[0]] + [swap(parts[m], masks[m]) for m in range(1, len(masks))]

    word_parts = add_and_cut(word_arrived, near, NEAR, place)
    word_parts, words_other = lax.optimization_barrier((word_parts, words_other))
    up_kept = tie(up_kept, word_parts)
    after_grad, feed_kept, feed_sent, char_sums = char_ffn_back(
        (langs, counts_of),
        blocks,
        first,
        place,
        after,
        hot,
        act,
        slope,
        inverse,
        up_kept,
        up_other,
        char_full,
        to_word_grad,
        (inward_kept, inward_sent),
    )
    word_parts = add_and_cut(tie(phase(word_parts, near_masks), feed_kept), far, FAR, place)
    feed_sent = tie(feed_sent, word_parts)
    late_parts = add_and_cut([feed_kept, swap(feed_sent, 1)], near, NEAR, place)
    after_grad = tie(after_grad, (word_parts, late_parts))
    operands = (packed, qkv, soft, mixed, after_grad, char_full, char_sums)
    *start_grad, attend_kept, attend_sent = char_attend_back(
        (langs, counts_of), blocks, rows_of, language_ids, place, *operands
    )
    arrived_words, arrived_late, attend_kept, attend_sent = lax.optimization_barrier(
        (phase(word_parts, far_masks), phase(late_parts, near_masks), attend_kept, attend_sent)
    )
    late_parts = add_and_cut(arrived_late, far, FAR, place)
    hidden, wide_hidden = FOLD * width, FOLD * wide
    grad_word_expand, grad_word_reduce, grad_word_outward = finish(
        arrived_words,
        (
            ("plain", 0, wide_hidden, word_expand.shape),
            ("folded", wide_hidden, 2 * wide_hidden, word_reduce.shape),
            ("plain", 2 * wide_hidden, 2 * wide_hidden + wide, word_outward.shape),
        ),
    )
    words_out = lax.dynamic_update_index_in_dim(words_both, words_other, 1 - my_row, 0)
    earlier = (words_out, grad_word_expand, grad_word_reduce, grad_word_outward)
    arrived, earlier, late_parts = lax.optimization_barrier(
        ([attend_kept, swap(attend_sent, 1)], earlier, late_parts)
    )
    attend_parts = add_and_cut(arrived, near, NEAR, place)
    char_input_grad = unpack(offs, char_counts, tie(start_grad, attend_parts), slots)
    arrived, arrived_late, char_input_grad = lax.optimization_barrier(
        (phase(attend_parts, near_masks), phase(late_parts, far_masks), char_input_grad)
    )
    attend_parts = add_and_cut(arrived, far, FAR, place)
    char_input_grad = unpack(offs, char_counts, tie(start_grad, attend_parts), slots, char_input_grad)
    arrived, arrived_late, char_input_grad = lax.optimization_barrier(
        (phase(attend_parts, far_masks), arrived_late, char_input_grad)
    )
    at_inward = 2 * hidden + wide
    stop = at_inward + (3 * wide + SMALL) * (wide // width)
    grad_expand, grad_reduce, grad_to_word, grad_word_inward, *word_vectors = finish(
        arrived_late,
        (
            ("plain", 0, hidden, char_expand.shape),
            ("folded", hidden, 2 * hidden, char_reduce.shape),
            ("plain", 2 * hidden, at_inward, char_to_word.shape),
            ("halves", at_inward, stop, word_inward.shape),
        )
        + tuple(
            ("vector", at_inward + 3 * wide, (wide // width, 3 * wide + SMALL, at), vector.shape)
            for at, vector in (
                (0, word_gain_one),
                (1, word_bias_one),
                (2, word_gain_two),
                (3, word_bias_two),
                (4, word_reduce_bias),
                (5, char_to_word_bias),
                (6, word_expand_bias),
            )
        ),
    )
    grad_inward, grad_outward, grad_table, *char_vectors = finish(
        arrived,
        (
            ("plain", 0, 3 * width, char_inward.shape),
            ("plain", 3 * width, 4 * width, char_outward.shape),
            ("plain", 4 * width, 4 * width + langs, (char_inward.shape[0], langs)),
        )
        + tuple(
            ("vector", 4 * width, (1, 0, langs + at), vector.shape)
            for at, vector in (
                (0, char_gain_one),
                (1, char_bias_one),
                (2, char_gain_two),
                (3, char_bias_two),
                (4, char_reduce_bias),
                (5, char_expand_bias),
            )
        ),
    )
    words_out, grad_word_expand, grad_word_reduce, grad_word_outward = earlier

    gain_one, bias_one, gain_two, bias_two, reduce_bias, expand_bias = char_vectors
    wide_gain_one, wide_bias_one, wide_gain_two, wide_bias_two, wide_reduce_bias = word_vectors[:5]
    to_word_bias, wide_expand_bias = word_vectors[5:]
    return (
        words_out,
        char_input_grad.reshape(char_inputs.shape),
        grad_table.T,
        gain_one,
        bias_one,
        grad_inward,
        grad_outward,
        gain_two,
        bias_two,
        grad_expand,
        expand_bias,
        grad_reduce,
        reduce_bias,
        grad_to_word,
        to_word_bias,
        wide_gain_one,
        wide_bias_one,
        grad_word_inward,
        grad_word_outward,
        wide_gain_two,
        wide_bias_two,
        grad_word_expand,
        wide_expand_bias,
        grad_word_reduce,
        wide_reduce_bias,
    )


def solution(mesh):
    both = ("dp", "fsdp")
    vector, matrix = P(both), P(both, None)
    weights = (
        (P(None, both), vector, vector, matrix, matrix, vector, vector)
        + (matrix, vector, matrix, vector, matrix, vector)
        + (vector, vector, matrix, matrix, vector, vector, matrix, vector, matrix, vector)
    )
    in_specs = (
        P("dp", "fsdp", None, None),
        P("dp"),
        P("dp", "fsdp"),
        P("dp"),
        P("dp", "fsdp", None),
    ) + weights
    out_specs = (P("dp", "fsdp", None), P("dp", "fsdp", None, None)) + weights
    return jax.shard_map(body, mesh=mesh, in_specs=in_specs, out_specs=out_specs, check_vma=False)
```

```python
import functools

import jax
import jax.numpy as jnp
from jax import lax
from jax.experimental import pallas as pl
from jax.experimental.pallas import tpu as pltpu
from jax.sharding import PartitionSpec as P

BF = jnp.bfloat16
F32 = jnp.float32
EPS = 1e-05
MASKED = -1e30
CHEADS = 4
WHEADS = 8
HEAD = 64
SCALE = HEAD ** (-0.5)
GROUP = 128
GROUP_BITS = 7
BLOCK = 1024
SPLIT = BLOCK // GROUP
FOLD = 4
SMALL = 128
GELU_A = 0.7978845608028654
GELU_B = 0.044715
MIB = 1024 * 1024
VMEM_LIMIT = 63 * MIB
MEMBER, ROW, LENGTH, CORE, NEAR, FAR = range(6)


def whole_to_word(held, devices):
    tall, width = held.shape
    rows = tall // 2
    each = rows // devices
    line = lax.broadcasted_iota(jnp.int32, (rows, tall), 0)
    lane = lax.broadcasted_iota(jnp.int32, (rows, tall), 1)
    source = lax.div(line, each) * (2 * each) + lax.rem(line, each)
    halves = [dot((lane == source + k * each).astype(F32).astype(BF), held[...]).astype(BF) for k in range(2)]
    return jnp.concatenate(halves, 1)


def columns(array, width, start):
    return array, pl.BlockSpec((array.shape[0], width), lambda *_: (0, start // width))


def dot(a, b):
    return jnp.dot(a, b, preferred_element_type=F32)


def dot_t(a, b):
    return lax.dot_general(a, b, (((1,), (1,)), ((), ())), preferred_element_type=F32)


def t_dot(a, b):
    return dot(a.T, b)


def norm_parts(hidden):
    centred = hidden - jnp.mean(hidden, -1, keepdims=True)
    spread = lax.rsqrt(jnp.mean(centred * centred, -1, keepdims=True) + EPS)
    return centred * spread, spread


def norm_back(unit, spread, gained):
    return (
        gained
        - jnp.mean(gained, -1, keepdims=True)
        - unit * jnp.mean(gained * unit, -1, keepdims=True)
    ) * spread


def gelu_both(pre):
    square = pre * pre
    turn = jnp.tanh(pre * (GELU_A + (GELU_A * GELU_B) * square))
    half = 0.5 + 0.5 * turn
    slope = half + pre * half * (1.0 - turn) * (GELU_A + (3.0 * GELU_A * GELU_B) * square)
    return pre * half, slope


def fold_rows(values):
    rows, width = values.shape
    return jnp.sum(values.reshape(rows // 8, 8, width), 0)


def head_masks(width, heads):
    lanes = lax.broadcasted_iota(jnp.int32, (1, width), 1) // HEAD
    return [(lanes == h).astype(F32).astype(BF) for h in range(heads)]


def run_blocks(step, begin, end, inputs, outputs):
    def one(*refs):
        step(begin + pl.program_id(0), *refs)

    def spec(ref):
        return pl.BlockSpec((BLOCK, ref.shape[1]), lambda i: (begin + i, 0))

    pltpu.emit_pipeline(
        one,
        grid=(end - begin,),
        in_specs=[spec(ref) for ref in inputs],
        out_specs=[spec(ref) for ref in outputs],
    )(*inputs, *outputs)


def streamed(kernel, scalars, streams, fixed, stream_outs, fixed_outs, scratch, cost, aliases=None):
    hbm = pl.BlockSpec(memory_space=pltpu.HBM)
    fixed = [one if isinstance(one, tuple) else (one, full(one.shape)) for one in fixed]
    return pl.pallas_call(
        kernel,
        out_shape=tuple(jax.ShapeDtypeStruct(*out) for out in tuple(stream_outs) + tuple(fixed_outs)),
        grid_spec=pltpu.PrefetchScalarGridSpec(
            num_scalar_prefetch=len(scalars),
            grid=(1,),
            in_specs=[hbm] * len(streams) + [spec for _, spec in fixed],
            out_specs=(hbm,) * len(stream_outs) + tuple(full(shape) for shape, _ in fixed_outs),
            scratch_shapes=[pltpu.VMEM(*one) if isinstance(one, tuple) else one for one in scratch],
        ),
        input_output_aliases=aliases or {},
        compiler_params=pltpu.CompilerParams(vmem_limit_bytes=VMEM_LIMIT),
        cost_estimate=cost,
    )(*scalars, *streams, *(one for one, _ in fixed))


def full(shape):
    return pl.BlockSpec(shape, lambda *_: (0,) * len(shape))


def offsets_kernel(layout, counts, lengths, index, offs, first, rows_of, blocks, place_out):
    share, members = layout
    rows, per_row = counts.shape
    deep, part = lax.div(index[0], share), lax.rem(index[0], share)
    my_row = lax.div(part, members)
    place_out[MEMBER] = lax.rem(part, members)
    place_out[ROW] = my_row
    place_out[LENGTH] = lengths[my_row]
    place_out[CORE] = lax.rem(part, 2)
    place_out[NEAR] = lax.rem(deep, 2) * (share // 2) + lax.div(part, 2)
    place_out[FAR] = lax.div(deep, 2)

    def clear(g, carry):
        first[g] = 0
        rows_of[g] = 0
        return carry

    lax.fori_loop(0, first.shape[0], clear, 0, unroll=True)
    spare = first.shape[0] - 1

    def place(row, k, at):
        live = counts[row, k]
        w = row * per_row + k
        inside = at & (GROUP - 1)
        at = jnp.where(inside + live > GROUP, at - inside + GROUP, at)
        group = jnp.where((at & (GROUP - 1)) == 0, at >> GROUP_BITS, spare)
        first[group] = w
        rows_of[group] = row
        offs[w] = at
        return at + live

    at = 0
    for row in range(rows):
        at = lax.fori_loop(0, per_row, functools.partial(place, row), at, unroll=8)
        at = ((at + (GROUP - 1)) >> GROUP_BITS) << GROUP_BITS
    blocks[0] = lax.div(at + (BLOCK - 1), BLOCK)


def group_count(words, slots, per_row):
    groups = (words * slots) // (GROUP - slots + 1) + 1 + words // per_row
    return -(-groups // SPLIT) * SPLIT


def offsets(layout, counts, lengths, index, slots):
    rows, per_row = counts.shape
    words = rows * per_row
    groups = group_count(words, slots, per_row)
    smem = pl.BlockSpec(memory_space=pltpu.SMEM)
    sizes = (words, groups + 1, groups + 1, 1, 6)
    return pl.pallas_call(
        functools.partial(offsets_kernel, layout),
        out_shape=tuple(jax.ShapeDtypeStruct((size,), jnp.int32) for size in sizes),
        in_specs=[smem] * 3,
        out_specs=(smem,) * 5,
        cost_estimate=pl.CostEstimate(flops=words * 4000, bytes_accessed=12 * MIB, transcendentals=0),
    )(counts, lengths, index)


def pack_kernel(
    counts, offs, first, blocks, chars, packed_all, bias_all, hot_all, inverse, tags, *wide
):
    slots = chars.shape[1]
    rows, per_row = counts.shape
    slot = lax.broadcasted_iota(jnp.int32, (slots, GROUP), 0)

    def clear_rows(k, carry):
        there = pl.ds(pl.multiple_of(k * GROUP, GROUP), GROUP)
        for part in wide:
            part[there, :] = jnp.zeros((GROUP, GROUP), F32)
        tags[there, :] = jnp.full((GROUP, GROUP), -1.0, F32)
        return carry

    lax.fori_loop(0, blocks[0] * SPLIT, clear_rows, 0)

    def put(row, n, carry):
        w = row * per_row + n
        at = offs[w]
        for k, part in enumerate(wide):
            part[pl.ds(at, slots), :] = chars[w, :, k * GROUP : (k + 1) * GROUP].astype(F32)
        tags[pl.ds(at, slots), :] = jnp.where(slot < counts[row, n], w.astype(F32), -1.0)
        inverse[pl.ds(w, 1), :] = 1.0 / jnp.full((1, GROUP), counts[row, n], jnp.int32).astype(F32)
        return carry

    for row in range(rows):
        lax.fori_loop(0, per_row, functools.partial(put, row), 0, unroll=8)
    lane = lax.broadcasted_iota(jnp.int32, (GROUP, GROUP), 1).astype(F32)

    def step(i, packed, bias, hot):
        for g in range(SPLIT):
            here = slice(g * GROUP, (g + 1) * GROUP)
            there = pl.ds(pl.multiple_of((i * SPLIT + g) * GROUP, GROUP), GROUP)
            tag = tags[there, :]
            bias[here, :] = jnp.where(tag == tag.T, 0.0, MASKED).astype(BF)
            hot[here, :] = (tag - first[i * SPLIT + g].astype(F32) == lane).astype(F32).astype(BF)
            for k, part in enumerate(wide):
                packed[here, k * GROUP : (k + 1) * GROUP] = part[there, :].astype(BF)

    run_blocks(step, 0, blocks[0], (), (packed_all, bias_all, hot_all))


def pack(counts, offs, first, blocks, chars):
    words, slots, width = chars.shape
    rows = group_count(words, slots, counts.shape[1]) * GROUP
    return streamed(
        pack_kernel,
        (counts, offs, first, blocks),
        (),
        (chars,),
        (((rows, width), BF), ((rows, GROUP), BF), ((rows, GROUP), BF)),
        (((words, GROUP), F32),),
        (((rows + GROUP, GROUP), F32),) * (1 + width // GROUP),
        pl.CostEstimate(flops=rows * width * 4, bytes_accessed=rows * width * 10, transcendentals=0),
    )


def unpack_kernel(row, halves, offs, counts, *refs):
    packed = refs[:halves]
    out, held, arrived = refs[-2 - halves], refs[-1 - halves : -1], refs[-1]
    slots = out.shape[1]
    count = counts.shape[1]
    begin = row * count
    here = pl.program_id(0) * out.shape[0]
    slot = lax.broadcasted_iota(jnp.int32, (slots, GROUP), 0)

    @pl.when(pl.program_id(0) == 0)
    def _():
        low = lax.div(offs[begin], BLOCK)
        high = lax.div(offs[begin + count - 1] + (slots + BLOCK - 1), BLOCK)

        def copy(k, j):
            there = pl.ds(pl.multiple_of(k * BLOCK, BLOCK), BLOCK)
            return pltpu.make_async_copy(packed[j].at[there, :], held[j].at[there, :], arrived.at[j, k])

        def fetch(k, carry):
            for j in range(halves):
                copy(k, j).start()
            return carry

        def await_one(k, carry):
            for j in range(halves):
                copy(k, j).wait()
            return carry

        lax.fori_loop(low, high, fetch, 0)
        lax.fori_loop(low, high, await_one, 0)

    def take(k, carry):
        n = here + k
        for j, part in enumerate(held):
            rows = part[pl.ds(offs[begin + n], slots), :]
            out[k, :, j * GROUP : (j + 1) * GROUP] = jnp.where(slot < counts[row, n], rows, 0.0)
        return carry

    lax.fori_loop(0, out.shape[0], take, 0, unroll=8)


def unpack(offs, counts, packed, slots, before=None):
    words = counts.size
    halves = len(packed)
    width = halves * GROUP
    step = words // 8
    row = 0 if before is None else 1
    extra = [] if before is None else [before]
    hbm = pl.BlockSpec(memory_space=pltpu.HBM)
    return pl.pallas_call(
        functools.partial(unpack_kernel, row, halves),
        out_shape=jax.ShapeDtypeStruct((words, slots, width), F32),
        grid_spec=pltpu.PrefetchScalarGridSpec(
            num_scalar_prefetch=2,
            grid=(4,),
            in_specs=[hbm] * (halves + len(extra)),
            out_specs=pl.BlockSpec((step, slots, width), lambda i, *_: (4 * row + i, 0, 0)),
            scratch_shapes=[pltpu.VMEM(part.shape, F32) for part in packed]
            + [pltpu.SemaphoreType.DMA((halves, packed[0].shape[0] // BLOCK))],
        ),
        input_output_aliases={2 + halves: 0} if extra else {},
        compiler_params=pltpu.CompilerParams(vmem_limit_bytes=VMEM_LIMIT),
        cost_estimate=pl.CostEstimate(
            flops=words * slots * width, bytes_accessed=words * slots * width * 4, transcendentals=0
        ),
    )(offs, counts, *packed, *extra)


def with_language(i, rows_of, ids, packed, small_rows):
    parts = []
    for g in range(SPLIT):
        row = small_rows[pl.ds(ids[rows_of[i * SPLIT + g]], 1), :]
        parts.append(packed[g * GROUP : (g + 1) * GROUP, :].astype(F32) + row)
    return jnp.concatenate(parts, 0)


def both_heads(values, lower):
    wide = values.astype(F32)
    return jnp.concatenate([jnp.where(lower, wide, 0.0), jnp.where(lower, 0.0, wide)], 0).astype(BF)


def pick_heads(stacked, lower):
    rows = stacked.shape[0] // 2
    return jnp.where(lower, stacked[:rows], stacked[rows:])


def char_attend_kernel(
    langs,
    blocks,
    rows_of,
    ids,
    place,
    packed_all,
    bias_all,
    cotangent,
    weights,
    small,
    qkv_all,
    soft_all,
    mixed_all,
    after_all,
    cotangent_out,
    small_rows,
    sent,
):
    copy = pltpu.make_async_copy(cotangent.at[1 - place[ROW]], cotangent_out, sent)
    copy.start()
    width = packed_all.shape[1]
    small_rows[...] = small[...].astype(F32).T

    def step(i, packed, bias, qkv_out, soft_out, mixed_out, after_out):
        start = with_language(i, rows_of, ids, packed, small_rows)
        unit, _ = norm_parts(start)
        normed = (unit * small_rows[langs : langs + 1, :] + small_rows[langs + 1 : langs + 2, :]).astype(BF)
        qkv_out[...] = dot(normed, weights[:, : 3 * width]).astype(BF)
        lower = lax.broadcasted_iota(jnp.int32, (GROUP, GROUP), 1) < HEAD
        places = [(slice(g * GROUP, (g + 1) * GROUP), t) for g in range(SPLIT) for t in range(CHEADS // 2)]
        scores = []
        for here, t in places:
            tile = slice(t * GROUP, (t + 1) * GROUP)
            keys = both_heads(qkv_out[here, width + t * GROUP : width + (t + 1) * GROUP], lower)
            scores.append(dot_t(keys, qkv_out[here, tile]))
        softs = []
        for (here, t), score in zip(places, scores):
            blocked = bias[here, :].astype(F32)
            for h in range(2):
                one = score[h * GROUP : (h + 1) * GROUP] * SCALE + blocked
                one = jnp.exp(one - jnp.max(one, 0, keepdims=True))
                one = (one * (1.0 / jnp.sum(one, 0, keepdims=True))).astype(BF)
                soft_out[here, (2 * t + h) * GROUP : (2 * t + h + 1) * GROUP] = one
                softs.append(one)
        for k, (here, t) in enumerate(places):
            values = qkv_out[here, 2 * width + t * GROUP : 2 * width + (t + 1) * GROUP]
            mixed = dot(jnp.concatenate([softs[2 * k].T, softs[2 * k + 1].T], 0), values)
            mixed_out[here, t * GROUP : (t + 1) * GROUP] = pick_heads(mixed, lower).astype(BF)
        after_out[...] = start + dot(mixed_out[...], weights[:, 3 * width : 4 * width])

    run_blocks(step, 0, blocks[0], (packed_all, bias_all), (qkv_all, soft_all, mixed_all, after_all))
    copy.wait()


def char_attend(langs, blocks, rows_of, ids, place, packed, bias, weights, cotangent):
    rows, width = packed.shape
    at_small = weights.shape[1] - SMALL
    return streamed(
        functools.partial(char_attend_kernel, langs),
        (blocks, rows_of, ids, place),
        (packed, bias, cotangent),
        (columns(weights, 4 * width, 0), columns(weights, SMALL, at_small)),
        (
            ((rows, 3 * width), BF),
            ((rows, CHEADS * GROUP), BF),
            ((rows, width), BF),
            ((rows, width), F32),
            (cotangent.shape[1:], BF),
        ),
        (),
        (((SMALL, width), F32), pltpu.SemaphoreType.DMA),
        pl.CostEstimate(
            flops=rows * width * width * 12, bytes_accessed=rows * width * 12, transcendentals=rows * 512
        ),
    )


def char_ffn_kernel(
    langs,
    blocks,
    first,
    place,
    after_all,
    hot_all,
    inverse,
    expand,
    reduced,
    small,
    act_all,
    slope_all,
    kept_out,
    sent_out,
    small_rows,
    *total,
):
    width = after_all.shape[1]
    small_rows[...] = small[...].astype(F32).T
    for part in total:
        part[...] = jnp.zeros_like(part)

    def step(i, after, hot, act_out, slope_out):
        unit, _ = norm_parts(after[...])
        normed = (unit * small_rows[langs + 2 : langs + 3, :] + small_rows[langs + 3 : langs + 4, :]).astype(BF)
        out = after[...] + small_rows[langs + 4 : langs + 5, :]
        pres = [dot(normed, expand[:, j * width : (j + 1) * width]) for j in range(FOLD)]
        acts = []
        for j, pre in enumerate(pres):
            cols = slice(j * width, (j + 1) * width)
            act, slope = gelu_both(pre + small_rows[langs + 5 + j : langs + 6 + j, :])
            act = act.astype(BF)
            act_out[:, cols] = act
            slope_out[:, cols] = slope.astype(BF)
            acts.append(act)
        for j, act in enumerate(acts):
            out = out + dot(act, reduced[:, j * width : (j + 1) * width])
        out = out.astype(BF)
        for g in range(SPLIT):
            here = slice(g * GROUP, (g + 1) * GROUP)
            words = pl.ds(first[i * SPLIT + g], GROUP)
            found = t_dot(hot[here, :], out[here, :])
            for k, part in enumerate(total):
                part[words, :] = part[words, :] + found[:, k * GROUP : (k + 1) * GROUP]

    run_blocks(step, 0, blocks[0], (after_all, hot_all), (act_all, slope_all))
    local = kept_out.shape[0]
    for out_ref, row in ((kept_out, place[ROW]), (sent_out, 1 - place[ROW])):
        there = pl.ds(pl.multiple_of(row * local, local), local)
        for k, part in enumerate(total):
            out_ref[:, k * GROUP : (k + 1) * GROUP] = (part[there, :] * inverse[there, :]).astype(BF)


def feed_columns(weights, width):
    hidden = FOLD * width
    return (
        columns(weights, hidden, 4 * width),
        columns(weights, hidden, 4 * width + hidden),
        columns(weights, SMALL, weights.shape[1] - SMALL),
    )


def char_ffn(langs, blocks, first, place, after, hot, inverse, weights):
    rows, width = after.shape
    words = inverse.shape[0]
    hidden = FOLD * width
    return streamed(
        functools.partial(char_ffn_kernel, langs),
        (blocks, first, place),
        (after, hot),
        (inverse, *feed_columns(weights, width)),
        (((rows, hidden), BF), ((rows, hidden), BF)),
        (((words // 2, width), BF), ((words // 2, width), BF)),
        (((SMALL, width), F32),) + (((words + GROUP, GROUP), F32),) * (width // GROUP),
        pl.CostEstimate(
            flops=rows * width * width * 16, bytes_accessed=rows * width * 20, transcendentals=rows * 1024
        ),
    )


def sorted_rows(core, counts, rows, cuts=1):
    far, near = counts
    each = rows // (2 * far * near)
    some = each // cuts
    low = near // 2
    line = lax.broadcasted_iota(jnp.int32, (rows, rows), 0)
    piece = lax.div(line, rows // (2 * cuts))
    line = lax.rem(line, rows // (2 * cuts))
    which = lax.rem(piece, cuts)
    core = jnp.bitwise_xor(core, lax.div(piece, cuts))
    inner = lax.rem(line, some)
    part = lax.div(line, some)
    at_far, at_near = lax.rem(part, far), lax.div(part, far)
    device = ((at_far * 2 + lax.div(at_near, low)) * low + lax.rem(at_near, low)) * 2 + core
    source = device * each + which * some + inner
    return (source == lax.broadcasted_iota(jnp.int32, source.shape, 1)).astype(F32).astype(BF)


def folding(back):
    size = FOLD * HEAD
    unit = lax.broadcasted_iota(jnp.int32, (size, size), 1 if back else 0)
    held = lax.broadcasted_iota(jnp.int32, (size, size), 0 if back else 1)
    return (held == (unit & (FOLD - 1)) * HEAD + lax.div(unit, FOLD)).astype(F32).astype(BF)


def unfold_into(out, folded, width):
    size = FOLD * HEAD
    matrix = folding(True)
    for m in range(width // HEAD):
        near = [folded[:, j * width + m * HEAD : j * width + (m + 1) * HEAD] for j in range(FOLD)]
        out[:, m * size : (m + 1) * size] = dot(jnp.concatenate(near, 1), matrix).astype(BF)


def char_ffn_back_kernel(
    settings,
    blocks,
    first,
    place,
    after_all,
    hot_all,
    act_all,
    slope_all,
    inverse,
    up_kept,
    up_sent,
    expand,
    reduced,
    small,
    grad_to_word,
    riding_kept,
    riding_sent,
    grad_after_all,
    kept_out,
    sent_out,
    sums,
    small_rows,
    grad_expand,
    grad_reduce,
    up_rows,
    grads,
    *spread_up,
):
    langs, counts = settings
    width = after_all.shape[1]
    hidden = FOLD * width
    local = up_kept.shape[0]
    small_rows[...] = small[...].astype(F32).T
    for up_in, row in ((up_kept, place[ROW]), (up_sent, 1 - place[ROW])):
        there = pl.ds(pl.multiple_of(row * local, local), local)
        for k, part in enumerate(spread_up):
            cols = slice(k * GROUP, (k + 1) * GROUP)
            part[there, :] = up_in[:, cols].astype(F32) * inverse[there, :]
    for part in spread_up:
        part[2 * local :, :] = jnp.zeros((GROUP, GROUP), F32)
    grad_expand[...] = jnp.zeros_like(grad_expand)
    grad_reduce[...] = jnp.zeros_like(grad_reduce)
    sums[...] = jnp.zeros_like(sums)

    def step(i, after, hot, act, slope, grad_after):
        for g in range(SPLIT):
            here = slice(g * GROUP, (g + 1) * GROUP)
            for k, part in enumerate(spread_up):
                words_here = part[pl.ds(first[i * SPLIT + g], GROUP), :].astype(BF)
                up_rows[here, k * GROUP : (k + 1) * GROUP] = dot(hot[here, :], words_here).astype(BF)
        up = up_rows[...]
        unit, spread = norm_parts(after[...])
        gain = small_rows[langs + 2 : langs + 3, :]
        normed = (unit * gain + small_rows[langs + 3 : langs + 4, :]).astype(BF)
        grad_normed = jnp.zeros((BLOCK, width), F32)
        parts = [slice(j * width, (j + 1) * width) for j in range(FOLD)]
        grad_acts = [
            dot_t(up, reduced[:, j * width : (j + 1) * width]) for j in range(FOLD)
        ]
        grad_pres = []
        for j, cols in enumerate(parts):
            grad_pre = grad_acts[j] * slope[:, cols].astype(F32)
            sums[8 * j : 8 * j + 8, :] += fold_rows(grad_pre)
            grad_pres.append(grad_pre.astype(BF))
        for j, grad_pre in enumerate(grad_pres):
            grad_normed = grad_normed + dot_t(grad_pre, expand[:, j * width : (j + 1) * width])
        turned = normed.T
        for cols, grad_pre in zip(parts, grad_pres):
            grad_expand[:, cols] += dot(turned, grad_pre)
        turned = up.T
        for cols in parts:
            grad_reduce[:, cols] += dot(turned, act[:, cols])
        up_wide = up.astype(F32)
        sums[32:40, :] += fold_rows(grad_normed * unit)
        sums[40:48, :] += fold_rows(grad_normed)
        sums[48:56, :] += fold_rows(up_wide)
        grad_after[...] = up_wide + norm_back(unit, spread, grad_normed * gain)

    run_blocks(step, 0, blocks[0], (after_all, hot_all, act_all, slope_all), (grad_after_all,))
    unfold_into(grads.at[:, :hidden], grad_expand[...].astype(BF), width)
    for j in range(FOLD):
        grads[:, hidden + j * width : hidden + (j + 1) * width] = (
            grad_reduce[:, j * width : (j + 1) * width].T.astype(BF)
        )
    grads[:, 2 * hidden :] = grad_to_word[...]
    own = grads.shape[1]
    ranked = dot(sorted_rows(place[CORE], counts, width), grads[...]).astype(BF)
    kept_out[:, :own] = ranked[: width // 2]
    sent_out[:, :own] = ranked[width // 2 :]
    kept_out[:, own:] = riding_kept[...]
    sent_out[:, own:] = riding_sent[...]


def char_ffn_back(
    settings,
    blocks,
    first,
    place,
    after,
    hot,
    act,
    slope,
    inverse,
    up_kept,
    up_sent,
    weights,
    grad_to_word,
    riding,
):
    rows, width = after.shape
    words = inverse.shape[0]
    hidden = FOLD * width
    span = 2 * hidden + grad_to_word.shape[1]
    return streamed(
        functools.partial(char_ffn_back_kernel, settings),
        (blocks, first, place),
        (after, hot, act, slope),
        (inverse, up_kept, up_sent, *feed_columns(weights, width), grad_to_word, *riding),
        (((rows, width), F32),),
        (((width // 2, span + riding[0].shape[1]), BF),) * 2 + (((64, width), F32),),
        (
            ((SMALL, width), F32),
            ((width, hidden), F32),
            ((width, hidden), F32),
            ((BLOCK, width), BF),
            ((width, span), BF),
        )
        + (((words + GROUP, GROUP), F32),) * (width // GROUP),
        pl.CostEstimate(
            flops=rows * width * width * 32, bytes_accessed=rows * width * 20, transcendentals=0
        ),
    )


def char_attend_back_kernel(settings, blocks, rows_of, ids, place, *refs):
    langs, counts = settings
    streams, refs = refs[:5], refs[5:]
    width = streams[0].shape[1]
    halves = width // GROUP
    (weights, small, sums_in), refs = refs[:3], refs[3:]
    start_all, refs = refs[:halves], refs[halves:]
    kept_out, sent_out, small_rows, grad_mixed, grad_qkv, grad_in, lines, grads = refs
    grad_in[...] = jnp.zeros_like(grad_in)
    lines[...] = jnp.zeros_like(lines)
    small_rows[...] = small[...].astype(F32).T

    def step(i, packed, qkv, soft, mixed, grad_after, *grad_start):
        start = with_language(i, rows_of, ids, packed, small_rows)
        unit, spread = norm_parts(start)
        gain = small_rows[langs : langs + 1, :]
        normed = (unit * gain + small_rows[langs + 1 : langs + 2, :]).astype(BF)
        after_low = grad_after[...].astype(BF)
        grad_in[:, 3 * width :] += t_dot(mixed[...], after_low)
        grad_mixed[...] = dot_t(after_low, weights[:, 3 * width : 4 * width]).astype(BF)
        lower = lax.broadcasted_iota(jnp.int32, (GROUP, GROUP), 1) < HEAD
        places = [(slice(g * GROUP, (g + 1) * GROUP), t) for g in range(SPLIT) for t in range(CHEADS // 2)]

        def tile_of(values, which, k):
            here, t = places[k]
            return values[here, which * width + t * GROUP : which * width + (t + 1) * GROUP]

        every = range(len(places))
        lows = [both_heads(tile_of(grad_mixed, 0, k), lower) for k in every]
        grad_softs = [dot_t(tile_of(qkv, 2, k), lows[k]) for k in every]
        weights_of = [soft[here, 2 * t * GROUP : (2 * t + 2) * GROUP] for here, t in places]
        ones = []
        for weight, grad_soft in zip(weights_of, grad_softs):
            wide = weight.astype(F32)
            ones.append((wide * (grad_soft - jnp.sum(wide * grad_soft, 0, keepdims=True))).astype(BF))
        for k, (here, t) in enumerate(places):
            value = dot(weights_of[k], lows[k])
            grad_qkv[here, 2 * width + t * GROUP : 2 * width + (t + 1) * GROUP] = value.astype(BF)
        for k, (here, t) in enumerate(places):
            value = dot(ones[k], both_heads(tile_of(qkv, 0, k), lower))
            grad_qkv[here, width + t * GROUP : width + (t + 1) * GROUP] = (value * SCALE).astype(BF)
        for k, (here, t) in enumerate(places):
            turned = jnp.concatenate([ones[k][:, :GROUP].T, ones[k][:, GROUP:].T], 1)
            value = dot(turned, both_heads(tile_of(qkv, 1, k), lower))
            grad_qkv[here, t * GROUP : (t + 1) * GROUP] = (value * SCALE).astype(BF)
        grad_in[:, : 3 * width] += t_dot(normed, grad_qkv[...])
        grad_normed = dot_t(grad_qkv[...], weights[:, : 3 * width])
        lines[SMALL : SMALL + 8, :] += fold_rows(grad_normed * unit)
        lines[SMALL + 8 :, :] += fold_rows(grad_normed)
        result = grad_after[...] + norm_back(unit, spread, grad_normed * gain)
        for k, part in enumerate(grad_start):
            part[...] = result[:, k * GROUP : (k + 1) * GROUP]
        for g in range(SPLIT):
            line = pl.ds(ids[rows_of[i * SPLIT + g]], 1)
            part = jnp.sum(result[g * GROUP : (g + 1) * GROUP, :], 0, keepdims=True)
            lines[line, :] = lines[line, :] + part

    run_blocks(step, 0, blocks[0], streams, start_all)

    def put(at, block):
        lines[langs + at : langs + at + 1, :] = jnp.sum(block, 0, keepdims=True)

    put(0, lines[SMALL : SMALL + 8, :])
    put(1, lines[SMALL + 8 :, :])
    put(2, sums_in[32:40, :])
    put(3, sums_in[40:48, :])
    put(4, sums_in[48:56, :])
    for j in range(FOLD):
        put(5 + j, sums_in[8 * j : 8 * j + 8, :])
    grads[:, : 4 * width] = grad_in[...].astype(BF)
    grads[:, 4 * width :] = lines[:SMALL, :].T.astype(BF)
    ranked = dot(sorted_rows(place[CORE], counts, width), grads[...]).astype(BF)
    kept_out[...] = ranked[: width // 2]
    sent_out[...] = ranked[width // 2 :]


def char_attend_back(
    settings, blocks, rows_of, ids, place, packed, qkv, soft, mixed, grad_after, weights, sums
):
    rows, width = packed.shape
    span = 4 * width + SMALL
    return streamed(
        functools.partial(char_attend_back_kernel, settings),
        (blocks, rows_of, ids, place),
        (packed, qkv, soft, mixed, grad_after),
        (columns(weights, 4 * width, 0), columns(weights, SMALL, weights.shape[1] - SMALL), sums),
        (((rows + BLOCK, GROUP), F32),) * (width // GROUP),
        (((width // 2, span), BF),) * 2,
        (
            ((SMALL, width), F32),
            ((BLOCK, width), BF),
            ((BLOCK, 3 * width), BF),
            ((width, 4 * width), F32),
            ((SMALL + 16, width), F32),
            ((width, span), BF),
        ),
        pl.CostEstimate(
            flops=rows * width * width * 24, bytes_accessed=rows * width * 20, transcendentals=0
        ),
    )


def word_kernel(
    counts,
    members,
    place,
    weights_all,
    cotangent,
    cotangent_other,
    *refs,
):
    pieces, refs = refs[: 2 * members], refs[2 * members :]
    away, refs = refs[:7], refs[7:]
    grad_query_out, sums_out = refs[:2]
    pair_outs, refs = refs[2 : 2 + members], refs[2 + members :]
    words_both, words_sent, grad_after_out, normed_out, word_in_out, kept_out, sent_out = refs[:7]
    sent_sem, weights, to_word, held_sem = refs[7:11]
    refs = refs[11:]
    (
        small_rows,
        pooled,
        word_all,
        normed_all,
        pair,
        query,
        blocked,
        soft_near,
        soft_far,
        mixed,
        after,
        unit_two,
        normed_two,
        up_low,
        total,
        grad_normed,
        grads,
        natural,
        grad_pair,
    ) = refs
    member = place[MEMBER]
    my_row = place[ROW]
    length = place[LENGTH]
    all_words, narrow = pooled.shape
    width = up_low.shape[1]
    own_words = up_low.shape[0]
    local = own_words // 2
    half = all_words // 2
    hidden = FOLD * width
    reach = (half, all_words)
    at_out, at_expand, at_reduce = 3 * width, 4 * width, 4 * width + hidden
    at_to_word = at_reduce + hidden
    at_small = at_to_word + width // 2

    def fetch(k, start, stop):
        return pltpu.make_async_copy(
            weights_all.at[:, start:stop], weights.at[:, start:stop], held_sem.at[k]
        )

    early = (
        fetch(0, at_to_word, at_small + SMALL),
        fetch(1, 0, at_out),
    )
    late = (fetch(2, at_out, at_expand), fetch(3, at_expand, at_to_word))
    for copy in early + late:
        copy.start()
    leaving = [
        pltpu.make_async_copy(here, there, sent_sem.at[k])
        for k, (here, there) in enumerate(
            zip((words_both, words_sent, grad_after_out, normed_out, word_in_out, kept_out, sent_out), away)
        )
    ]
    for copy in early:
        copy.wait()
    small_rows[...] = weights[:, at_small:].astype(F32).T
    to_word[...] = whole_to_word(weights.at[:, at_to_word:at_small], 2 * counts[0] * counts[1])

    def rows_at(index):
        return pl.ds(pl.multiple_of(index * local, local), local)

    for m in range(members):
        there = jnp.bitwise_xor(member, m)
        pooled[rows_at(my_row * members + there), :] = pieces[2 * m][...]
        pooled[rows_at((1 - my_row) * members + there), :] = pieces[2 * m + 1][...]

    def embed(t, carry):
        here = pl.ds(pl.multiple_of(t * local, local), local)
        value = dot(pooled[here, :], to_word[...]) + small_rows[5:6, :]
        word_all[here, :] = value
        unit, _ = norm_parts(value)
        normed = (unit * small_rows[0:1, :] + small_rows[1:2, :]).astype(BF)
        normed_all[here, :] = normed
        pair[here, :] = dot(normed, weights[:, width : 3 * width]).astype(BF)
        return carry

    lax.fori_loop(0, all_words // local, embed, 0, unroll=4)
    origin = []
    for t in range(2):
        base = member * local + t * half
        origin.append(base)
        here = slice(t * local, (t + 1) * local)
        word_in_out[here, :] = word_all[rows_at(member + t * members), :]
        normed_out[here, :] = normed_all[rows_at(member + t * members), :]
    leaving[3].start()
    leaving[4].start()
    query[...] = dot(normed_out[...], weights[:, :width]).astype(BF)
    masks = head_masks(GROUP, 2)
    lower = lax.broadcasted_iota(jnp.int32, (local, GROUP), 1) < HEAD
    softs = (soft_near, soft_far)

    for t in range(2):
        seen = lax.broadcasted_iota(jnp.int32, (local, reach[t]), 1)
        asks = lax.broadcasted_iota(jnp.int32, (local, reach[t]), 0) + origin[t]
        blocked[t * local : (t + 1) * local, : reach[t]] = jnp.where((seen <= asks) & (seen < length), 0.0, MASKED)
    chains = [(slice(t * local, (t + 1) * local), t, h) for t in range(2) for h in range(2)]

    def attend(p, carry):
        lanes = pl.ds(pl.multiple_of(p * GROUP, GROUP), GROUP)
        after_lanes = pl.ds(pl.multiple_of(width + p * GROUP, GROUP), GROUP)
        scores = [dot_t(query[here, lanes] * masks[h], pair[: reach[t], lanes]) for here, t, h in chains]
        weights_of = []
        for (here, t, h), score in zip(chains, scores):
            score = score * SCALE + blocked[here, : reach[t]]
            score = jnp.exp(score - jnp.max(score, -1, keepdims=True))
            soft = (score * (1.0 / jnp.sum(score, -1, keepdims=True))).astype(BF)
            softs[t][2 * p + h] = soft
            weights_of.append(soft)
        outs = [dot(soft, pair[: reach[t], after_lanes]) for (_, t, h), soft in zip(chains, weights_of)]
        for t in range(2):
            mixed[t * local : (t + 1) * local, lanes] = jnp.where(lower, outs[2 * t], outs[2 * t + 1]).astype(BF)
        return carry

    lax.fori_loop(0, WHEADS // 2, attend, 0, unroll=4)
    for copy in late:
        copy.wait()
    value = word_in_out[...] + dot(mixed[...], weights[:, at_out : at_out + width])
    after[...] = value
    unit, spread = norm_parts(value)
    unit_two[...] = unit
    normed_two[...] = (unit * small_rows[2:3, :] + small_rows[3:4, :]).astype(BF)
    row = lax.broadcasted_iota(jnp.int32, (own_words, 1), 0)
    index = jnp.where(row < local, origin[0] + row, origin[1] + row - local)
    valid = index < length
    up_low[rows_at(my_row), :] = cotangent[my_row]
    up_low[rows_at(1 - my_row), :] = cotangent_other[...]
    up_low[...] = jnp.where(valid, up_low[...].astype(F32), 0.0).astype(BF)
    total[...] = jnp.zeros_like(total)
    grad_normed[...] = jnp.zeros_like(grad_normed)

    def feed(j, carry):
        expand = weights[:, pl.ds(pl.multiple_of(at_expand + j * width, GROUP), width)]
        shrink = weights[:, pl.ds(pl.multiple_of(at_reduce + j * width, GROUP), width)]
        pre = dot(normed_two[...], expand) + small_rows[pl.ds(6 + j, 1), :]
        act, slope = gelu_both(pre)
        act = act.astype(BF)
        total[...] += dot(act, shrink)
        grad_pre = dot_t(up_low[...], shrink) * slope
        sums_out[pl.ds(6 + j, 1), :] = jnp.sum(grad_pre, 0, keepdims=True)
        grad_pre = grad_pre.astype(BF)
        grad_normed[...] += dot_t(grad_pre, expand)
        cols = pl.multiple_of(j * width, GROUP)
        grads[:, pl.ds(cols, width)] = t_dot(normed_two[...], grad_pre).astype(BF)
        grads[:, pl.ds(pl.multiple_of(hidden + j * width, GROUP), width)] = t_dot(
            act, up_low[...]
        ).astype(BF)
        return carry

    lax.fori_loop(0, FOLD, feed, 0, unroll=4)
    total[...] = jnp.where(valid, after[...] + (total[...] + small_rows[4:5, :]), 0.0)
    for t in range(2):
        words_both[t] = total[t * local : (t + 1) * local, :]
    words_sent[...] = total[rows_at(1 - my_row), :]
    leaving[0].start()
    leaving[1].start()
    upstream = up_low[...].astype(F32)
    incoming = grad_normed[...]
    sums_out[2:3, :] = jnp.sum(incoming * unit_two[...], 0, keepdims=True)
    sums_out[3:4, :] = jnp.sum(incoming, 0, keepdims=True)
    sums_out[4:5, :] = jnp.sum(upstream, 0, keepdims=True)
    grad_after = upstream + norm_back(unit_two[...], spread, incoming * small_rows[2:3, :])
    grad_after_out[...] = grad_after
    leaving[2].start()
    grad_low = grad_after.astype(BF)
    grads[:, 2 * hidden :] = t_dot(mixed[...], grad_low).astype(BF)
    mixed[...] = dot_t(grad_low, weights[:, at_out : at_out + width]).astype(BF)
    unfold_into(natural, grads[:, :hidden], width)
    chosen = sorted_rows(place[CORE], counts, width)
    for from_ref, start, stop in ((natural, 0, hidden), (grads, hidden, grads.shape[1])):
        ranked = dot(chosen, from_ref[:, start:stop]).astype(BF)
        kept_out[:, start:stop] = ranked[: width // 2]
        sent_out[:, start:stop] = ranked[width // 2 :]
    leaving[5].start()
    leaving[6].start()

    def attend_back(p, carry):
        lanes = pl.ds(pl.multiple_of(p * GROUP, GROUP), GROUP)
        after_lanes = pl.ds(pl.multiple_of(width + p * GROUP, GROUP), GROUP)
        lows = [mixed[here, lanes] * masks[h] for here, t, h in chains]
        ones = [dot_t(low, pair[: reach[t], after_lanes]) for low, (_, t, h) in zip(lows, chains)]
        weights_of = [softs[t][2 * p + h] for _, t, h in chains]
        grads_of = []
        for one, soft in zip(ones, weights_of):
            wide = soft.astype(F32)
            grads_of.append((wide * (one - jnp.sum(wide * one, -1, keepdims=True))).astype(BF))
        grad_values = [dot(soft.T, low) for soft, low in zip(weights_of, lows)]
        grad_keys = [
            dot(one.T, query[here, lanes] * masks[h]) for one, (here, t, h) in zip(grads_of, chains)
        ]
        grad_queries = [dot(one, pair[: reach[t], lanes]) for one, (_, t, h) in zip(grads_of, chains)]
        grad_values = [grad_values[2 * t] + grad_values[2 * t + 1] for t in range(2)]
        grad_keys = [grad_keys[2 * t] + grad_keys[2 * t + 1] for t in range(2)]
        for t in range(2):
            grad_query = jnp.where(lower, grad_queries[2 * t], grad_queries[2 * t + 1])
            grad_query_out[t * local : (t + 1) * local, lanes] = (grad_query * SCALE).astype(BF)
        for parts, at, factor in ((grad_keys, lanes, SCALE), (grad_values, after_lanes, 1.0)):
            grad_pair[:half, at] = ((parts[0] + parts[1][:half]) * factor).astype(BF)
            grad_pair[half:, at] = (parts[1][half:] * factor).astype(BF)
        return carry

    lax.fori_loop(0, WHEADS // 2, attend_back, 0)
    for m in range(members):
        there = jnp.bitwise_xor(member, m)
        for t in range(2):
            pair_outs[m][t * local : (t + 1) * local, :] = grad_pair[rows_at(t * members + there), :]
    for copy in leaving:
        copy.wait()


def word_part(counts, place, pieces, weights, cotangent, cotangent_other):
    members = len(pieces) // 2
    local, narrow = pieces[0].shape
    all_words = local * len(pieces)
    width = cotangent.shape[2]
    own = 2 * local
    hidden = FOLD * width
    vmem = pl.BlockSpec(memory_space=pltpu.VMEM)
    hbm = pl.BlockSpec(memory_space=pltpu.HBM)
    share = ((width // 2, 2 * hidden + width), BF)
    away = (
        ((2, local, width), F32),
        ((local, width), F32),
        ((own, width), F32),
        ((own, width), BF),
        ((own, width), F32),
        share,
        share,
    )
    stay = (((own, width), BF), ((16, width), F32)) + (((own, 2 * width), BF),) * members
    return pl.pallas_call(
        functools.partial(word_kernel, counts, members),
        out_shape=tuple(jax.ShapeDtypeStruct(*out) for out in away + stay),
        in_specs=[pl.BlockSpec(memory_space=pltpu.SMEM), hbm] + [vmem] * (2 + len(pieces)),
        out_specs=(hbm,) * len(away) + (vmem,) * len(stay),
        scratch_shapes=[pltpu.VMEM(*out) for out in away]
        + [
            pltpu.SemaphoreType.DMA((len(away),)),
            pltpu.VMEM(weights.shape, BF),
            pltpu.VMEM((narrow, width), BF),
            pltpu.SemaphoreType.DMA((4,)),
            pltpu.VMEM((SMALL, width), F32),
            pltpu.VMEM((all_words, narrow), BF),
            pltpu.VMEM((all_words, width), F32),
            pltpu.VMEM((all_words, width), BF),
            pltpu.VMEM((all_words, 2 * width), BF),
            pltpu.VMEM((own, width), BF),
            pltpu.VMEM((own, all_words), F32),
            pltpu.VMEM((WHEADS, local, all_words // 2), BF),
            pltpu.VMEM((WHEADS, local, all_words), BF),
            pltpu.VMEM((own, width), BF),
            pltpu.VMEM((own, width), F32),
            pltpu.VMEM((own, width), F32),
            pltpu.VMEM((own, width), BF),
            pltpu.VMEM((own, width), BF),
            pltpu.VMEM((own, width), F32),
            pltpu.VMEM((own, width), F32),
            pltpu.VMEM((width, 2 * hidden + width), BF),
            pltpu.VMEM((width, hidden), BF),
            pltpu.VMEM((all_words, 2 * width), BF),
        ],
        compiler_params=pltpu.CompilerParams(vmem_limit_bytes=VMEM_LIMIT),
        cost_estimate=pl.CostEstimate(
            flops=own * width * width * 60, bytes_accessed=20 * MIB, transcendentals=own * 8192
        ),
    )(place, weights, cotangent, cotangent_other, *pieces)


def word_end_kernel(
    counts,
    place,
    pooled_kept,
    pooled_other,
    to_word_ref,
    weights,
    small,
    grad_query,
    normed,
    word_in,
    grad_after,
    sums,
    *refs,
):
    pairs, refs = refs[:-8], refs[-8:]
    up_kept, up_sent, grad_to_word, kept_out, sent_out, small_rows, small_grads, incoming = refs
    width = grad_query.shape[1]
    local, narrow = pooled_kept.shape
    to_word = whole_to_word(to_word_ref, 2 * counts[0] * counts[1])
    small_rows[...] = small[...].astype(F32).T
    incoming[:, :width] = grad_query[...]
    pair = pairs[0][...].astype(F32)
    for other in pairs[1:]:
        pair = pair + other[...].astype(F32)
    incoming[:, width:] = pair.astype(BF)
    grad_normed = dot_t(incoming[...], weights[...])
    unit, spread = norm_parts(word_in[...])
    small_grads[...] = jnp.zeros_like(small_grads)
    small_grads[0:1, :] = jnp.sum(grad_normed * unit, 0, keepdims=True)
    small_grads[1:2, :] = jnp.sum(grad_normed, 0, keepdims=True)
    small_grads[2:5, :] = sums[2:5, :]
    small_grads[6:10, :] = sums[6:10, :]
    value = grad_after[...] + norm_back(unit, spread, grad_normed * small_rows[0:1, :])
    small_grads[5:6, :] = jnp.sum(value, 0, keepdims=True)
    low = value.astype(BF)
    back = dot_t(low, to_word).astype(BF)
    first_half = place[ROW] == 0
    up_kept[...] = jnp.where(first_half, back[:local].astype(F32), back[local:].astype(F32)).astype(BF)
    up_sent[...] = jnp.where(first_half, back[local:].astype(F32), back[:local].astype(F32)).astype(BF)
    low_kept = jnp.where(first_half, value[:local], value[local:]).astype(BF)
    low_other = jnp.where(first_half, value[local:], value[:local]).astype(BF)
    grad_to_word[...] = (t_dot(pooled_kept[...], low_kept) + t_dot(pooled_other[...], low_other)).astype(BF)
    inward = t_dot(normed[...], incoming[...]).astype(BF)
    small_turned = small_grads[...].T.astype(BF)
    span = 3 * width + SMALL
    cuts = width // narrow
    chosen = sorted_rows(place[CORE], counts, width, cuts)
    ranked = dot(chosen, inward).astype(BF)
    ranked_small = dot(chosen, small_turned).astype(BF)
    some = narrow // 2
    for k in range(2 * cuts):
        out_ref = (kept_out, sent_out)[k // cuts]
        at = k % cuts * span
        out_ref[:, at : at + 3 * width] = ranked[k * some : (k + 1) * some]
        out_ref[:, at + 3 * width : at + span] = ranked_small[k * some : (k + 1) * some]


def word_end(
    counts,
    place,
    pooled_kept,
    pooled_other,
    weights,
    grad_query,
    normed,
    word_in,
    grad_after,
    sums,
    pairs,
):
    local, narrow = pooled_kept.shape
    own, width = grad_query.shape
    last = weights.shape[1] // SMALL - 1
    share = (narrow // 2, (3 * width + SMALL) * (width // narrow))
    outs = ((local, narrow), (local, narrow), (narrow, width), share, share)
    operands = (grad_query, normed, word_in, grad_after, sums) + tuple(pairs)
    return pl.pallas_call(
        functools.partial(word_end_kernel, counts),
        out_shape=tuple(jax.ShapeDtypeStruct(shape, BF) for shape in outs),
        grid_spec=pltpu.PrefetchScalarGridSpec(
            num_scalar_prefetch=1,
            grid=(1,),
            in_specs=[
                full(pooled_kept.shape),
                full(pooled_other.shape),
                columns(weights, width // 2, 12 * width)[1],
                pl.BlockSpec((width, 3 * width), lambda i, *_: (0, 0)),
                pl.BlockSpec((width, SMALL), lambda i, *_: (0, last)),
            ]
            + [full(operand.shape) for operand in operands],
            out_specs=tuple(full(shape) for shape in outs),
            scratch_shapes=[
                pltpu.VMEM((SMALL, width), F32),
                pltpu.VMEM((SMALL, width), F32),
                pltpu.VMEM((own, 3 * width), BF),
            ],
        ),
        compiler_params=pltpu.CompilerParams(vmem_limit_bytes=VMEM_LIMIT),
        cost_estimate=pl.CostEstimate(
            flops=own * width * width * 14, bytes_accessed=10 * MIB, transcendentals=0
        ),
    )(place, pooled_kept, pooled_other, weights, weights, weights, *operands)


def column(vector, rows):
    each = vector.shape[0] // rows
    wide = vector[...].astype(F32).reshape(1, rows * each)
    line = lax.broadcasted_iota(jnp.int32, (rows, rows * each), 0)
    lane = lax.broadcasted_iota(jnp.int32, (rows, rows * each), 1)
    return [
        jnp.sum(jnp.where(line * each + j == lane, wide, 0.0), 1, keepdims=True) for j in range(each)
    ]


def columns_beside(rows, vectors, at):
    lane = lax.broadcasted_iota(jnp.int32, (rows, SMALL), 1)
    block = jnp.zeros((rows, SMALL), F32)
    for vector in vectors:
        for one in column(vector, rows):
            block = block + jnp.where(lane == at, one, 0.0)
            at += 1
    return block


def fold_into(out, at, weights, width):
    size = FOLD * HEAD
    matrix = folding(False)
    for m in range(width // HEAD):
        block = dot(weights[:, m * size : (m + 1) * size], matrix).astype(BF)
        for j in range(FOLD):
            there = at + j * width + m * HEAD
            out[:, there : there + HEAD] = block[:, j * HEAD : (j + 1) * HEAD]


def fold_shard(weights):
    tall = weights.shape[0]
    rows = tall // FOLD
    line = lax.broadcasted_iota(jnp.int32, (rows, tall), 0)
    lane = lax.broadcasted_iota(jnp.int32, (rows, tall), 1)
    return [
        dot((lane == FOLD * line + j).astype(F32).astype(BF), weights[...]).astype(BF) for j in range(FOLD)
    ]


def char_shard_kernel(table, inward, outward, expand, reduced, *refs):
    vectors, out = refs[:-1], refs[-1]
    rows, langs = table.shape
    width = outward.shape[1]
    at_expand, at_reduce, at_small = 4 * width, (4 + FOLD) * width, (4 + 2 * FOLD) * width
    out[:, : 3 * width] = inward[...]
    out[:, 3 * width : 4 * width] = outward[...]
    line = lax.broadcasted_iota(jnp.int32, (langs, SMALL), 0)
    lane = lax.broadcasted_iota(jnp.int32, (langs, SMALL), 1)
    spread = (line == lane).astype(F32).astype(BF)
    small = dot(table[...], spread) + columns_beside(rows, vectors, langs)
    out[:, at_small:] = small.astype(BF)
    fold_into(out, at_expand, expand, width)
    for j, part in enumerate(fold_shard(reduced)):
        out[:, at_reduce + j * width : at_reduce + (j + 1) * width] = part


def char_shard(table, inward, outward, expand, reduced, vectors):
    rows, width = outward.shape
    vmem = pl.BlockSpec(memory_space=pltpu.VMEM)
    return pl.pallas_call(
        char_shard_kernel,
        out_shape=jax.ShapeDtypeStruct((rows, (4 + 2 * FOLD) * width + SMALL), BF),
        in_specs=[vmem] * (5 + len(vectors)),
        out_specs=vmem,
    )(table, inward, outward, expand, reduced, *vectors)


def word_shard_kernel(inward, outward, expand, reduced, to_word, *refs):
    vectors, out = refs[:-1], refs[-1]
    rows, width = outward.shape
    out[:, : 3 * width] = inward[...]
    out[:, 3 * width : 4 * width] = outward[...]
    fold_into(out, 4 * width, expand, width)
    for j, part in enumerate(fold_shard(reduced)):
        out[:, (8 + j) * width : (9 + j) * width] = part
    narrow, half = to_word.shape[0], width // 2
    for k in range(2):
        out[k * narrow : (k + 1) * narrow, 12 * width : 12 * width + half] = to_word[:, k * half : (k + 1) * half]
    out[:, 12 * width + half :] = columns_beside(rows, vectors, 0).astype(BF)


def word_shard(inward, outward, expand, reduced, to_word, vectors):
    rows, width = outward.shape
    vmem = pl.BlockSpec(memory_space=pltpu.VMEM)
    return pl.pallas_call(
        word_shard_kernel,
        out_shape=jax.ShapeDtypeStruct((rows, 12 * width + width // 2 + SMALL), BF),
        in_specs=[vmem] * (5 + len(vectors)),
        out_specs=vmem,
    )(inward, outward, expand, reduced, to_word, *vectors)


def assemble_kernel(masks, index, *refs):
    pieces, out = refs[:-1], refs[-1]
    me = index[0]
    size = pieces[0].shape[0]
    for k, piece in enumerate(pieces):
        for t in range(size):
            out[jnp.bitwise_xor(me, masks[k * size + t])] = piece[t]


def assemble(masks, index, pieces):
    size, rows, columns = pieces[0].shape
    vmem = pl.BlockSpec(memory_space=pltpu.VMEM)
    out = pl.pallas_call(
        functools.partial(assemble_kernel, tuple(masks)),
        out_shape=jax.ShapeDtypeStruct((size * len(pieces), rows, columns), BF),
        in_specs=[pl.BlockSpec(memory_space=pltpu.SMEM)] + [vmem] * len(pieces),
        out_specs=vmem,
        compiler_params=pltpu.CompilerParams(vmem_limit_bytes=VMEM_LIMIT),
        cost_estimate=pl.CostEstimate(
            flops=0, bytes_accessed=4 * size * len(pieces) * rows * columns, transcendentals=0
        ),
    )(index, *pieces)
    return out.reshape(-1, columns)


def add_and_cut_kernel(which, arrivals, place, *refs):
    arrived, outs = refs[:arrivals], refs[arrivals:]
    total = arrived[0][...].astype(F32)
    for one in arrived[1:]:
        total = total + one[...].astype(F32)
    total = total.astype(BF)
    rows = total.shape[0]
    each = rows // len(outs)
    line = lax.broadcasted_iota(jnp.int32, (rows, rows), 0)
    lane = lax.broadcasted_iota(jnp.int32, (rows, rows), 1)
    part = jnp.bitwise_xor(lax.div(line, each), place[which])
    chosen = (lane == part * each + lax.rem(line, each)).astype(F32).astype(BF)
    sorted_total = dot(chosen, total).astype(BF)
    for m, out in enumerate(outs):
        out[...] = sorted_total[m * each : (m + 1) * each]


def add_and_cut(arrived, parts, which, place):
    rows, columns = arrived[0].shape

    vmem = pl.BlockSpec(memory_space=pltpu.VMEM)
    return pl.pallas_call(
        functools.partial(add_and_cut_kernel, which, len(arrived)),
        out_shape=(jax.ShapeDtypeStruct((rows // parts, columns), BF),) * parts,
        in_specs=[pl.BlockSpec(memory_space=pltpu.SMEM)] + [vmem] * len(arrived),
        out_specs=(vmem,) * parts,
        compiler_params=pltpu.CompilerParams(vmem_limit_bytes=VMEM_LIMIT),
        cost_estimate=pl.CostEstimate(
            flops=0, bytes_accessed=sum(4 * one.size for one in arrived), transcendentals=0
        ),
    )(place, *arrived)


def unfold_rows(folded, rows, out):
    width = out.shape[1]
    line = lax.broadcasted_iota(jnp.int32, (FOLD * rows, rows), 0)
    lane = lax.broadcasted_iota(jnp.int32, (FOLD * rows, rows), 1)
    total = jnp.zeros(out.shape, F32)
    for j in range(FOLD):
        chosen = (line == FOLD * lane + j).astype(F32)
        total = total + lax.dot_general(
            chosen,
            folded[:, j * width : (j + 1) * width],
            (((1,), (0,)), ((), ())),
            precision=lax.Precision.HIGHEST,
            preferred_element_type=F32,
        )
    out[...] = total


def finish_kernel(plan, count, *refs):
    arrived, outs = refs[:count], refs[count:]
    total = arrived[0][...].astype(F32)
    for one in arrived[1:]:
        total = total + one[...].astype(F32)
    rows = total.shape[0]
    for (kind, start, stop), out in zip(plan, outs):
        if kind == "folded":
            unfold_rows(total[:, start:stop], rows, out)
        elif kind == "plain":
            out[...] = total[:, start:stop]
        elif kind == "halves":
            height, width = out.shape
            pieces = height // rows
            stride = (stop - start) // pieces
            for k in range(pieces):
                out[k * rows : (k + 1) * rows, :] = total[:, start + k * stride : start + k * stride + width]
        else:
            pieces = stop[0]
            height = rows * pieces
            each = out.shape[0] // height
            value = jnp.zeros((1, out.shape[0]), F32)
            for k in range(pieces):
                block = total[:, start + k * stop[1] : start + k * stop[1] + SMALL]
                line = lax.broadcasted_iota(jnp.int32, (rows, out.shape[0]), 0) + k * rows
                lane = lax.broadcasted_iota(jnp.int32, (rows, out.shape[0]), 1)
                for j in range(each):
                    at = stop[2] + j
                    found = jnp.where(lane == line * each + j, block[:, at : at + 1], 0.0)
                    value = value + jnp.sum(found, 0, keepdims=True)
            out[...] = value.reshape(out.shape[0])


def finish(arrived, plan):
    vmem = pl.BlockSpec(memory_space=pltpu.VMEM)
    return pl.pallas_call(
        functools.partial(finish_kernel, tuple(one[:3] for one in plan), len(arrived)),
        out_shape=tuple(jax.ShapeDtypeStruct(shape, F32) for _, _, _, shape in plan),
        in_specs=[vmem] * len(arrived),
        out_specs=(vmem,) * len(plan),
        compiler_params=pltpu.CompilerParams(vmem_limit_bytes=VMEM_LIMIT),
    )(*arrived)


def tie(values, after):
    return lax.optimization_barrier((values, after))[0]


def body(
    char_inputs,
    language_ids,
    char_counts,
    row_lengths,
    cotangent,
    language_table,
    char_gain_one,
    char_bias_one,
    char_inward,
    char_outward,
    char_gain_two,
    char_bias_two,
    char_expand,
    char_expand_bias,
    char_reduce,
    char_reduce_bias,
    char_to_word,
    char_to_word_bias,
    word_gain_one,
    word_bias_one,
    word_inward,
    word_outward,
    word_gain_two,
    word_bias_two,
    word_expand,
    word_expand_bias,
    word_reduce,
    word_reduce_bias,
):
    rows, local, slots, width = char_inputs.shape
    words = rows * local
    langs = language_table.shape[0]
    wide = word_inward.shape[1] // 3
    deep, share = lax.axis_size("dp"), lax.axis_size("fsdp")
    devices = deep * share
    members = share // rows
    axes = ("dp", "fsdp")
    at_deep, at_share = lax.axis_index("dp"), lax.axis_index("fsdp")

    def swap(values, mask):
        return lax.ppermute(values, axes, [(k, k ^ mask) for k in range(devices)])

    far, low = deep // 2, share // 2
    near = 2 * low
    far_masks = [m * 2 * share for m in range(far)]
    near_masks = [(m // low) * share + (m % low) * 2 for m in range(near)]
    core_masks = [0, 1]
    counts_of = (far, near)
    top = members
    my_row = at_share // members
    index = (at_deep * share + at_share).reshape(1)

    def swaps(values, masks):
        return [values] + [swap(values, m) for m in masks[1:]]

    def together(pieces, rows):
        return jnp.stack(pieces).reshape(-1, rows, pieces[0].shape[-1])

    order = [c | n | f for c in core_masks for n in near_masks for f in far_masks]

    char_piece = char_shard(
        language_table.T,
        char_inward,
        char_outward,
        char_expand,
        char_reduce,
        (char_gain_one, char_bias_one, char_gain_two, char_bias_two, char_reduce_bias, char_expand_bias),
    )
    each = char_piece.shape[0]
    counts = tie(char_counts, char_piece)
    offs, first, rows_of, blocks, place = offsets((share, members), counts, row_lengths, index, slots)
    char_piece = together(tie(swaps(char_piece, far_masks), offs), each)
    packed, bias, hot, inverse = pack(
        tie(counts, char_piece), offs, first, blocks, char_inputs.reshape(words, slots, width)
    )
    char_piece = together(swaps(char_piece, near_masks), each)
    char_full = assemble(order, index, swaps(tie(char_piece, packed), core_masks))
    word_full = lax.all_gather(
        word_shard(
            word_inward,
            word_outward,
            word_expand,
            word_reduce,
            char_to_word,
            (
                word_gain_one,
                word_bias_one,
                word_gain_two,
                word_bias_two,
                word_reduce_bias,
                char_to_word_bias,
                word_expand_bias,
            ),
        ),
        axes,
        axis=0,
        tiled=True,
    )

    qkv, soft, mixed, after, cotangent_sent = char_attend(
        langs, blocks, rows_of, language_ids, place, packed, bias, char_full, cotangent
    )
    cotangent_other = swap(cotangent_sent, top)
    act, slope, pooled_kept, pooled_sent = char_ffn(
        langs, blocks, first, place, after, hot, inverse, char_full
    )
    cotangent_other, pooled_kept, pooled_sent = lax.optimization_barrier(
        (cotangent_other, pooled_kept, pooled_sent)
    )
    pooled_other = swap(pooled_sent, top)
    pieces = []
    for m in range(members):
        pieces += [swap(pooled_kept, m), swap(pooled_other, m)] if m else [pooled_kept, pooled_other]
    words_both, words_sent, word_after_grad, word_normed, word_in, word_kept, word_sent, *others = word_part(
        counts_of, place, pieces, word_full, cotangent, cotangent_other
    )
    query_grad, word_sums, *pair_grads = others
    pairs = [pair_grads[0]] + [swap(pair_grads[m], m) for m in range(1, members)]
    word_sent, words_sent, pairs = lax.optimization_barrier((word_sent, words_sent, pairs))
    words_other = swap(words_sent, top)
    word_arrived = [word_kept, swap(word_sent, 1)]
    up_kept, up_sent, to_word_grad, inward_kept, inward_sent = word_end(
        counts_of,
        place,
        pooled_kept,
        pooled_other,
        word_full,
        query_grad,
        word_normed,
        word_in,
        word_after_grad,
        word_sums,
        pairs,
    )
    up_other = swap(up_sent, top)

    def phase(parts, masks):
        return [parts[0]] + [swap(parts[m], masks[m]) for m in range(1, len(masks))]

    word_parts = add_and_cut(word_arrived, near, NEAR, place)
    word_parts, words_other = lax.optimization_barrier((word_parts, words_other))
    up_kept = tie(up_kept, word_parts)
    after_grad, feed_kept, feed_sent, char_sums = char_ffn_back(
        (langs, counts_of),
        blocks,
        first,
        place,
        after,
        hot,
        act,
        slope,
        inverse,
        up_kept,
        up_other,
        char_full,
        to_word_grad,
        (inward_kept, inward_sent),
    )
    word_parts = add_and_cut(tie(phase(word_parts, near_masks), feed_kept), far, FAR, place)
    feed_sent = tie(feed_sent, word_parts)
    late_parts = add_and_cut([feed_kept, swap(feed_sent, 1)], near, NEAR, place)
    after_grad = tie(after_grad, (word_parts, late_parts))
    operands = (packed, qkv, soft, mixed, after_grad, char_full, char_sums)
    *start_grad, attend_kept, attend_sent = char_attend_back(
        (langs, counts_of), blocks, rows_of, language_ids, place, *operands
    )
    arrived_words, arrived_late, attend_kept, attend_sent = lax.optimization_barrier(
        (phase(word_parts, far_masks), phase(late_parts, near_masks), attend_kept, attend_sent)
    )
    late_parts = add_and_cut(arrived_late, far, FAR, place)
    hidden, wide_hidden = FOLD * width, FOLD * wide
    grad_word_expand, grad_word_reduce, grad_word_outward = finish(
        arrived_words,
        (
            ("plain", 0, wide_hidden, word_expand.shape),
            ("folded", wide_hidden, 2 * wide_hidden, word_reduce.shape),
            ("plain", 2 * wide_hidden, 2 * wide_hidden + wide, word_outward.shape),
        ),
    )
    words_out = lax.dynamic_update_index_in_dim(words_both, words_other, 1 - my_row, 0)
    earlier = (words_out, grad_word_expand, grad_word_reduce, grad_word_outward)
    arrived, earlier, late_parts = lax.optimization_barrier(
        ([attend_kept, swap(attend_sent, 1)], earlier, late_parts)
    )
    attend_parts = add_and_cut(arrived, near, NEAR, place)
    char_input_grad = unpack(offs, char_counts, tie(start_grad, attend_parts), slots)
    arrived, arrived_late, char_input_grad = lax.optimization_barrier(
        (phase(attend_parts, near_masks), phase(late_parts, far_masks), char_input_grad)
    )
    attend_parts = add_and_cut(arrived, far, FAR, place)
    char_input_grad = unpack(offs, char_counts, tie(start_grad, attend_parts), slots, char_input_grad)
    arrived, arrived_late, char_input_grad = lax.optimization_barrier(
        (phase(attend_parts, far_masks), arrived_late, char_input_grad)
    )
    at_inward = 2 * hidden + wide
    stop = at_inward + (3 * wide + SMALL) * (wide // width)
    grad_expand, grad_reduce, grad_to_word, grad_word_inward, *word_vectors = finish(
        arrived_late,
        (
            ("plain", 0, hidden, char_expand.shape),
            ("folded", hidden, 2 * hidden, char_reduce.shape),
            ("plain", 2 * hidden, at_inward, char_to_word.shape),
            ("halves", at_inward, stop, word_inward.shape),
        )
        + tuple(
            ("vector", at_inward + 3 * wide, (wide // width, 3 * wide + SMALL, at), vector.shape)
            for at, vector in (
                (0, word_gain_one),
                (1, word_bias_one),
                (2, word_gain_two),
                (3, word_bias_two),
                (4, word_reduce_bias),
                (5, char_to_word_bias),
                (6, word_expand_bias),
            )
        ),
    )
    grad_inward, grad_outward, grad_table, *char_vectors = finish(
        arrived,
        (
            ("plain", 0, 3 * width, char_inward.shape),
            ("plain", 3 * width, 4 * width, char_outward.shape),
            ("plain", 4 * width, 4 * width + langs, (char_inward.shape[0], langs)),
        )
        + tuple(
            ("vector", 4 * width, (1, 0, langs + at), vector.shape)
            for at, vector in (
                (0, char_gain_one),
                (1, char_bias_one),
                (2, char_gain_two),
                (3, char_bias_two),
                (4, char_reduce_bias),
                (5, char_expand_bias),
            )
        ),
    )
    words_out, grad_word_expand, grad_word_reduce, grad_word_outward = earlier

    gain_one, bias_one, gain_two, bias_two, reduce_bias, expand_bias = char_vectors
    wide_gain_one, wide_bias_one, wide_gain_two, wide_bias_two, wide_reduce_bias = word_vectors[:5]
    to_word_bias, wide_expand_bias = word_vectors[5:]
    return (
        words_out,
        char_input_grad.reshape(char_inputs.shape),
        grad_table.T,
        gain_one,
        bias_one,
        grad_inward,
        grad_outward,
        gain_two,
        bias_two,
        grad_expand,
        expand_bias,
        grad_reduce,
        reduce_bias,
        grad_to_word,
        to_word_bias,
        wide_gain_one,
        wide_bias_one,
        grad_word_inward,
        grad_word_outward,
        wide_gain_two,
        wide_bias_two,
        grad_word_expand,
        wide_expand_bias,
        grad_word_reduce,
        wide_reduce_bias,
    )


def solution(mesh):
    both = ("dp", "fsdp")
    vector, matrix = P(both), P(both, None)
    weights = (
        (P(None, both), vector, vector, matrix, matrix, vector, vector)
        + (matrix, vector, matrix, vector, matrix, vector)
        + (vector, vector, matrix, matrix, vector, vector, matrix, vector, matrix, vector)
    )
    in_specs = (
        P("dp", "fsdp", None, None),
        P("dp"),
        P("dp", "fsdp"),
        P("dp"),
        P("dp", "fsdp", None),
    ) + weights
    out_specs = (P("dp", "fsdp", None), P("dp", "fsdp", None, None)) + weights
    return jax.shard_map(body, mesh=mesh, in_specs=in_specs, out_specs=out_specs, check_vma=False)
```

```python
import functools

import jax
import jax.numpy as jnp
from jax import lax
from jax.experimental import pallas as pl
from jax.experimental.pallas import tpu as pltpu
from jax.sharding import PartitionSpec as P

BF = jnp.bfloat16
F32 = jnp.float32
EPS = 1e-05
MASKED = -1e30
CHEADS = 4
WHEADS = 8
HEAD = 64
SCALE = HEAD ** (-0.5)
GROUP = 128
GROUP_BITS = 7
BLOCK = 1024
SPLIT = BLOCK // GROUP
FOLD = 4
SMALL = 128
GELU_A = 0.7978845608028654
GELU_B = 0.044715
MIB = 1024 * 1024
VMEM_LIMIT = 64 * MIB - 65536
MEMBER, ROW, LENGTH, CORE, NEAR, FAR = range(6)


def whole_to_word(held, devices):
    tall, width = held.shape
    rows = tall // 2
    each = rows // devices
    line = lax.broadcasted_iota(jnp.int32, (rows, tall), 0)
    lane = lax.broadcasted_iota(jnp.int32, (rows, tall), 1)
    source = lax.div(line, each) * (2 * each) + lax.rem(line, each)
    halves = [dot((lane == source + k * each).astype(F32).astype(BF), held[...]).astype(BF) for k in range(2)]
    return jnp.concatenate(halves, 1)


def columns(array, width, start):
    return array, pl.BlockSpec((array.shape[0], width), lambda *_: (0, start // width))


def dot(a, b):
    return jnp.dot(a, b, preferred_element_type=F32)


def dot_t(a, b):
    return lax.dot_general(a, b, (((1,), (1,)), ((), ())), preferred_element_type=F32)


def t_dot(a, b):
    return dot(a.T, b)


def norm_parts(hidden):
    centred = hidden - jnp.mean(hidden, -1, keepdims=True)
    spread = lax.rsqrt(jnp.mean(centred * centred, -1, keepdims=True) + EPS)
    return centred * spread, spread


def norm_back(unit, spread, gained):
    return (
        gained
        - jnp.mean(gained, -1, keepdims=True)
        - unit * jnp.mean(gained * unit, -1, keepdims=True)
    ) * spread


def gelu_both(pre):
    square = pre * pre
    turn = jnp.tanh(pre * (GELU_A + (GELU_A * GELU_B) * square))
    half = 0.5 + 0.5 * turn
    slope = half + pre * half * (1.0 - turn) * (GELU_A + (3.0 * GELU_A * GELU_B) * square)
    return pre * half, slope


def fold_rows(values):
    rows, width = values.shape
    return jnp.sum(values.reshape(rows // 8, 8, width), 0)


def head_masks(width, heads):
    lanes = lax.broadcasted_iota(jnp.int32, (1, width), 1) // HEAD
    return [(lanes == h).astype(F32).astype(BF) for h in range(heads)]


def run_blocks(step, begin, end, inputs, outputs):
    def one(*refs):
        step(begin + pl.program_id(0), *refs)

    def spec(ref):
        return pl.BlockSpec((BLOCK, ref.shape[1]), lambda i: (begin + i, 0))

    pltpu.emit_pipeline(
        one,
        grid=(end - begin,),
        in_specs=[spec(ref) for ref in inputs],
        out_specs=[spec(ref) for ref in outputs],
    )(*inputs, *outputs)


def streamed(kernel, scalars, streams, fixed, stream_outs, fixed_outs, scratch, cost, aliases=None):
    hbm = pl.BlockSpec(memory_space=pltpu.HBM)
    fixed = [one if isinstance(one, tuple) else (one, full(one.shape)) for one in fixed]
    return pl.pallas_call(
        kernel,
        out_shape=tuple(jax.ShapeDtypeStruct(*out) for out in tuple(stream_outs) + tuple(fixed_outs)),
        grid_spec=pltpu.PrefetchScalarGridSpec(
            num_scalar_prefetch=len(scalars),
            grid=(1,),
            in_specs=[hbm] * len(streams) + [spec for _, spec in fixed],
            out_specs=(hbm,) * len(stream_outs) + tuple(full(shape) for shape, _ in fixed_outs),
            scratch_shapes=[pltpu.VMEM(*one) if isinstance(one, tuple) else one for one in scratch],
        ),
        input_output_aliases=aliases or {},
        compiler_params=pltpu.CompilerParams(vmem_limit_bytes=VMEM_LIMIT),
        cost_estimate=cost,
    )(*scalars, *streams, *(one for one, _ in fixed))


def full(shape):
    return pl.BlockSpec(shape, lambda *_: (0,) * len(shape))


def offsets_kernel(layout, counts, lengths, index, offs, first, rows_of, blocks, place_out):
    share, members = layout
    rows, per_row = counts.shape
    deep, part = lax.div(index[0], share), lax.rem(index[0], share)
    my_row = lax.div(part, members)
    place_out[MEMBER] = lax.rem(part, members)
    place_out[ROW] = my_row
    place_out[LENGTH] = lengths[my_row]
    place_out[CORE] = lax.rem(part, 2)
    place_out[NEAR] = lax.rem(deep, 2) * (share // 2) + lax.div(part, 2)
    place_out[FAR] = lax.div(deep, 2)

    def clear(g, carry):
        first[g] = 0
        rows_of[g] = 0
        return carry

    lax.fori_loop(0, first.shape[0], clear, 0, unroll=True)
    spare = first.shape[0] - 1

    def place(row, k, at):
        live = counts[row, k]
        w = row * per_row + k
        inside = at & (GROUP - 1)
        at = jnp.where(inside + live > GROUP, at - inside + GROUP, at)
        group = jnp.where((at & (GROUP - 1)) == 0, at >> GROUP_BITS, spare)
        first[group] = w
        rows_of[group] = row
        offs[w] = at
        return at + live

    at = 0
    for row in range(rows):
        at = lax.fori_loop(0, per_row, functools.partial(place, row), at, unroll=8)
        at = ((at + (GROUP - 1)) >> GROUP_BITS) << GROUP_BITS
    blocks[0] = lax.div(at + (BLOCK - 1), BLOCK)


def group_count(words, slots, per_row):
    groups = (words * slots) // (GROUP - slots + 1) + 1 + words // per_row
    return -(-groups // SPLIT) * SPLIT


def offsets(layout, counts, lengths, index, slots):
    rows, per_row = counts.shape
    words = rows * per_row
    groups = group_count(words, slots, per_row)
    smem = pl.BlockSpec(memory_space=pltpu.SMEM)
    sizes = (words, groups + 1, groups + 1, 1, 6)
    return pl.pallas_call(
        functools.partial(offsets_kernel, layout),
        out_shape=tuple(jax.ShapeDtypeStruct((size,), jnp.int32) for size in sizes),
        in_specs=[smem] * 3,
        out_specs=(smem,) * 5,
        cost_estimate=pl.CostEstimate(flops=words * 4000, bytes_accessed=12 * MIB, transcendentals=0),
    )(counts, lengths, index)


def pack_kernel(
    counts, offs, first, blocks, chars, packed_all, bias_all, hot_all, inverse, tags, *wide
):
    slots = chars.shape[1]
    rows, per_row = counts.shape
    slot = lax.broadcasted_iota(jnp.int32, (slots, GROUP), 0)

    def clear_rows(k, carry):
        there = pl.ds(pl.multiple_of(k * GROUP, GROUP), GROUP)
        for part in wide:
            part[there, :] = jnp.zeros((GROUP, GROUP), F32)
        tags[there, :] = jnp.full((GROUP, GROUP), -1.0, F32)
        return carry

    lax.fori_loop(0, blocks[0] * SPLIT, clear_rows, 0)

    def put(row, n, carry):
        w = row * per_row + n
        at = offs[w]
        for k, part in enumerate(wide):
            part[pl.ds(at, slots), :] = chars[w, :, k * GROUP : (k + 1) * GROUP].astype(F32)
        tags[pl.ds(at, slots), :] = jnp.where(slot < counts[row, n], w.astype(F32), -1.0)
        inverse[pl.ds(w, 1), :] = 1.0 / jnp.full((1, GROUP), counts[row, n], jnp.int32).astype(F32)
        return carry

    for row in range(rows):
        lax.fori_loop(0, per_row, functools.partial(put, row), 0, unroll=8)
    lane = lax.broadcasted_iota(jnp.int32, (GROUP, GROUP), 1).astype(F32)

    def step(i, packed, bias, hot):
        for g in range(SPLIT):
            here = slice(g * GROUP, (g + 1) * GROUP)
            there = pl.ds(pl.multiple_of((i * SPLIT + g) * GROUP, GROUP), GROUP)
            tag = tags[there, :]
            bias[here, :] = jnp.where(tag == tag.T, 0.0, MASKED).astype(BF)
            hot[here, :] = (tag - first[i * SPLIT + g].astype(F32) == lane).astype(F32).astype(BF)
            for k, part in enumerate(wide):
                packed[here, k * GROUP : (k + 1) * GROUP] = part[there, :].astype(BF)

    run_blocks(step, 0, blocks[0], (), (packed_all, bias_all, hot_all))


def pack(counts, offs, first, blocks, chars):
    words, slots, width = chars.shape
    rows = group_count(words, slots, counts.shape[1]) * GROUP
    return streamed(
        pack_kernel,
        (counts, offs, first, blocks),
        (),
        (chars,),
        (((rows, width), BF), ((rows, GROUP), BF), ((rows, GROUP), BF)),
        (((words, GROUP), F32),),
        (((rows + GROUP, GROUP), F32),) * (1 + width // GROUP),
        pl.CostEstimate(flops=rows * width * 4, bytes_accessed=rows * width * 10, transcendentals=0),
    )


def unpack_kernel(row, halves, offs, counts, *refs):
    packed = refs[:halves]
    out, held, arrived = refs[-2 - halves], refs[-1 - halves : -1], refs[-1]
    slots = out.shape[1]
    count = counts.shape[1]
    begin = row * count
    here = pl.program_id(0) * out.shape[0]
    slot = lax.broadcasted_iota(jnp.int32, (slots, GROUP), 0)

    @pl.when(pl.program_id(0) == 0)
    def _():
        low = lax.div(offs[begin], BLOCK)
        high = lax.div(offs[begin + count - 1] + (slots + BLOCK - 1), BLOCK)

        def copy(k, j):
            there = pl.ds(pl.multiple_of(k * BLOCK, BLOCK), BLOCK)
            return pltpu.make_async_copy(packed[j].at[there, :], held[j].at[there, :], arrived.at[j, k])

        def fetch(k, carry):
            for j in range(halves):
                copy(k, j).start()
            return carry

        def await_one(k, carry):
            for j in range(halves):
                copy(k, j).wait()
            return carry

        lax.fori_loop(low, high, fetch, 0)
        lax.fori_loop(low, high, await_one, 0)

    def take(k, carry):
        n = here + k
        for j, part in enumerate(held):
            rows = part[pl.ds(offs[begin + n], slots), :]
            out[k, :, j * GROUP : (j + 1) * GROUP] = jnp.where(slot < counts[row, n], rows, 0.0)
        return carry

    lax.fori_loop(0, out.shape[0], take, 0, unroll=8)


def unpack(offs, counts, packed, slots, before=None):
    words = counts.size
    halves = len(packed)
    width = halves * GROUP
    step = words // 8
    row = 0 if before is None else 1
    extra = [] if before is None else [before]
    hbm = pl.BlockSpec(memory_space=pltpu.HBM)
    return pl.pallas_call(
        functools.partial(unpack_kernel, row, halves),
        out_shape=jax.ShapeDtypeStruct((words, slots, width), F32),
        grid_spec=pltpu.PrefetchScalarGridSpec(
            num_scalar_prefetch=2,
            grid=(4,),
            in_specs=[hbm] * (halves + len(extra)),
            out_specs=pl.BlockSpec((step, slots, width), lambda i, *_: (4 * row + i, 0, 0)),
            scratch_shapes=[pltpu.VMEM(part.shape, F32) for part in packed]
            + [pltpu.SemaphoreType.DMA((halves, packed[0].shape[0] // BLOCK))],
        ),
        input_output_aliases={2 + halves: 0} if extra else {},
        compiler_params=pltpu.CompilerParams(vmem_limit_bytes=VMEM_LIMIT),
        cost_estimate=pl.CostEstimate(
            flops=words * slots * width, bytes_accessed=words * slots * width * 4, transcendentals=0
        ),
    )(offs, counts, *packed, *extra)


def with_language(i, rows_of, ids, packed, small_rows):
    parts = []
    for g in range(SPLIT):
        row = small_rows[pl.ds(ids[rows_of[i * SPLIT + g]], 1), :]
        parts.append(packed[g * GROUP : (g + 1) * GROUP, :].astype(F32) + row)
    return jnp.concatenate(parts, 0)


def both_heads(values, lower):
    wide = values.astype(F32)
    return jnp.concatenate([jnp.where(lower, wide, 0.0), jnp.where(lower, 0.0, wide)], 0).astype(BF)


def pick_heads(stacked, lower):
    rows = stacked.shape[0] // 2
    return jnp.where(lower, stacked[:rows], stacked[rows:])


def char_attend_kernel(
    langs,
    blocks,
    rows_of,
    ids,
    place,
    packed_all,
    bias_all,
    cotangent,
    weights,
    small,
    qkv_all,
    soft_all,
    mixed_all,
    after_all,
    cotangent_out,
    small_rows,
    sent,
):
    copy = pltpu.make_async_copy(cotangent.at[1 - place[ROW]], cotangent_out, sent)
    copy.start()
    width = packed_all.shape[1]
    small_rows[...] = small[...].astype(F32).T

    def step(i, packed, bias, qkv_out, soft_out, mixed_out, after_out):
        start = with_language(i, rows_of, ids, packed, small_rows)
        unit, _ = norm_parts(start)
        normed = (unit * small_rows[langs : langs + 1, :] + small_rows[langs + 1 : langs + 2, :]).astype(BF)
        qkv_out[...] = dot(normed, weights[:, : 3 * width]).astype(BF)
        lower = lax.broadcasted_iota(jnp.int32, (GROUP, GROUP), 1) < HEAD
        places = [(slice(g * GROUP, (g + 1) * GROUP), t) for g in range(SPLIT) for t in range(CHEADS // 2)]
        scores = []
        for here, t in places:
            tile = slice(t * GROUP, (t + 1) * GROUP)
            keys = both_heads(qkv_out[here, width + t * GROUP : width + (t + 1) * GROUP], lower)
            scores.append(dot_t(keys, qkv_out[here, tile]))
        softs = []
        for (here, t), score in zip(places, scores):
            blocked = bias[here, :].astype(F32)
            for h in range(2):
                one = score[h * GROUP : (h + 1) * GROUP] * SCALE + blocked
                one = jnp.exp(one - jnp.max(one, 0, keepdims=True))
                one = (one * (1.0 / jnp.sum(one, 0, keepdims=True))).astype(BF)
                soft_out[here, (2 * t + h) * GROUP : (2 * t + h + 1) * GROUP] = one
                softs.append(one)
        for k, (here, t) in enumerate(places):
            values = qkv_out[here, 2 * width + t * GROUP : 2 * width + (t + 1) * GROUP]
            mixed = dot(jnp.concatenate([softs[2 * k].T, softs[2 * k + 1].T], 0), values)
            mixed_out[here, t * GROUP : (t + 1) * GROUP] = pick_heads(mixed, lower).astype(BF)
        after_out[...] = start + dot(mixed_out[...], weights[:, 3 * width : 4 * width])

    run_blocks(step, 0, blocks[0], (packed_all, bias_all), (qkv_all, soft_all, mixed_all, after_all))
    copy.wait()


def char_attend(langs, blocks, rows_of, ids, place, packed, bias, weights, cotangent):
    rows, width = packed.shape
    at_small = weights.shape[1] - SMALL
    return streamed(
        functools.partial(char_attend_kernel, langs),
        (blocks, rows_of, ids, place),
        (packed, bias, cotangent),
        (columns(weights, 4 * width, 0), columns(weights, SMALL, at_small)),
        (
            ((rows, 3 * width), BF),
            ((rows, CHEADS * GROUP), BF),
            ((rows, width), BF),
            ((rows, width), F32),
            (cotangent.shape[1:], BF),
        ),
        (),
        (((SMALL, width), F32), pltpu.SemaphoreType.DMA),
        pl.CostEstimate(
            flops=rows * width * width * 12, bytes_accessed=rows * width * 12, transcendentals=rows * 512
        ),
    )


def char_ffn_kernel(
    langs,
    blocks,
    first,
    place,
    after_all,
    hot_all,
    inverse,
    expand,
    reduced,
    small,
    act_all,
    slope_all,
    kept_out,
    sent_out,
    small_rows,
    *total,
):
    width = after_all.shape[1]
    small_rows[...] = small[...].astype(F32).T
    for part in total:
        part[...] = jnp.zeros_like(part)

    def step(i, after, hot, act_out, slope_out):
        unit, _ = norm_parts(after[...])
        normed = (unit * small_rows[langs + 2 : langs + 3, :] + small_rows[langs + 3 : langs + 4, :]).astype(BF)
        out = after[...] + small_rows[langs + 4 : langs + 5, :]
        for j in range(FOLD):
            cols = slice(j * width, (j + 1) * width)
            pre = dot(normed, expand[:, cols]) + small_rows[langs + 5 + j : langs + 6 + j, :]
            act, slope = gelu_both(pre)
            act = act.astype(BF)
            act_out[:, cols] = act
            slope_out[:, cols] = slope.astype(BF)
            out = out + dot(act, reduced[:, cols])
        out = out.astype(BF)
        for g in range(SPLIT):
            here = slice(g * GROUP, (g + 1) * GROUP)
            words = pl.ds(first[i * SPLIT + g], GROUP)
            found = t_dot(hot[here, :], out[here, :])
            for k, part in enumerate(total):
                part[words, :] = part[words, :] + found[:, k * GROUP : (k + 1) * GROUP]

    run_blocks(step, 0, blocks[0], (after_all, hot_all), (act_all, slope_all))
    local = kept_out.shape[0]
    for out_ref, row in ((kept_out, place[ROW]), (sent_out, 1 - place[ROW])):
        there = pl.ds(pl.multiple_of(row * local, local), local)
        for k, part in enumerate(total):
            out_ref[:, k * GROUP : (k + 1) * GROUP] = (part[there, :] * inverse[there, :]).astype(BF)


def feed_columns(weights, width):
    hidden = FOLD * width
    return (
        columns(weights, hidden, 4 * width),
        columns(weights, hidden, 4 * width + hidden),
        columns(weights, SMALL, weights.shape[1] - SMALL),
    )


def char_ffn(langs, blocks, first, place, after, hot, inverse, weights):
    rows, width = after.shape
    words = inverse.shape[0]
    hidden = FOLD * width
    return streamed(
        functools.partial(char_ffn_kernel, langs),
        (blocks, first, place),
        (after, hot),
        (inverse, *feed_columns(weights, width)),
        (((rows, hidden), BF), ((rows, hidden), BF)),
        (((words // 2, width), BF), ((words // 2, width), BF)),
        (((SMALL, width), F32),) + (((words + GROUP, GROUP), F32),) * (width // GROUP),
        pl.CostEstimate(
            flops=rows * width * width * 16, bytes_accessed=rows * width * 20, transcendentals=rows * 1024
        ),
    )


def sorted_rows(core, counts, rows, cuts=1):
    far, near = counts
    each = rows // (2 * far * near)
    some = each // cuts
    low = near // 2
    line = lax.broadcasted_iota(jnp.int32, (rows, rows), 0)
    piece = lax.div(line, rows // (2 * cuts))
    line = lax.rem(line, rows // (2 * cuts))
    which = lax.rem(piece, cuts)
    core = jnp.bitwise_xor(core, lax.div(piece, cuts))
    inner = lax.rem(line, some)
    part = lax.div(line, some)
    at_far, at_near = lax.rem(part, far), lax.div(part, far)
    device = ((at_far * 2 + lax.div(at_near, low)) * low + lax.rem(at_near, low)) * 2 + core
    source = device * each + which * some + inner
    return (source == lax.broadcasted_iota(jnp.int32, source.shape, 1)).astype(F32).astype(BF)


def folding(back):
    size = FOLD * HEAD
    unit = lax.broadcasted_iota(jnp.int32, (size, size), 1 if back else 0)
    held = lax.broadcasted_iota(jnp.int32, (size, size), 0 if back else 1)
    return (held == (unit & (FOLD - 1)) * HEAD + lax.div(unit, FOLD)).astype(F32).astype(BF)


def unfold_into(out, folded, width):
    size = FOLD * HEAD
    matrix = folding(True)
    for m in range(width // HEAD):
        near = [folded[:, j * width + m * HEAD : j * width + (m + 1) * HEAD] for j in range(FOLD)]
        out[:, m * size : (m + 1) * size] = dot(jnp.concatenate(near, 1), matrix).astype(BF)


def char_ffn_back_kernel(
    settings,
    blocks,
    first,
    place,
    after_all,
    hot_all,
    act_all,
    slope_all,
    inverse,
    up_kept,
    up_sent,
    expand,
    reduced,
    small,
    grad_to_word,
    riding_kept,
    riding_sent,
    grad_after_all,
    kept_out,
    sent_out,
    sums,
    small_rows,
    grad_expand,
    grad_reduce,
    up_rows,
    grads,
    *spread_up,
):
    langs, counts = settings
    width = after_all.shape[1]
    hidden = FOLD * width
    local = up_kept.shape[0]
    small_rows[...] = small[...].astype(F32).T
    for up_in, row in ((up_kept, place[ROW]), (up_sent, 1 - place[ROW])):
        there = pl.ds(pl.multiple_of(row * local, local), local)
        for k, part in enumerate(spread_up):
            cols = slice(k * GROUP, (k + 1) * GROUP)
            part[there, :] = up_in[:, cols].astype(F32) * inverse[there, :]
    for part in spread_up:
        part[2 * local :, :] = jnp.zeros((GROUP, GROUP), F32)
    grad_expand[...] = jnp.zeros_like(grad_expand)
    grad_reduce[...] = jnp.zeros_like(grad_reduce)
    sums[...] = jnp.zeros_like(sums)

    def step(i, after, hot, act, slope, grad_after):
        for g in range(SPLIT):
            here = slice(g * GROUP, (g + 1) * GROUP)
            for k, part in enumerate(spread_up):
                words_here = part[pl.ds(first[i * SPLIT + g], GROUP), :].astype(BF)
                up_rows[here, k * GROUP : (k + 1) * GROUP] = dot(hot[here, :], words_here).astype(BF)
        up = up_rows[...]
        unit, spread = norm_parts(after[...])
        gain = small_rows[langs + 2 : langs + 3, :]
        normed = (unit * gain + small_rows[langs + 3 : langs + 4, :]).astype(BF)
        grad_normed = jnp.zeros((BLOCK, width), F32)
        parts = [slice(j * width, (j + 1) * width) for j in range(FOLD)]
        grad_acts = [
            dot_t(up, reduced[:, j * width : (j + 1) * width]) for j in range(FOLD)
        ]
        grad_pres = []
        for j, cols in enumerate(parts):
            grad_pre = grad_acts[j] * slope[:, cols].astype(F32)
            sums[8 * j : 8 * j + 8, :] += fold_rows(grad_pre)
            grad_pres.append(grad_pre.astype(BF))
        for j, grad_pre in enumerate(grad_pres):
            grad_normed = grad_normed + dot_t(grad_pre, expand[:, j * width : (j + 1) * width])
        turned = normed.T
        for cols, grad_pre in zip(parts, grad_pres):
            grad_expand[:, cols] += dot(turned, grad_pre)
        turned = up.T
        for cols in parts:
            grad_reduce[:, cols] += dot(turned, act[:, cols])
        up_wide = up.astype(F32)
        sums[32:40, :] += fold_rows(grad_normed * unit)
        sums[40:48, :] += fold_rows(grad_normed)
        sums[48:56, :] += fold_rows(up_wide)
        grad_after[...] = up_wide + norm_back(unit, spread, grad_normed * gain)

    run_blocks(step, 0, blocks[0], (after_all, hot_all, act_all, slope_all), (grad_after_all,))
    unfold_into(grads.at[:, :hidden], grad_expand[...].astype(BF), width)
    for j in range(FOLD):
        grads[:, hidden + j * width : hidden + (j + 1) * width] = (
            grad_reduce[:, j * width : (j + 1) * width].T.astype(BF)
        )
    grads[:, 2 * hidden :] = grad_to_word[...]
    own = grads.shape[1]
    ranked = dot(sorted_rows(place[CORE], counts, width), grads[...]).astype(BF)
    kept_out[:, :own] = ranked[: width // 2]
    sent_out[:, :own] = ranked[width // 2 :]
    kept_out[:, own:] = riding_kept[...]
    sent_out[:, own:] = riding_sent[...]


def char_ffn_back(
    settings,
    blocks,
    first,
    place,
    after,
    hot,
    act,
    slope,
    inverse,
    up_kept,
    up_sent,
    weights,
    grad_to_word,
    riding,
):
    rows, width = after.shape
    words = inverse.shape[0]
    hidden = FOLD * width
    span = 2 * hidden + grad_to_word.shape[1]
    return streamed(
        functools.partial(char_ffn_back_kernel, settings),
        (blocks, first, place),
        (after, hot, act, slope),
        (inverse, up_kept, up_sent, *feed_columns(weights, width), grad_to_word, *riding),
        (((rows, width), F32),),
        (((width // 2, span + riding[0].shape[1]), BF),) * 2 + (((64, width), F32),),
        (
            ((SMALL, width), F32),
            ((width, hidden), F32),
            ((width, hidden), F32),
            ((BLOCK, width), BF),
            ((width, span), BF),
        )
        + (((words + GROUP, GROUP), F32),) * (width // GROUP),
        pl.CostEstimate(
            flops=rows * width * width * 32, bytes_accessed=rows * width * 20, transcendentals=0
        ),
    )


def char_attend_back_kernel(settings, blocks, rows_of, ids, place, *refs):
    langs, counts = settings
    streams, refs = refs[:5], refs[5:]
    width = streams[0].shape[1]
    halves = width // GROUP
    (weights, small, sums_in), refs = refs[:3], refs[3:]
    start_all, refs = refs[:halves], refs[halves:]
    kept_out, sent_out, small_rows, grad_mixed, grad_qkv, grad_in, lines, grads = refs
    grad_in[...] = jnp.zeros_like(grad_in)
    lines[...] = jnp.zeros_like(lines)
    small_rows[...] = small[...].astype(F32).T

    def step(i, packed, qkv, soft, mixed, grad_after, *grad_start):
        start = with_language(i, rows_of, ids, packed, small_rows)
        unit, spread = norm_parts(start)
        gain = small_rows[langs : langs + 1, :]
        normed = (unit * gain + small_rows[langs + 1 : langs + 2, :]).astype(BF)
        after_low = grad_after[...].astype(BF)
        grad_in[:, 3 * width :] += t_dot(mixed[...], after_low)
        grad_mixed[...] = dot_t(after_low, weights[:, 3 * width : 4 * width]).astype(BF)
        lower = lax.broadcasted_iota(jnp.int32, (GROUP, GROUP), 1) < HEAD
        places = [(slice(g * GROUP, (g + 1) * GROUP), t) for g in range(SPLIT) for t in range(CHEADS // 2)]

        def tile_of(values, which, k):
            here, t = places[k]
            return values[here, which * width + t * GROUP : which * width + (t + 1) * GROUP]

        every = range(len(places))
        lows = [both_heads(tile_of(grad_mixed, 0, k), lower) for k in every]
        grad_softs = [dot_t(tile_of(qkv, 2, k), lows[k]) for k in every]
        weights_of = [soft[here, 2 * t * GROUP : (2 * t + 2) * GROUP] for here, t in places]
        ones = []
        for weight, grad_soft in zip(weights_of, grad_softs):
            wide = weight.astype(F32)
            ones.append((wide * (grad_soft - jnp.sum(wide * grad_soft, 0, keepdims=True))).astype(BF))
        for k, (here, t) in enumerate(places):
            value = dot(weights_of[k], lows[k])
            grad_qkv[here, 2 * width + t * GROUP : 2 * width + (t + 1) * GROUP] = value.astype(BF)
        for k, (here, t) in enumerate(places):
            value = dot(ones[k], both_heads(tile_of(qkv, 0, k), lower))
            grad_qkv[here, width + t * GROUP : width + (t + 1) * GROUP] = (value * SCALE).astype(BF)
        for k, (here, t) in enumerate(places):
            turned = jnp.concatenate([ones[k][:, :GROUP].T, ones[k][:, GROUP:].T], 1)
            value = dot(turned, both_heads(tile_of(qkv, 1, k), lower))
            grad_qkv[here, t * GROUP : (t + 1) * GROUP] = (value * SCALE).astype(BF)
        grad_in[:, : 3 * width] += t_dot(normed, grad_qkv[...])
        grad_normed = dot_t(grad_qkv[...], weights[:, : 3 * width])
        lines[SMALL : SMALL + 8, :] += fold_rows(grad_normed * unit)
        lines[SMALL + 8 :, :] += fold_rows(grad_normed)
        result = grad_after[...] + norm_back(unit, spread, grad_normed * gain)
        for k, part in enumerate(grad_start):
            part[...] = result[:, k * GROUP : (k + 1) * GROUP]
        for g in range(SPLIT):
            line = pl.ds(ids[rows_of[i * SPLIT + g]], 1)
            part = jnp.sum(result[g * GROUP : (g + 1) * GROUP, :], 0, keepdims=True)
            lines[line, :] = lines[line, :] + part

    run_blocks(step, 0, blocks[0], streams, start_all)

    def put(at, block):
        lines[langs + at : langs + at + 1, :] = jnp.sum(block, 0, keepdims=True)

    put(0, lines[SMALL : SMALL + 8, :])
    put(1, lines[SMALL + 8 :, :])
    put(2, sums_in[32:40, :])
    put(3, sums_in[40:48, :])
    put(4, sums_in[48:56, :])
    for j in range(FOLD):
        put(5 + j, sums_in[8 * j : 8 * j + 8, :])
    grads[:, : 4 * width] = grad_in[...].astype(BF)
    grads[:, 4 * width :] = lines[:SMALL, :].T.astype(BF)
    ranked = dot(sorted_rows(place[CORE], counts, width), grads[...]).astype(BF)
    kept_out[...] = ranked[: width // 2]
    sent_out[...] = ranked[width // 2 :]


def char_attend_back(
    settings, blocks, rows_of, ids, place, packed, qkv, soft, mixed, grad_after, weights, sums
):
    rows, width = packed.shape
    span = 4 * width + SMALL
    return streamed(
        functools.partial(char_attend_back_kernel, settings),
        (blocks, rows_of, ids, place),
        (packed, qkv, soft, mixed, grad_after),
        (columns(weights, 4 * width, 0), columns(weights, SMALL, weights.shape[1] - SMALL), sums),
        (((rows + BLOCK, GROUP), F32),) * (width // GROUP),
        (((width // 2, span), BF),) * 2,
        (
            ((SMALL, width), F32),
            ((BLOCK, width), BF),
            ((BLOCK, 3 * width), BF),
            ((width, 4 * width), F32),
            ((SMALL + 16, width), F32),
            ((width, span), BF),
        ),
        pl.CostEstimate(
            flops=rows * width * width * 24, bytes_accessed=rows * width * 20, transcendentals=0
        ),
    )


def word_kernel(
    counts,
    members,
    place,
    weights_all,
    cotangent,
    cotangent_other,
    *refs,
):
    pieces, refs = refs[: 2 * members], refs[2 * members :]
    away, refs = refs[:7], refs[7:]
    grad_query_out, sums_out = refs[:2]
    pair_outs, refs = refs[2 : 2 + members], refs[2 + members :]
    words_both, words_sent, grad_after_out, normed_out, word_in_out, kept_out, sent_out = refs[:7]
    sent_sem, weights, to_word, held_sem = refs[7:11]
    refs = refs[11:]
    (
        small_rows,
        pooled,
        word_all,
        normed_all,
        pair,
        query,
        blocked,
        soft_near,
        soft_far,
        mixed,
        after,
        unit_two,
        normed_two,
        up_low,
        total,
        grad_normed,
        grads,
        natural,
        grad_pair,
    ) = refs
    member = place[MEMBER]
    my_row = place[ROW]
    length = place[LENGTH]
    all_words, narrow = pooled.shape
    width = up_low.shape[1]
    own_words = up_low.shape[0]
    local = own_words // 2
    half = all_words // 2
    hidden = FOLD * width
    reach = (half, all_words)
    at_out, at_expand, at_reduce = 3 * width, 4 * width, 4 * width + hidden
    at_to_word = at_reduce + hidden
    at_small = at_to_word + width // 2

    def fetch(k, start, stop):
        return pltpu.make_async_copy(
            weights_all.at[:, start:stop], weights.at[:, start:stop], held_sem.at[k]
        )

    early = (
        fetch(0, at_to_word, at_small + SMALL),
        fetch(1, 0, at_out),
    )
    late = (fetch(2, at_out, at_expand), fetch(3, at_expand, at_to_word))
    for copy in early + late:
        copy.start()
    leaving = [
        pltpu.make_async_copy(here, there, sent_sem.at[k])
        for k, (here, there) in enumerate(
            zip((words_both, words_sent, grad_after_out, normed_out, word_in_out, kept_out, sent_out), away)
        )
    ]
    for copy in early:
        copy.wait()
    small_rows[...] = weights[:, at_small:].astype(F32).T
    to_word[...] = whole_to_word(weights.at[:, at_to_word:at_small], 2 * counts[0] * counts[1])

    def rows_at(index):
        return pl.ds(pl.multiple_of(index * local, local), local)

    for m in range(members):
        there = jnp.bitwise_xor(member, m)
        pooled[rows_at(my_row * members + there), :] = pieces[2 * m][...]
        pooled[rows_at((1 - my_row) * members + there), :] = pieces[2 * m + 1][...]

    def embed(t, carry):
        here = pl.ds(pl.multiple_of(t * local, local), local)
        value = dot(pooled[here, :], to_word[...]) + small_rows[5:6, :]
        word_all[here, :] = value
        unit, _ = norm_parts(value)
        normed = (unit * small_rows[0:1, :] + small_rows[1:2, :]).astype(BF)
        normed_all[here, :] = normed
        pair[here, :] = dot(normed, weights[:, width : 3 * width]).astype(BF)
        return carry

    lax.fori_loop(0, all_words // local, embed, 0, unroll=4)
    origin = []
    for t in range(2):
        base = member * local + t * half
        origin.append(base)
        here = slice(t * local, (t + 1) * local)
        word_in_out[here, :] = word_all[rows_at(member + t * members), :]
        normed_out[here, :] = normed_all[rows_at(member + t * members), :]
    leaving[3].start()
    leaving[4].start()
    query[...] = dot(normed_out[...], weights[:, :width]).astype(BF)
    masks = head_masks(GROUP, 2)
    lower = lax.broadcasted_iota(jnp.int32, (local, GROUP), 1) < HEAD
    softs = (soft_near, soft_far)

    for t in range(2):
        seen = lax.broadcasted_iota(jnp.int32, (local, reach[t]), 1)
        asks = lax.broadcasted_iota(jnp.int32, (local, reach[t]), 0) + origin[t]
        blocked[t * local : (t + 1) * local, : reach[t]] = jnp.where((seen <= asks) & (seen < length), 0.0, MASKED)
    chains = [(slice(t * local, (t + 1) * local), t, h) for t in range(2) for h in range(2)]

    def attend(p, carry):
        lanes = pl.ds(pl.multiple_of(p * GROUP, GROUP), GROUP)
        after_lanes = pl.ds(pl.multiple_of(width + p * GROUP, GROUP), GROUP)
        scores = [dot_t(query[here, lanes] * masks[h], pair[: reach[t], lanes]) for here, t, h in chains]
        weights_of = []
        for (here, t, h), score in zip(chains, scores):
            score = score * SCALE + blocked[here, : reach[t]]
            score = jnp.exp(score - jnp.max(score, -1, keepdims=True))
            soft = (score * (1.0 / jnp.sum(score, -1, keepdims=True))).astype(BF)
            softs[t][2 * p + h] = soft
            weights_of.append(soft)
        outs = [dot(soft, pair[: reach[t], after_lanes]) for (_, t, h), soft in zip(chains, weights_of)]
        for t in range(2):
            mixed[t * local : (t + 1) * local, lanes] = jnp.where(lower, outs[2 * t], outs[2 * t + 1]).astype(BF)
        return carry

    lax.fori_loop(0, WHEADS // 2, attend, 0, unroll=4)
    for copy in late:
        copy.wait()
    value = word_in_out[...] + dot(mixed[...], weights[:, at_out : at_out + width])
    after[...] = value
    unit, spread = norm_parts(value)
    unit_two[...] = unit
    normed_two[...] = (unit * small_rows[2:3, :] + small_rows[3:4, :]).astype(BF)
    row = lax.broadcasted_iota(jnp.int32, (own_words, 1), 0)
    index = jnp.where(row < local, origin[0] + row, origin[1] + row - local)
    valid = index < length
    up_low[rows_at(my_row), :] = cotangent[my_row]
    up_low[rows_at(1 - my_row), :] = cotangent_other[...]
    up_low[...] = jnp.where(valid, up_low[...].astype(F32), 0.0).astype(BF)
    total[...] = jnp.zeros_like(total)
    grad_normed[...] = jnp.zeros_like(grad_normed)

    def feed(j, carry):
        expand = weights[:, pl.ds(pl.multiple_of(at_expand + j * width, GROUP), width)]
        shrink = weights[:, pl.ds(pl.multiple_of(at_reduce + j * width, GROUP), width)]
        pre = dot(normed_two[...], expand) + small_rows[pl.ds(6 + j, 1), :]
        act, slope = gelu_both(pre)
        act = act.astype(BF)
        total[...] += dot(act, shrink)
        grad_pre = dot_t(up_low[...], shrink) * slope
        sums_out[pl.ds(6 + j, 1), :] = jnp.sum(grad_pre, 0, keepdims=True)
        grad_pre = grad_pre.astype(BF)
        grad_normed[...] += dot_t(grad_pre, expand)
        cols = pl.multiple_of(j * width, GROUP)
        grads[:, pl.ds(cols, width)] = t_dot(normed_two[...], grad_pre).astype(BF)
        grads[:, pl.ds(pl.multiple_of(hidden + j * width, GROUP), width)] = t_dot(
            act, up_low[...]
        ).astype(BF)
        return carry

    lax.fori_loop(0, FOLD, feed, 0, unroll=4)
    total[...] = jnp.where(valid, after[...] + (total[...] + small_rows[4:5, :]), 0.0)
    for t in range(2):
        words_both[t] = total[t * local : (t + 1) * local, :]
    words_sent[...] = total[rows_at(1 - my_row), :]
    leaving[0].start()
    leaving[1].start()
    upstream = up_low[...].astype(F32)
    incoming = grad_normed[...]
    sums_out[2:3, :] = jnp.sum(incoming * unit_two[...], 0, keepdims=True)
    sums_out[3:4, :] = jnp.sum(incoming, 0, keepdims=True)
    sums_out[4:5, :] = jnp.sum(upstream, 0, keepdims=True)
    grad_after = upstream + norm_back(unit_two[...], spread, incoming * small_rows[2:3, :])
    grad_after_out[...] = grad_after
    leaving[2].start()
    grad_low = grad_after.astype(BF)
    grads[:, 2 * hidden :] = t_dot(mixed[...], grad_low).astype(BF)
    mixed[...] = dot_t(grad_low, weights[:, at_out : at_out + width]).astype(BF)
    unfold_into(natural, grads[:, :hidden], width)
    chosen = sorted_rows(place[CORE], counts, width)
    for from_ref, start, stop in ((natural, 0, hidden), (grads, hidden, grads.shape[1])):
        ranked = dot(chosen, from_ref[:, start:stop]).astype(BF)
        kept_out[:, start:stop] = ranked[: width // 2]
        sent_out[:, start:stop] = ranked[width // 2 :]
    leaving[5].start()
    leaving[6].start()

    def attend_back(p, carry):
        lanes = pl.ds(pl.multiple_of(p * GROUP, GROUP), GROUP)
        after_lanes = pl.ds(pl.multiple_of(width + p * GROUP, GROUP), GROUP)
        lows = [mixed[here, lanes] * masks[h] for here, t, h in chains]
        ones = [dot_t(low, pair[: reach[t], after_lanes]) for low, (_, t, h) in zip(lows, chains)]
        weights_of = [softs[t][2 * p + h] for _, t, h in chains]
        grads_of = []
        for one, soft in zip(ones, weights_of):
            wide = soft.astype(F32)
            grads_of.append((wide * (one - jnp.sum(wide * one, -1, keepdims=True))).astype(BF))
        grad_values = [dot(soft.T, low) for soft, low in zip(weights_of, lows)]
        grad_keys = [
            dot(one.T, query[here, lanes] * masks[h]) for one, (here, t, h) in zip(grads_of, chains)
        ]
        grad_queries = [dot(one, pair[: reach[t], lanes]) for one, (_, t, h) in zip(grads_of, chains)]
        grad_values = [grad_values[2 * t] + grad_values[2 * t + 1] for t in range(2)]
        grad_keys = [grad_keys[2 * t] + grad_keys[2 * t + 1] for t in range(2)]
        for t in range(2):
            grad_query = jnp.where(lower, grad_queries[2 * t], grad_queries[2 * t + 1])
            grad_query_out[t * local : (t + 1) * local, lanes] = (grad_query * SCALE).astype(BF)
        for parts, at, factor in ((grad_keys, lanes, SCALE), (grad_values, after_lanes, 1.0)):
            grad_pair[:half, at] = ((parts[0] + parts[1][:half]) * factor).astype(BF)
            grad_pair[half:, at] = (parts[1][half:] * factor).astype(BF)
        return carry

    lax.fori_loop(0, WHEADS // 2, attend_back, 0)
    for m in range(members):
        there = jnp.bitwise_xor(member, m)
        for t in range(2):
            pair_outs[m][t * local : (t + 1) * local, :] = grad_pair[rows_at(t * members + there), :]
    for copy in leaving:
        copy.wait()


def word_part(counts, place, pieces, weights, cotangent, cotangent_other):
    members = len(pieces) // 2
    local, narrow = pieces[0].shape
    all_words = local * len(pieces)
    width = cotangent.shape[2]
    own = 2 * local
    hidden = FOLD * width
    vmem = pl.BlockSpec(memory_space=pltpu.VMEM)
    hbm = pl.BlockSpec(memory_space=pltpu.HBM)
    share = ((width // 2, 2 * hidden + width), BF)
    away = (
        ((2, local, width), F32),
        ((local, width), F32),
        ((own, width), F32),
        ((own, width), BF),
        ((own, width), F32),
        share,
        share,
    )
    stay = (((own, width), BF), ((16, width), F32)) + (((own, 2 * width), BF),) * members
    return pl.pallas_call(
        functools.partial(word_kernel, counts, members),
        out_shape=tuple(jax.ShapeDtypeStruct(*out) for out in away + stay),
        in_specs=[pl.BlockSpec(memory_space=pltpu.SMEM), hbm] + [vmem] * (2 + len(pieces)),
        out_specs=(hbm,) * len(away) + (vmem,) * len(stay),
        scratch_shapes=[pltpu.VMEM(*out) for out in away]
        + [
            pltpu.SemaphoreType.DMA((len(away),)),
            pltpu.VMEM(weights.shape, BF),
            pltpu.VMEM((narrow, width), BF),
            pltpu.SemaphoreType.DMA((4,)),
            pltpu.VMEM((SMALL, width), F32),
            pltpu.VMEM((all_words, narrow), BF),
            pltpu.VMEM((all_words, width), F32),
            pltpu.VMEM((all_words, width), BF),
            pltpu.VMEM((all_words, 2 * width), BF),
            pltpu.VMEM((own, width), BF),
            pltpu.VMEM((own, all_words), F32),
            pltpu.VMEM((WHEADS, local, all_words // 2), BF),
            pltpu.VMEM((WHEADS, local, all_words), BF),
            pltpu.VMEM((own, width), BF),
            pltpu.VMEM((own, width), F32),
            pltpu.VMEM((own, width), F32),
            pltpu.VMEM((own, width), BF),
            pltpu.VMEM((own, width), BF),
            pltpu.VMEM((own, width), F32),
            pltpu.VMEM((own, width), F32),
            pltpu.VMEM((width, 2 * hidden + width), BF),
            pltpu.VMEM((width, hidden), BF),
            pltpu.VMEM((all_words, 2 * width), BF),
        ],
        compiler_params=pltpu.CompilerParams(vmem_limit_bytes=VMEM_LIMIT),
        cost_estimate=pl.CostEstimate(
            flops=own * width * width * 60, bytes_accessed=20 * MIB, transcendentals=own * 8192
        ),
    )(place, weights, cotangent, cotangent_other, *pieces)


def word_end_kernel(
    counts,
    place,
    pooled_kept,
    pooled_other,
    to_word_ref,
    weights,
    small,
    grad_query,
    normed,
    word_in,
    grad_after,
    sums,
    *refs,
):
    pairs, refs = refs[:-8], refs[-8:]
    up_kept, up_sent, grad_to_word, kept_out, sent_out, small_rows, small_grads, incoming = refs
    width = grad_query.shape[1]
    local, narrow = pooled_kept.shape
    to_word = whole_to_word(to_word_ref, 2 * counts[0] * counts[1])
    small_rows[...] = small[...].astype(F32).T
    incoming[:, :width] = grad_query[...]
    pair = pairs[0][...].astype(F32)
    for other in pairs[1:]:
        pair = pair + other[...].astype(F32)
    incoming[:, width:] = pair.astype(BF)
    grad_normed = dot_t(incoming[...], weights[...])
    unit, spread = norm_parts(word_in[...])
    small_grads[...] = jnp.zeros_like(small_grads)
    small_grads[0:1, :] = jnp.sum(grad_normed * unit, 0, keepdims=True)
    small_grads[1:2, :] = jnp.sum(grad_normed, 0, keepdims=True)
    small_grads[2:5, :] = sums[2:5, :]
    small_grads[6:10, :] = sums[6:10, :]
    value = grad_after[...] + norm_back(unit, spread, grad_normed * small_rows[0:1, :])
    small_grads[5:6, :] = jnp.sum(value, 0, keepdims=True)
    low = value.astype(BF)
    back = dot_t(low, to_word).astype(BF)
    first_half = place[ROW] == 0
    up_kept[...] = jnp.where(first_half, back[:local].astype(F32), back[local:].astype(F32)).astype(BF)
    up_sent[...] = jnp.where(first_half, back[local:].astype(F32), back[:local].astype(F32)).astype(BF)
    low_kept = jnp.where(first_half, value[:local], value[local:]).astype(BF)
    low_other = jnp.where(first_half, value[local:], value[:local]).astype(BF)
    grad_to_word[...] = (t_dot(pooled_kept[...], low_kept) + t_dot(pooled_other[...], low_other)).astype(BF)
    inward = t_dot(normed[...], incoming[...]).astype(BF)
    small_turned = small_grads[...].T.astype(BF)
    span = 3 * width + SMALL
    cuts = width // narrow
    chosen = sorted_rows(place[CORE], counts, width, cuts)
    ranked = dot(chosen, inward).astype(BF)
    ranked_small = dot(chosen, small_turned).astype(BF)
    some = narrow // 2
    for k in range(2 * cuts):
        out_ref = (kept_out, sent_out)[k // cuts]
        at = k % cuts * span
        out_ref[:, at : at + 3 * width] = ranked[k * some : (k + 1) * some]
        out_ref[:, at + 3 * width : at + span] = ranked_small[k * some : (k + 1) * some]


def word_end(
    counts,
    place,
    pooled_kept,
    pooled_other,
    weights,
    grad_query,
    normed,
    word_in,
    grad_after,
    sums,
    pairs,
):
    local, narrow = pooled_kept.shape
    own, width = grad_query.shape
    last = weights.shape[1] // SMALL - 1
    share = (narrow // 2, (3 * width + SMALL) * (width // narrow))
    outs = ((local, narrow), (local, narrow), (narrow, width), share, share)
    operands = (grad_query, normed, word_in, grad_after, sums) + tuple(pairs)
    return pl.pallas_call(
        functools.partial(word_end_kernel, counts),
        out_shape=tuple(jax.ShapeDtypeStruct(shape, BF) for shape in outs),
        grid_spec=pltpu.PrefetchScalarGridSpec(
            num_scalar_prefetch=1,
            grid=(1,),
            in_specs=[
                full(pooled_kept.shape),
                full(pooled_other.shape),
                columns(weights, width // 2, 12 * width)[1],
                pl.BlockSpec((width, 3 * width), lambda i, *_: (0, 0)),
                pl.BlockSpec((width, SMALL), lambda i, *_: (0, last)),
            ]
            + [full(operand.shape) for operand in operands],
            out_specs=tuple(full(shape) for shape in outs),
            scratch_shapes=[
                pltpu.VMEM((SMALL, width), F32),
                pltpu.VMEM((SMALL, width), F32),
                pltpu.VMEM((own, 3 * width), BF),
            ],
        ),
        compiler_params=pltpu.CompilerParams(vmem_limit_bytes=VMEM_LIMIT),
        cost_estimate=pl.CostEstimate(
            flops=own * width * width * 14, bytes_accessed=10 * MIB, transcendentals=0
        ),
    )(place, pooled_kept, pooled_other, weights, weights, weights, *operands)


def column(vector, rows):
    each = vector.shape[0] // rows
    wide = vector[...].astype(F32).reshape(1, rows * each)
    line = lax.broadcasted_iota(jnp.int32, (rows, rows * each), 0)
    lane = lax.broadcasted_iota(jnp.int32, (rows, rows * each), 1)
    return [
        jnp.sum(jnp.where(line * each + j == lane, wide, 0.0), 1, keepdims=True) for j in range(each)
    ]


def columns_beside(rows, vectors, at):
    lane = lax.broadcasted_iota(jnp.int32, (rows, SMALL), 1)
    block = jnp.zeros((rows, SMALL), F32)
    for vector in vectors:
        for one in column(vector, rows):
            block = block + jnp.where(lane == at, one, 0.0)
            at += 1
    return block


def fold_into(out, at, weights, width):
    size = FOLD * HEAD
    matrix = folding(False)
    for m in range(width // HEAD):
        block = dot(weights[:, m * size : (m + 1) * size], matrix).astype(BF)
        for j in range(FOLD):
            there = at + j * width + m * HEAD
            out[:, there : there + HEAD] = block[:, j * HEAD : (j + 1) * HEAD]


def fold_shard(weights):
    tall = weights.shape[0]
    rows = tall // FOLD
    line = lax.broadcasted_iota(jnp.int32, (rows, tall), 0)
    lane = lax.broadcasted_iota(jnp.int32, (rows, tall), 1)
    return [
        dot((lane == FOLD * line + j).astype(F32).astype(BF), weights[...]).astype(BF) for j in range(FOLD)
    ]


def char_shard_kernel(table, inward, outward, expand, reduced, *refs):
    vectors, out = refs[:-1], refs[-1]
    rows, langs = table.shape
    width = outward.shape[1]
    at_expand, at_reduce, at_small = 4 * width, (4 + FOLD) * width, (4 + 2 * FOLD) * width
    out[:, : 3 * width] = inward[...]
    out[:, 3 * width : 4 * width] = outward[...]
    line = lax.broadcasted_iota(jnp.int32, (langs, SMALL), 0)
    lane = lax.broadcasted_iota(jnp.int32, (langs, SMALL), 1)
    spread = (line == lane).astype(F32).astype(BF)
    small = dot(table[...], spread) + columns_beside(rows, vectors, langs)
    out[:, at_small:] = small.astype(BF)
    fold_into(out, at_expand, expand, width)
    for j, part in enumerate(fold_shard(reduced)):
        out[:, at_reduce + j * width : at_reduce + (j + 1) * width] = part


def char_shard(table, inward, outward, expand, reduced, vectors):
    rows, width = outward.shape
    vmem = pl.BlockSpec(memory_space=pltpu.VMEM)
    return pl.pallas_call(
        char_shard_kernel,
        out_shape=jax.ShapeDtypeStruct((rows, (4 + 2 * FOLD) * width + SMALL), BF),
        in_specs=[vmem] * (5 + len(vectors)),
        out_specs=vmem,
    )(table, inward, outward, expand, reduced, *vectors)


def word_shard_kernel(inward, outward, expand, reduced, to_word, *refs):
    vectors, out = refs[:-1], refs[-1]
    rows, width = outward.shape
    out[:, : 3 * width] = inward[...]
    out[:, 3 * width : 4 * width] = outward[...]
    fold_into(out, 4 * width, expand, width)
    for j, part in enumerate(fold_shard(reduced)):
        out[:, (8 + j) * width : (9 + j) * width] = part
    narrow, half = to_word.shape[0], width // 2
    for k in range(2):
        out[k * narrow : (k + 1) * narrow, 12 * width : 12 * width + half] = to_word[:, k * half : (k + 1) * half]
    out[:, 12 * width + half :] = columns_beside(rows, vectors, 0).astype(BF)


def word_shard(inward, outward, expand, reduced, to_word, vectors):
    rows, width = outward.shape
    vmem = pl.BlockSpec(memory_space=pltpu.VMEM)
    return pl.pallas_call(
        word_shard_kernel,
        out_shape=jax.ShapeDtypeStruct((rows, 12 * width + width // 2 + SMALL), BF),
        in_specs=[vmem] * (5 + len(vectors)),
        out_specs=vmem,
    )(inward, outward, expand, reduced, to_word, *vectors)


def assemble_kernel(masks, index, *refs):
    pieces, out = refs[:-1], refs[-1]
    me = index[0]
    size = pieces[0].shape[0]
    for k, piece in enumerate(pieces):
        for t in range(size):
            out[jnp.bitwise_xor(me, masks[k * size + t])] = piece[t]


def assemble(masks, index, pieces):
    size, rows, columns = pieces[0].shape
    vmem = pl.BlockSpec(memory_space=pltpu.VMEM)
    out = pl.pallas_call(
        functools.partial(assemble_kernel, tuple(masks)),
        out_shape=jax.ShapeDtypeStruct((size * len(pieces), rows, columns), BF),
        in_specs=[pl.BlockSpec(memory_space=pltpu.SMEM)] + [vmem] * len(pieces),
        out_specs=vmem,
        compiler_params=pltpu.CompilerParams(vmem_limit_bytes=VMEM_LIMIT),
        cost_estimate=pl.CostEstimate(
            flops=0, bytes_accessed=4 * size * len(pieces) * rows * columns, transcendentals=0
        ),
    )(index, *pieces)
    return out.reshape(-1, columns)


def add_and_cut_kernel(which, arrivals, place, *refs):
    arrived, outs = refs[:arrivals], refs[arrivals:]
    total = arrived[0][...].astype(F32)
    for one in arrived[1:]:
        total = total + one[...].astype(F32)
    total = total.astype(BF)
    rows = total.shape[0]
    each = rows // len(outs)
    line = lax.broadcasted_iota(jnp.int32, (rows, rows), 0)
    lane = lax.broadcasted_iota(jnp.int32, (rows, rows), 1)
    part = jnp.bitwise_xor(lax.div(line, each), place[which])
    chosen = (lane == part * each + lax.rem(line, each)).astype(F32).astype(BF)
    sorted_total = dot(chosen, total).astype(BF)
    for m, out in enumerate(outs):
        out[...] = sorted_total[m * each : (m + 1) * each]


def add_and_cut(arrived, parts, which, place):
    rows, columns = arrived[0].shape

    vmem = pl.BlockSpec(memory_space=pltpu.VMEM)
    return pl.pallas_call(
        functools.partial(add_and_cut_kernel, which, len(arrived)),
        out_shape=(jax.ShapeDtypeStruct((rows // parts, columns), BF),) * parts,
        in_specs=[pl.BlockSpec(memory_space=pltpu.SMEM)] + [vmem] * len(arrived),
        out_specs=(vmem,) * parts,
        compiler_params=pltpu.CompilerParams(vmem_limit_bytes=VMEM_LIMIT),
        cost_estimate=pl.CostEstimate(
            flops=0, bytes_accessed=sum(4 * one.size for one in arrived), transcendentals=0
        ),
    )(place, *arrived)


def unfold_rows(folded, rows, out):
    width = out.shape[1]
    line = lax.broadcasted_iota(jnp.int32, (FOLD * rows, rows), 0)
    lane = lax.broadcasted_iota(jnp.int32, (FOLD * rows, rows), 1)
    total = jnp.zeros(out.shape, F32)
    for j in range(FOLD):
        chosen = (line == FOLD * lane + j).astype(F32)
        total = total + lax.dot_general(
            chosen,
            folded[:, j * width : (j + 1) * width],
            (((1,), (0,)), ((), ())),
            precision=lax.Precision.HIGHEST,
            preferred_element_type=F32,
        )
    out[...] = total


def finish_kernel(plan, count, *refs):
    arrived, outs = refs[:count], refs[count:]
    total = arrived[0][...].astype(F32)
    for one in arrived[1:]:
        total = total + one[...].astype(F32)
    rows = total.shape[0]
    for (kind, start, stop), out in zip(plan, outs):
        if kind == "folded":
            unfold_rows(total[:, start:stop], rows, out)
        elif kind == "plain":
            out[...] = total[:, start:stop]
        elif kind == "halves":
            height, width = out.shape
            pieces = height // rows
            stride = (stop - start) // pieces
            for k in range(pieces):
                out[k * rows : (k + 1) * rows, :] = total[:, start + k * stride : start + k * stride + width]
        else:
            pieces = stop[0]
            height = rows * pieces
            each = out.shape[0] // height
            value = jnp.zeros((1, out.shape[0]), F32)
            for k in range(pieces):
                block = total[:, start + k * stop[1] : start + k * stop[1] + SMALL]
                line = lax.broadcasted_iota(jnp.int32, (rows, out.shape[0]), 0) + k * rows
                lane = lax.broadcasted_iota(jnp.int32, (rows, out.shape[0]), 1)
                for j in range(each):
                    at = stop[2] + j
                    found = jnp.where(lane == line * each + j, block[:, at : at + 1], 0.0)
                    value = value + jnp.sum(found, 0, keepdims=True)
            out[...] = value.reshape(out.shape[0])


def finish(arrived, plan):
    vmem = pl.BlockSpec(memory_space=pltpu.VMEM)
    return pl.pallas_call(
        functools.partial(finish_kernel, tuple(one[:3] for one in plan), len(arrived)),
        out_shape=tuple(jax.ShapeDtypeStruct(shape, F32) for _, _, _, shape in plan),
        in_specs=[vmem] * len(arrived),
        out_specs=(vmem,) * len(plan),
        compiler_params=pltpu.CompilerParams(vmem_limit_bytes=VMEM_LIMIT),
    )(*arrived)


def tie(values, after):
    return lax.optimization_barrier((values, after))[0]


def body(
    char_inputs,
    language_ids,
    char_counts,
    row_lengths,
    cotangent,
    language_table,
    char_gain_one,
    char_bias_one,
    char_inward,
    char_outward,
    char_gain_two,
    char_bias_two,
    char_expand,
    char_expand_bias,
    char_reduce,
    char_reduce_bias,
    char_to_word,
    char_to_word_bias,
    word_gain_one,
    word_bias_one,
    word_inward,
    word_outward,
    word_gain_two,
    word_bias_two,
    word_expand,
    word_expand_bias,
    word_reduce,
    word_reduce_bias,
):
    rows, local, slots, width = char_inputs.shape
    words = rows * local
    langs = language_table.shape[0]
    wide = word_inward.shape[1] // 3
    deep, share = lax.axis_size("dp"), lax.axis_size("fsdp")
    devices = deep * share
    members = share // rows
    axes = ("dp", "fsdp")
    at_deep, at_share = lax.axis_index("dp"), lax.axis_index("fsdp")

    def swap(values, mask):
        return lax.ppermute(values, axes, [(k, k ^ mask) for k in range(devices)])

    far, low = deep // 2, share // 2
    near = 2 * low
    far_masks = [m * 2 * share for m in range(far)]
    near_masks = [(m // low) * share + (m % low) * 2 for m in range(near)]
    core_masks = [0, 1]
    counts_of = (far, near)
    top = members
    my_row = at_share // members
    index = (at_deep * share + at_share).reshape(1)

    def swaps(values, masks):
        return [values] + [swap(values, m) for m in masks[1:]]

    def together(pieces, rows):
        return jnp.stack(pieces).reshape(-1, rows, pieces[0].shape[-1])

    order = [c | n | f for c in core_masks for n in near_masks for f in far_masks]

    char_piece = char_shard(
        language_table.T,
        char_inward,
        char_outward,
        char_expand,
        char_reduce,
        (char_gain_one, char_bias_one, char_gain_two, char_bias_two, char_reduce_bias, char_expand_bias),
    )
    each = char_piece.shape[0]
    counts = tie(char_counts, char_piece)
    offs, first, rows_of, blocks, place = offsets((share, members), counts, row_lengths, index, slots)
    char_piece = together(tie(swaps(char_piece, far_masks), offs), each)
    packed, bias, hot, inverse = pack(
        tie(counts, char_piece), offs, first, blocks, char_inputs.reshape(words, slots, width)
    )
    char_piece = together(swaps(char_piece, near_masks), each)
    char_full = assemble(order, index, swaps(tie(char_piece, packed), core_masks))
    word_full = lax.all_gather(
        word_shard(
            word_inward,
            word_outward,
            word_expand,
            word_reduce,
            char_to_word,
            (
                word_gain_one,
                word_bias_one,
                word_gain_two,
                word_bias_two,
                word_reduce_bias,
                char_to_word_bias,
                word_expand_bias,
            ),
        ),
        axes,
        axis=0,
        tiled=True,
    )

    qkv, soft, mixed, after, cotangent_sent = char_attend(
        langs, blocks, rows_of, language_ids, place, packed, bias, char_full, cotangent
    )
    cotangent_other = swap(cotangent_sent, top)
    act, slope, pooled_kept, pooled_sent = char_ffn(
        langs, blocks, first, place, after, hot, inverse, char_full
    )
    cotangent_other, pooled_kept, pooled_sent = lax.optimization_barrier(
        (cotangent_other, pooled_kept, pooled_sent)
    )
    pooled_other = swap(pooled_sent, top)
    pieces = []
    for m in range(members):
        pieces += [swap(pooled_kept, m), swap(pooled_other, m)] if m else [pooled_kept, pooled_other]
    words_both, words_sent, word_after_grad, word_normed, word_in, word_kept, word_sent, *others = word_part(
        counts_of, place, pieces, word_full, cotangent, cotangent_other
    )
    query_grad, word_sums, *pair_grads = others
    pairs = [pair_grads[0]] + [swap(pair_grads[m], m) for m in range(1, members)]
    word_sent, words_sent, pairs = lax.optimization_barrier((word_sent, words_sent, pairs))
    words_other = swap(words_sent, top)
    word_arrived = [word_kept, swap(word_sent, 1)]
    up_kept, up_sent, to_word_grad, inward_kept, inward_sent = word_end(
        counts_of,
        place,
        pooled_kept,
        pooled_other,
        word_full,
        query_grad,
        word_normed,
        word_in,
        word_after_grad,
        word_sums,
        pairs,
    )
    up_other = swap(up_sent, top)

    def phase(parts, masks):
        return [parts[0]] + [swap(parts[m], masks[m]) for m in range(1, len(masks))]

    word_parts = add_and_cut(word_arrived, near, NEAR, place)
    word_parts, words_other = lax.optimization_barrier((word_parts, words_other))
    up_kept = tie(up_kept, word_parts)
    after_grad, feed_kept, feed_sent, char_sums = char_ffn_back(
        (langs, counts_of),
        blocks,
        first,
        place,
        after,
        hot,
        act,
        slope,
        inverse,
        up_kept,
        up_other,
        char_full,
        to_word_grad,
        (inward_kept, inward_sent),
    )
    word_parts = add_and_cut(tie(phase(word_parts, near_masks), feed_kept), far, FAR, place)
    feed_sent = tie(feed_sent, word_parts)
    late_parts = add_and_cut([feed_kept, swap(feed_sent, 1)], near, NEAR, place)
    after_grad = tie(after_grad, (word_parts, late_parts))
    operands = (packed, qkv, soft, mixed, after_grad, char_full, char_sums)
    *start_grad, attend_kept, attend_sent = char_attend_back(
        (langs, counts_of), blocks, rows_of, language_ids, place, *operands
    )
    arrived_words, arrived_late, attend_kept, attend_sent = lax.optimization_barrier(
        (phase(word_parts, far_masks), phase(late_parts, near_masks), attend_kept, attend_sent)
    )
    late_parts = add_and_cut(arrived_late, far, FAR, place)
    hidden, wide_hidden = FOLD * width, FOLD * wide
    grad_word_expand, grad_word_reduce, grad_word_outward = finish(
        arrived_words,
        (
            ("plain", 0, wide_hidden, word_expand.shape),
            ("folded", wide_hidden, 2 * wide_hidden, word_reduce.shape),
            ("plain", 2 * wide_hidden, 2 * wide_hidden + wide, word_outward.shape),
        ),
    )
    words_out = lax.dynamic_update_index_in_dim(words_both, words_other, 1 - my_row, 0)
    earlier = (words_out, grad_word_expand, grad_word_reduce, grad_word_outward)
    arrived, earlier, late_parts = lax.optimization_barrier(
        ([attend_kept, swap(attend_sent, 1)], earlier, late_parts)
    )
    attend_parts = add_and_cut(arrived, near, NEAR, place)
    char_input_grad = unpack(offs, char_counts, tie(start_grad, attend_parts), slots)
    arrived, arrived_late, char_input_grad = lax.optimization_barrier(
        (phase(attend_parts, near_masks), phase(late_parts, far_masks), char_input_grad)
    )
    attend_parts = add_and_cut(arrived, far, FAR, place)
    char_input_grad = unpack(offs, char_counts, tie(start_grad, attend_parts), slots, char_input_grad)
    arrived, arrived_late, char_input_grad = lax.optimization_barrier(
        (phase(attend_parts, far_masks), arrived_late, char_input_grad)
    )
    at_inward = 2 * hidden + wide
    stop = at_inward + (3 * wide + SMALL) * (wide // width)
    grad_expand, grad_reduce, grad_to_word, grad_word_inward, *word_vectors = finish(
        arrived_late,
        (
            ("plain", 0, hidden, char_expand.shape),
            ("folded", hidden, 2 * hidden, char_reduce.shape),
            ("plain", 2 * hidden, at_inward, char_to_word.shape),
            ("halves", at_inward, stop, word_inward.shape),
        )
        + tuple(
            ("vector", at_inward + 3 * wide, (wide // width, 3 * wide + SMALL, at), vector.shape)
            for at, vector in (
                (0, word_gain_one),
                (1, word_bias_one),
                (2, word_gain_two),
                (3, word_bias_two),
                (4, word_reduce_bias),
                (5, char_to_word_bias),
                (6, word_expand_bias),
            )
        ),
    )
    grad_inward, grad_outward, grad_table, *char_vectors = finish(
        arrived,
        (
            ("plain", 0, 3 * width, char_inward.shape),
            ("plain", 3 * width, 4 * width, char_outward.shape),
            ("plain", 4 * width, 4 * width + langs, (char_inward.shape[0], langs)),
        )
        + tuple(
            ("vector", 4 * width, (1, 0, langs + at), vector.shape)
            for at, vector in (
                (0, char_gain_one),
                (1, char_bias_one),
                (2, char_gain_two),
                (3, char_bias_two),
                (4, char_reduce_bias),
                (5, char_expand_bias),
            )
        ),
    )
    words_out, grad_word_expand, grad_word_reduce, grad_word_outward = earlier

    gain_one, bias_one, gain_two, bias_two, reduce_bias, expand_bias = char_vectors
    wide_gain_one, wide_bias_one, wide_gain_two, wide_bias_two, wide_reduce_bias = word_vectors[:5]
    to_word_bias, wide_expand_bias = word_vectors[5:]
    return (
        words_out,
        char_input_grad.reshape(char_inputs.shape),
        grad_table.T,
        gain_one,
        bias_one,
        grad_inward,
        grad_outward,
        gain_two,
        bias_two,
        grad_expand,
        expand_bias,
        grad_reduce,
        reduce_bias,
        grad_to_word,
        to_word_bias,
        wide_gain_one,
        wide_bias_one,
        grad_word_inward,
        grad_word_outward,
        wide_gain_two,
        wide_bias_two,
        grad_word_expand,
        wide_expand_bias,
        grad_word_reduce,
        wide_reduce_bias,
    )


def solution(mesh):
    both = ("dp", "fsdp")
    vector, matrix = P(both), P(both, None)
    weights = (
        (P(None, both), vector, vector, matrix, matrix, vector, vector)
        + (matrix, vector, matrix, vector, matrix, vector)
        + (vector, vector, matrix, matrix, vector, vector, matrix, vector, matrix, vector)
    )
    in_specs = (
        P("dp", "fsdp", None, None),
        P("dp"),
        P("dp", "fsdp"),
        P("dp"),
        P("dp", "fsdp", None),
    ) + weights
    out_specs = (P("dp", "fsdp", None), P("dp", "fsdp", None, None)) + weights
    return jax.shard_map(body, mesh=mesh, in_specs=in_specs, out_specs=out_specs, check_vma=False)
```

```python
import functools

import jax
import jax.numpy as jnp
from jax import lax
from jax.experimental import pallas as pl
from jax.experimental.pallas import tpu as pltpu
from jax.sharding import PartitionSpec as P

BF = jnp.bfloat16
F32 = jnp.float32
EPS = 1e-05
MASKED = -1e30
CHEADS = 4
WHEADS = 8
HEAD = 64
SCALE = HEAD ** (-0.5)
GROUP = 128
GROUP_BITS = 7
BLOCK = 1024
SPLIT = BLOCK // GROUP
FOLD = 4
SMALL = 128
GELU_A = 0.7978845608028654
GELU_B = 0.044715
MIB = 1024 * 1024
VMEM_LIMIT = 64 * MIB - 65536
MEMBER, ROW, LENGTH, CORE, NEAR, FAR = range(6)


def whole_to_word(held, devices):
    tall, width = held.shape
    rows = tall // 2
    each = rows // devices
    line = lax.broadcasted_iota(jnp.int32, (rows, tall), 0)
    lane = lax.broadcasted_iota(jnp.int32, (rows, tall), 1)
    source = lax.div(line, each) * (2 * each) + lax.rem(line, each)
    halves = [dot((lane == source + k * each).astype(F32).astype(BF), held[...]).astype(BF) for k in range(2)]
    return jnp.concatenate(halves, 1)


def columns(array, width, start):
    return array, pl.BlockSpec((array.shape[0], width), lambda *_: (0, start // width))


def dot(a, b):
    return jnp.dot(a, b, preferred_element_type=F32)


def dot_t(a, b):
    return lax.dot_general(a, b, (((1,), (1,)), ((), ())), preferred_element_type=F32)


def t_dot(a, b):
    return dot(a.T, b)


def norm_parts(hidden):
    centred = hidden - jnp.mean(hidden, -1, keepdims=True)
    spread = lax.rsqrt(jnp.mean(centred * centred, -1, keepdims=True) + EPS)
    return centred * spread, spread


def norm_back(unit, spread, gained):
    return (
        gained
        - jnp.mean(gained, -1, keepdims=True)
        - unit * jnp.mean(gained * unit, -1, keepdims=True)
    ) * spread


def gelu_both(pre):
    square = pre * pre
    turn = jnp.tanh(pre * (GELU_A + (GELU_A * GELU_B) * square))
    half = 0.5 + 0.5 * turn
    slope = half + pre * half * (1.0 - turn) * (GELU_A + (3.0 * GELU_A * GELU_B) * square)
    return pre * half, slope


def fold_rows(values):
    rows, width = values.shape
    return jnp.sum(values.reshape(rows // 8, 8, width), 0)


def head_masks(width, heads):
    lanes = lax.broadcasted_iota(jnp.int32, (1, width), 1) // HEAD
    return [(lanes == h).astype(F32).astype(BF) for h in range(heads)]


def run_blocks(step, begin, end, inputs, outputs):
    def one(*refs):
        step(begin + pl.program_id(0), *refs)

    def spec(ref):
        return pl.BlockSpec((BLOCK, ref.shape[1]), lambda i: (begin + i, 0))

    pltpu.emit_pipeline(
        one,
        grid=(end - begin,),
        in_specs=[spec(ref) for ref in inputs],
        out_specs=[spec(ref) for ref in outputs],
    )(*inputs, *outputs)


def streamed(kernel, scalars, streams, fixed, stream_outs, fixed_outs, scratch, cost, aliases=None):
    hbm = pl.BlockSpec(memory_space=pltpu.HBM)
    fixed = [one if isinstance(one, tuple) else (one, full(one.shape)) for one in fixed]
    return pl.pallas_call(
        kernel,
        out_shape=tuple(jax.ShapeDtypeStruct(*out) for out in tuple(stream_outs) + tuple(fixed_outs)),
        grid_spec=pltpu.PrefetchScalarGridSpec(
            num_scalar_prefetch=len(scalars),
            grid=(1,),
            in_specs=[hbm] * len(streams) + [spec for _, spec in fixed],
            out_specs=(hbm,) * len(stream_outs) + tuple(full(shape) for shape, _ in fixed_outs),
            scratch_shapes=[pltpu.VMEM(*one) if isinstance(one, tuple) else one for one in scratch],
        ),
        input_output_aliases=aliases or {},
        compiler_params=pltpu.CompilerParams(vmem_limit_bytes=VMEM_LIMIT),
        cost_estimate=cost,
    )(*scalars, *streams, *(one for one, _ in fixed))


def full(shape):
    return pl.BlockSpec(shape, lambda *_: (0,) * len(shape))


def offsets_kernel(layout, counts, lengths, index, offs, first, rows_of, blocks, place_out):
    share, members = layout
    rows, per_row = counts.shape
    deep, part = lax.div(index[0], share), lax.rem(index[0], share)
    my_row = lax.div(part, members)
    place_out[MEMBER] = lax.rem(part, members)
    place_out[ROW] = my_row
    place_out[LENGTH] = lengths[my_row]
    place_out[CORE] = lax.rem(part, 2)
    place_out[NEAR] = lax.rem(deep, 2) * (share // 2) + lax.div(part, 2)
    place_out[FAR] = lax.div(deep, 2)

    def clear(g, carry):
        first[g] = 0
        rows_of[g] = 0
        return carry

    lax.fori_loop(0, first.shape[0], clear, 0, unroll=True)
    spare = first.shape[0] - 1

    def place(row, k, at):
        live = counts[row, k]
        w = row * per_row + k
        inside = at & (GROUP - 1)
        at = jnp.where(inside + live > GROUP, at - inside + GROUP, at)
        group = jnp.where((at & (GROUP - 1)) == 0, at >> GROUP_BITS, spare)
        first[group] = w
        rows_of[group] = row
        offs[w] = at
        return at + live

    at = 0
    for row in range(rows):
        at = lax.fori_loop(0, per_row, functools.partial(place, row), at, unroll=8)
        at = ((at + (GROUP - 1)) >> GROUP_BITS) << GROUP_BITS
    blocks[0] = lax.div(at + (BLOCK - 1), BLOCK)


def group_count(words, slots, per_row):
    groups = (words * slots) // (GROUP - slots + 1) + 1 + words // per_row
    return -(-groups // SPLIT) * SPLIT


def offsets(layout, counts, lengths, index, slots):
    rows, per_row = counts.shape
    words = rows * per_row
    groups = group_count(words, slots, per_row)
    smem = pl.BlockSpec(memory_space=pltpu.SMEM)
    sizes = (words, groups + 1, groups + 1, 1, 6)
    return pl.pallas_call(
        functools.partial(offsets_kernel, layout),
        out_shape=tuple(jax.ShapeDtypeStruct((size,), jnp.int32) for size in sizes),
        in_specs=[smem] * 3,
        out_specs=(smem,) * 5,
        cost_estimate=pl.CostEstimate(flops=words * 4000, bytes_accessed=12 * MIB, transcendentals=0),
    )(counts, lengths, index)


def pack_kernel(
    counts, offs, first, blocks, chars, packed_all, bias_all, hot_all, inverse, tags, *wide
):
    slots = chars.shape[1]
    rows, per_row = counts.shape
    slot = lax.broadcasted_iota(jnp.int32, (slots, GROUP), 0)

    def clear_rows(k, carry):
        there = pl.ds(pl.multiple_of(k * GROUP, GROUP), GROUP)
        for part in wide:
            part[there, :] = jnp.zeros((GROUP, GROUP), F32)
        tags[there, :] = jnp.full((GROUP, GROUP), -1.0, F32)
        return carry

    lax.fori_loop(0, blocks[0] * SPLIT, clear_rows, 0)

    def put(row, n, carry):
        w = row * per_row + n
        at = offs[w]
        for k, part in enumerate(wide):
            part[pl.ds(at, slots), :] = chars[w, :, k * GROUP : (k + 1) * GROUP].astype(F32)
        tags[pl.ds(at, slots), :] = jnp.where(slot < counts[row, n], w.astype(F32), -1.0)
        inverse[pl.ds(w, 1), :] = 1.0 / jnp.full((1, GROUP), counts[row, n], jnp.int32).astype(F32)
        return carry

    for row in range(rows):
        lax.fori_loop(0, per_row, functools.partial(put, row), 0, unroll=8)
    lane = lax.broadcasted_iota(jnp.int32, (GROUP, GROUP), 1).astype(F32)

    def step(i, packed, bias, hot):
        for g in range(SPLIT):
            here = slice(g * GROUP, (g + 1) * GROUP)
            there = pl.ds(pl.multiple_of((i * SPLIT + g) * GROUP, GROUP), GROUP)
            tag = tags[there, :]
            bias[here, :] = jnp.where(tag == tag.T, 0.0, MASKED).astype(BF)
            hot[here, :] = (tag - first[i * SPLIT + g].astype(F32) == lane).astype(F32).astype(BF)
            for k, part in enumerate(wide):
                packed[here, k * GROUP : (k + 1) * GROUP] = part[there, :].astype(BF)

    run_blocks(step, 0, blocks[0], (), (packed_all, bias_all, hot_all))


def pack(counts, offs, first, blocks, chars):
    words, slots, width = chars.shape
    rows = group_count(words, slots, counts.shape[1]) * GROUP
    return streamed(
        pack_kernel,
        (counts, offs, first, blocks),
        (),
        (chars,),
        (((rows, width), BF), ((rows, GROUP), BF), ((rows, GROUP), BF)),
        (((words, GROUP), F32),),
        (((rows + GROUP, GROUP), F32),) * (1 + width // GROUP),
        pl.CostEstimate(flops=rows * width * 4, bytes_accessed=rows * width * 10, transcendentals=0),
    )


def unpack_kernel(row, halves, offs, counts, *refs):
    packed = refs[:halves]
    out, held, arrived = refs[-2 - halves], refs[-1 - halves : -1], refs[-1]
    slots = out.shape[1]
    count = counts.shape[1]
    begin = row * count
    here = pl.program_id(0) * out.shape[0]
    slot = lax.broadcasted_iota(jnp.int32, (slots, GROUP), 0)

    @pl.when(pl.program_id(0) == 0)
    def _():
        low = lax.div(offs[begin], BLOCK)
        high = lax.div(offs[begin + count - 1] + (slots + BLOCK - 1), BLOCK)

        def copy(k, j):
            there = pl.ds(pl.multiple_of(k * BLOCK, BLOCK), BLOCK)
            return pltpu.make_async_copy(packed[j].at[there, :], held[j].at[there, :], arrived.at[j, k])

        def fetch(k, carry):
            for j in range(halves):
                copy(k, j).start()
            return carry

        def await_one(k, carry):
            for j in range(halves):
                copy(k, j).wait()
            return carry

        lax.fori_loop(low, high, fetch, 0)
        lax.fori_loop(low, high, await_one, 0)

    def take(k, carry):
        n = here + k
        for j, part in enumerate(held):
            rows = part[pl.ds(offs[begin + n], slots), :]
            out[k, :, j * GROUP : (j + 1) * GROUP] = jnp.where(slot < counts[row, n], rows, 0.0)
        return carry

    lax.fori_loop(0, out.shape[0], take, 0, unroll=8)


def unpack(offs, counts, packed, slots, before=None):
    words = counts.size
    halves = len(packed)
    width = halves * GROUP
    step = words // 4
    row = 0 if before is None else 1
    extra = [] if before is None else [before]
    hbm = pl.BlockSpec(memory_space=pltpu.HBM)
    return pl.pallas_call(
        functools.partial(unpack_kernel, row, halves),
        out_shape=jax.ShapeDtypeStruct((words, slots, width), F32),
        grid_spec=pltpu.PrefetchScalarGridSpec(
            num_scalar_prefetch=2,
            grid=(2,),
            in_specs=[hbm] * (halves + len(extra)),
            out_specs=pl.BlockSpec((step, slots, width), lambda i, *_: (2 * row + i, 0, 0)),
            scratch_shapes=[pltpu.VMEM(part.shape, F32) for part in packed]
            + [pltpu.SemaphoreType.DMA((halves, packed[0].shape[0] // BLOCK))],
        ),
        input_output_aliases={2 + halves: 0} if extra else {},
        compiler_params=pltpu.CompilerParams(vmem_limit_bytes=VMEM_LIMIT),
        cost_estimate=pl.CostEstimate(
            flops=words * slots * width, bytes_accessed=words * slots * width * 4, transcendentals=0
        ),
    )(offs, counts, *packed, *extra)


def with_language(i, rows_of, ids, packed, small_rows):
    parts = []
    for g in range(SPLIT):
        row = small_rows[pl.ds(ids[rows_of[i * SPLIT + g]], 1), :]
        parts.append(packed[g * GROUP : (g + 1) * GROUP, :].astype(F32) + row)
    return jnp.concatenate(parts, 0)


def both_heads(values, lower):
    wide = values.astype(F32)
    return jnp.concatenate([jnp.where(lower, wide, 0.0), jnp.where(lower, 0.0, wide)], 0).astype(BF)


def pick_heads(stacked, lower):
    rows = stacked.shape[0] // 2
    return jnp.where(lower, stacked[:rows], stacked[rows:])


def char_attend_kernel(
    langs,
    blocks,
    rows_of,
    ids,
    place,
    packed_all,
    bias_all,
    cotangent,
    weights,
    small,
    qkv_all,
    soft_all,
    mixed_all,
    after_all,
    cotangent_out,
    small_rows,
    sent,
):
    copy = pltpu.make_async_copy(cotangent.at[1 - place[ROW]], cotangent_out, sent)
    copy.start()
    width = packed_all.shape[1]
    small_rows[...] = small[...].astype(F32).T

    def step(i, packed, bias, qkv_out, soft_out, mixed_out, after_out):
        start = with_language(i, rows_of, ids, packed, small_rows)
        unit, _ = norm_parts(start)
        normed = (unit * small_rows[langs : langs + 1, :] + small_rows[langs + 1 : langs + 2, :]).astype(BF)
        qkv_out[...] = dot(normed, weights[:, : 3 * width]).astype(BF)
        lower = lax.broadcasted_iota(jnp.int32, (GROUP, GROUP), 1) < HEAD
        places = [(slice(g * GROUP, (g + 1) * GROUP), t) for g in range(SPLIT) for t in range(CHEADS // 2)]
        scores = []
        for here, t in places:
            tile = slice(t * GROUP, (t + 1) * GROUP)
            keys = both_heads(qkv_out[here, width + t * GROUP : width + (t + 1) * GROUP], lower)
            scores.append(dot_t(keys, qkv_out[here, tile]))
        softs = []
        for (here, t), score in zip(places, scores):
            blocked = bias[here, :].astype(F32)
            for h in range(2):
                one = score[h * GROUP : (h + 1) * GROUP] * SCALE + blocked
                one = jnp.exp(one - jnp.max(one, 0, keepdims=True))
                one = (one * (1.0 / jnp.sum(one, 0, keepdims=True))).astype(BF)
                soft_out[here, (2 * t + h) * GROUP : (2 * t + h + 1) * GROUP] = one
                softs.append(one)
        for k, (here, t) in enumerate(places):
            values = qkv_out[here, 2 * width + t * GROUP : 2 * width + (t + 1) * GROUP]
            mixed = dot(jnp.concatenate([softs[2 * k].T, softs[2 * k + 1].T], 0), values)
            mixed_out[here, t * GROUP : (t + 1) * GROUP] = pick_heads(mixed, lower).astype(BF)
        after_out[...] = start + dot(mixed_out[...], weights[:, 3 * width : 4 * width])

    run_blocks(step, 0, blocks[0], (packed_all, bias_all), (qkv_all, soft_all, mixed_all, after_all))
    copy.wait()


def char_attend(langs, blocks, rows_of, ids, place, packed, bias, weights, cotangent):
    rows, width = packed.shape
    at_small = weights.shape[1] - SMALL
    return streamed(
        functools.partial(char_attend_kernel, langs),
        (blocks, rows_of, ids, place),
        (packed, bias, cotangent),
        (columns(weights, 4 * width, 0), columns(weights, SMALL, at_small)),
        (
            ((rows, 3 * width), BF),
            ((rows, CHEADS * GROUP), BF),
            ((rows, width), BF),
            ((rows, width), F32),
            (cotangent.shape[1:], BF),
        ),
        (),
        (((SMALL, width), F32), pltpu.SemaphoreType.DMA),
        pl.CostEstimate(
            flops=rows * width * width * 12, bytes_accessed=rows * width * 12, transcendentals=rows * 512
        ),
    )


def char_ffn_kernel(
    langs,
    blocks,
    first,
    place,
    after_all,
    hot_all,
    inverse,
    expand,
    reduced,
    small,
    act_all,
    slope_all,
    kept_out,
    sent_out,
    small_rows,
    *total,
):
    width = after_all.shape[1]
    small_rows[...] = small[...].astype(F32).T
    for part in total:
        part[...] = jnp.zeros_like(part)

    def step(i, after, hot, act_out, slope_out):
        unit, _ = norm_parts(after[...])
        normed = (unit * small_rows[langs + 2 : langs + 3, :] + small_rows[langs + 3 : langs + 4, :]).astype(BF)
        out = after[...] + small_rows[langs + 4 : langs + 5, :]
        for j in range(FOLD):
            cols = slice(j * width, (j + 1) * width)
            pre = dot(normed, expand[:, cols]) + small_rows[langs + 5 + j : langs + 6 + j, :]
            act, slope = gelu_both(pre)
            act = act.astype(BF)
            act_out[:, cols] = act
            slope_out[:, cols] = slope.astype(BF)
            out = out + dot(act, reduced[:, cols])
        out = out.astype(BF)
        for g in range(SPLIT):
            here = slice(g * GROUP, (g + 1) * GROUP)
            words = pl.ds(first[i * SPLIT + g], GROUP)
            found = t_dot(hot[here, :], out[here, :])
            for k, part in enumerate(total):
                part[words, :] = part[words, :] + found[:, k * GROUP : (k + 1) * GROUP]

    run_blocks(step, 0, blocks[0], (after_all, hot_all), (act_all, slope_all))
    local = kept_out.shape[0]
    for out_ref, row in ((kept_out, place[ROW]), (sent_out, 1 - place[ROW])):
        there = pl.ds(pl.multiple_of(row * local, local), local)
        for k, part in enumerate(total):
            out_ref[:, k * GROUP : (k + 1) * GROUP] = (part[there, :] * inverse[there, :]).astype(BF)


def feed_columns(weights, width):
    hidden = FOLD * width
    return (
        columns(weights, hidden, 4 * width),
        columns(weights, hidden, 4 * width + hidden),
        columns(weights, SMALL, weights.shape[1] - SMALL),
    )


def char_ffn(langs, blocks, first, place, after, hot, inverse, weights):
    rows, width = after.shape
    words = inverse.shape[0]
    hidden = FOLD * width
    return streamed(
        functools.partial(char_ffn_kernel, langs),
        (blocks, first, place),
        (after, hot),
        (inverse, *feed_columns(weights, width)),
        (((rows, hidden), BF), ((rows, hidden), BF)),
        (((words // 2, width), BF), ((words // 2, width), BF)),
        (((SMALL, width), F32),) + (((words + GROUP, GROUP), F32),) * (width // GROUP),
        pl.CostEstimate(
            flops=rows * width * width * 16, bytes_accessed=rows * width * 20, transcendentals=rows * 1024
        ),
    )


def sorted_rows(core, counts, rows, cuts=1):
    far, near = counts
    each = rows // (2 * far * near)
    some = each // cuts
    low = near // 2
    line = lax.broadcasted_iota(jnp.int32, (rows, rows), 0)
    piece = lax.div(line, rows // (2 * cuts))
    line = lax.rem(line, rows // (2 * cuts))
    which = lax.rem(piece, cuts)
    core = jnp.bitwise_xor(core, lax.div(piece, cuts))
    inner = lax.rem(line, some)
    part = lax.div(line, some)
    at_far, at_near = lax.rem(part, far), lax.div(part, far)
    device = ((at_far * 2 + lax.div(at_near, low)) * low + lax.rem(at_near, low)) * 2 + core
    source = device * each + which * some + inner
    return (source == lax.broadcasted_iota(jnp.int32, source.shape, 1)).astype(F32).astype(BF)


def folding(back):
    size = FOLD * HEAD
    unit = lax.broadcasted_iota(jnp.int32, (size, size), 1 if back else 0)
    held = lax.broadcasted_iota(jnp.int32, (size, size), 0 if back else 1)
    return (held == (unit & (FOLD - 1)) * HEAD + lax.div(unit, FOLD)).astype(F32).astype(BF)


def unfold_into(out, folded, width):
    size = FOLD * HEAD
    matrix = folding(True)
    for m in range(width // HEAD):
        near = [folded[:, j * width + m * HEAD : j * width + (m + 1) * HEAD] for j in range(FOLD)]
        out[:, m * size : (m + 1) * size] = dot(jnp.concatenate(near, 1), matrix).astype(BF)


def char_ffn_back_kernel(
    settings,
    blocks,
    first,
    place,
    after_all,
    hot_all,
    act_all,
    slope_all,
    inverse,
    up_kept,
    up_sent,
    expand,
    reduced,
    small,
    grad_to_word,
    riding_kept,
    riding_sent,
    grad_after_all,
    kept_out,
    sent_out,
    sums,
    small_rows,
    grad_expand,
    grad_reduce,
    up_rows,
    grads,
    *spread_up,
):
    langs, counts = settings
    width = after_all.shape[1]
    hidden = FOLD * width
    local = up_kept.shape[0]
    small_rows[...] = small[...].astype(F32).T
    for up_in, row in ((up_kept, place[ROW]), (up_sent, 1 - place[ROW])):
        there = pl.ds(pl.multiple_of(row * local, local), local)
        for k, part in enumerate(spread_up):
            cols = slice(k * GROUP, (k + 1) * GROUP)
            part[there, :] = up_in[:, cols].astype(F32) * inverse[there, :]
    for part in spread_up:
        part[2 * local :, :] = jnp.zeros((GROUP, GROUP), F32)
    grad_expand[...] = jnp.zeros_like(grad_expand)
    grad_reduce[...] = jnp.zeros_like(grad_reduce)
    sums[...] = jnp.zeros_like(sums)

    def step(i, after, hot, act, slope, grad_after):
        for g in range(SPLIT):
            here = slice(g * GROUP, (g + 1) * GROUP)
            for k, part in enumerate(spread_up):
                words_here = part[pl.ds(first[i * SPLIT + g], GROUP), :].astype(BF)
                up_rows[here, k * GROUP : (k + 1) * GROUP] = dot(hot[here, :], words_here).astype(BF)
        up = up_rows[...]
        unit, spread = norm_parts(after[...])
        gain = small_rows[langs + 2 : langs + 3, :]
        normed = (unit * gain + small_rows[langs + 3 : langs + 4, :]).astype(BF)
        grad_normed = jnp.zeros((BLOCK, width), F32)
        parts = [slice(j * width, (j + 1) * width) for j in range(FOLD)]
        grad_acts = [
            dot_t(up, reduced[:, j * width : (j + 1) * width]) for j in range(FOLD)
        ]
        grad_pres = []
        for j, cols in enumerate(parts):
            grad_pre = grad_acts[j] * slope[:, cols].astype(F32)
            sums[8 * j : 8 * j + 8, :] += fold_rows(grad_pre)
            grad_pres.append(grad_pre.astype(BF))
        for j, grad_pre in enumerate(grad_pres):
            grad_normed = grad_normed + dot_t(grad_pre, expand[:, j * width : (j + 1) * width])
        turned = normed.T
        for cols, grad_pre in zip(parts, grad_pres):
            grad_expand[:, cols] += dot(turned, grad_pre)
        turned = up.T
        for cols in parts:
            grad_reduce[:, cols] += dot(turned, act[:, cols])
        up_wide = up.astype(F32)
        sums[32:40, :] += fold_rows(grad_normed * unit)
        sums[40:48, :] += fold_rows(grad_normed)
        sums[48:56, :] += fold_rows(up_wide)
        grad_after[...] = up_wide + norm_back(unit, spread, grad_normed * gain)

    run_blocks(step, 0, blocks[0], (after_all, hot_all, act_all, slope_all), (grad_after_all,))
    unfold_into(grads.at[:, :hidden], grad_expand[...].astype(BF), width)
    for j in range(FOLD):
        grads[:, hidden + j * width : hidden + (j + 1) * width] = (
            grad_reduce[:, j * width : (j + 1) * width].T.astype(BF)
        )
    grads[:, 2 * hidden :] = grad_to_word[...]
    own = grads.shape[1]
    ranked = dot(sorted_rows(place[CORE], counts, width), grads[...]).astype(BF)
    kept_out[:, :own] = ranked[: width // 2]
    sent_out[:, :own] = ranked[width // 2 :]
    kept_out[:, own:] = riding_kept[...]
    sent_out[:, own:] = riding_sent[...]


def char_ffn_back(
    settings,
    blocks,
    first,
    place,
    after,
    hot,
    act,
    slope,
    inverse,
    up_kept,
    up_sent,
    weights,
    grad_to_word,
    riding,
):
    rows, width = after.shape
    words = inverse.shape[0]
    hidden = FOLD * width
    span = 2 * hidden + grad_to_word.shape[1]
    return streamed(
        functools.partial(char_ffn_back_kernel, settings),
        (blocks, first, place),
        (after, hot, act, slope),
        (inverse, up_kept, up_sent, *feed_columns(weights, width), grad_to_word, *riding),
        (((rows, width), F32),),
        (((width // 2, span + riding[0].shape[1]), BF),) * 2 + (((64, width), F32),),
        (
            ((SMALL, width), F32),
            ((width, hidden), F32),
            ((width, hidden), F32),
            ((BLOCK, width), BF),
            ((width, span), BF),
        )
        + (((words + GROUP, GROUP), F32),) * (width // GROUP),
        pl.CostEstimate(
            flops=rows * width * width * 32, bytes_accessed=rows * width * 20, transcendentals=0
        ),
    )


def char_attend_back_kernel(settings, blocks, rows_of, ids, place, *refs):
    langs, counts = settings
    streams, refs = refs[:5], refs[5:]
    width = streams[0].shape[1]
    halves = width // GROUP
    (weights, small, sums_in), refs = refs[:3], refs[3:]
    start_all, refs = refs[:halves], refs[halves:]
    kept_out, sent_out, small_rows, grad_mixed, grad_qkv, grad_in, lines, grads = refs
    grad_in[...] = jnp.zeros_like(grad_in)
    lines[...] = jnp.zeros_like(lines)
    small_rows[...] = small[...].astype(F32).T

    def step(i, packed, qkv, soft, mixed, grad_after, *grad_start):
        start = with_language(i, rows_of, ids, packed, small_rows)
        unit, spread = norm_parts(start)
        gain = small_rows[langs : langs + 1, :]
        normed = (unit * gain + small_rows[langs + 1 : langs + 2, :]).astype(BF)
        after_low = grad_after[...].astype(BF)
        grad_in[:, 3 * width :] += t_dot(mixed[...], after_low)
        grad_mixed[...] = dot_t(after_low, weights[:, 3 * width : 4 * width]).astype(BF)
        lower = lax.broadcasted_iota(jnp.int32, (GROUP, GROUP), 1) < HEAD
        places = [(slice(g * GROUP, (g + 1) * GROUP), t) for g in range(SPLIT) for t in range(CHEADS // 2)]

        def tile_of(values, which, k):
            here, t = places[k]
            return values[here, which * width + t * GROUP : which * width + (t + 1) * GROUP]

        every = range(len(places))
        lows = [both_heads(tile_of(grad_mixed, 0, k), lower) for k in every]
        grad_softs = [dot_t(tile_of(qkv, 2, k), lows[k]) for k in every]
        weights_of = [soft[here, 2 * t * GROUP : (2 * t + 2) * GROUP] for here, t in places]
        ones = []
        for weight, grad_soft in zip(weights_of, grad_softs):
            wide = weight.astype(F32)
            ones.append((wide * (grad_soft - jnp.sum(wide * grad_soft, 0, keepdims=True))).astype(BF))
        for k, (here, t) in enumerate(places):
            value = dot(weights_of[k], lows[k])
            grad_qkv[here, 2 * width + t * GROUP : 2 * width + (t + 1) * GROUP] = value.astype(BF)
        for k, (here, t) in enumerate(places):
            value = dot(ones[k], both_heads(tile_of(qkv, 0, k), lower))
            grad_qkv[here, width + t * GROUP : width + (t + 1) * GROUP] = (value * SCALE).astype(BF)
        for k, (here, t) in enumerate(places):
            turned = jnp.concatenate([ones[k][:, :GROUP].T, ones[k][:, GROUP:].T], 1)
            value = dot(turned, both_heads(tile_of(qkv, 1, k), lower))
            grad_qkv[here, t * GROUP : (t + 1) * GROUP] = (value * SCALE).astype(BF)
        grad_in[:, : 3 * width] += t_dot(normed, grad_qkv[...])
        grad_normed = dot_t(grad_qkv[...], weights[:, : 3 * width])
        lines[SMALL : SMALL + 8, :] += fold_rows(grad_normed * unit)
        lines[SMALL + 8 :, :] += fold_rows(grad_normed)
        result = grad_after[...] + norm_back(unit, spread, grad_normed * gain)
        for k, part in enumerate(grad_start):
            part[...] = result[:, k * GROUP : (k + 1) * GROUP]
        for g in range(SPLIT):
            line = pl.ds(ids[rows_of[i * SPLIT + g]], 1)
            part = jnp.sum(result[g * GROUP : (g + 1) * GROUP, :], 0, keepdims=True)
            lines[line, :] = lines[line, :] + part

    run_blocks(step, 0, blocks[0], streams, start_all)

    def put(at, block):
        lines[langs + at : langs + at + 1, :] = jnp.sum(block, 0, keepdims=True)

    put(0, lines[SMALL : SMALL + 8, :])
    put(1, lines[SMALL + 8 :, :])
    put(2, sums_in[32:40, :])
    put(3, sums_in[40:48, :])
    put(4, sums_in[48:56, :])
    for j in range(FOLD):
        put(5 + j, sums_in[8 * j : 8 * j + 8, :])
    grads[:, : 4 * width] = grad_in[...].astype(BF)
    grads[:, 4 * width :] = lines[:SMALL, :].T.astype(BF)
    ranked = dot(sorted_rows(place[CORE], counts, width), grads[...]).astype(BF)
    kept_out[...] = ranked[: width // 2]
    sent_out[...] = ranked[width // 2 :]


def char_attend_back(
    settings, blocks, rows_of, ids, place, packed, qkv, soft, mixed, grad_after, weights, sums
):
    rows, width = packed.shape
    span = 4 * width + SMALL
    return streamed(
        functools.partial(char_attend_back_kernel, settings),
        (blocks, rows_of, ids, place),
        (packed, qkv, soft, mixed, grad_after),
        (columns(weights, 4 * width, 0), columns(weights, SMALL, weights.shape[1] - SMALL), sums),
        (((rows + BLOCK, GROUP), F32),) * (width // GROUP),
        (((width // 2, span), BF),) * 2,
        (
            ((SMALL, width), F32),
            ((BLOCK, width), BF),
            ((BLOCK, 3 * width), BF),
            ((width, 4 * width), F32),
            ((SMALL + 16, width), F32),
            ((width, span), BF),
        ),
        pl.CostEstimate(
            flops=rows * width * width * 24, bytes_accessed=rows * width * 20, transcendentals=0
        ),
    )


def word_kernel(
    counts,
    members,
    place,
    weights_all,
    cotangent,
    cotangent_other,
    *refs,
):
    pieces, refs = refs[: 2 * members], refs[2 * members :]
    away, refs = refs[:7], refs[7:]
    grad_query_out, sums_out = refs[:2]
    pair_outs, refs = refs[2 : 2 + members], refs[2 + members :]
    words_both, words_sent, grad_after_out, normed_out, word_in_out, kept_out, sent_out = refs[:7]
    sent_sem, weights, to_word, held_sem = refs[7:11]
    refs = refs[11:]
    (
        small_rows,
        pooled,
        word_all,
        normed_all,
        pair,
        query,
        blocked,
        soft_near,
        soft_far,
        mixed,
        after,
        unit_two,
        normed_two,
        up_low,
        total,
        grad_normed,
        grads,
        natural,
        grad_pair,
    ) = refs
    member = place[MEMBER]
    my_row = place[ROW]
    length = place[LENGTH]
    all_words, narrow = pooled.shape
    width = up_low.shape[1]
    own_words = up_low.shape[0]
    local = own_words // 2
    half = all_words // 2
    hidden = FOLD * width
    reach = (half, all_words)
    at_out, at_expand, at_reduce = 3 * width, 4 * width, 4 * width + hidden
    at_to_word = at_reduce + hidden
    at_small = at_to_word + width // 2

    def fetch(k, start, stop):
        return pltpu.make_async_copy(
            weights_all.at[:, start:stop], weights.at[:, start:stop], held_sem.at[k]
        )

    early = (
        fetch(0, at_to_word, at_small + SMALL),
        fetch(1, 0, at_out),
    )
    late = (fetch(2, at_out, at_expand), fetch(3, at_expand, at_to_word))
    for copy in early + late:
        copy.start()
    leaving = [
        pltpu.make_async_copy(here, there, sent_sem.at[k])
        for k, (here, there) in enumerate(
            zip((words_both, words_sent, grad_after_out, normed_out, word_in_out, kept_out, sent_out), away)
        )
    ]
    for copy in early:
        copy.wait()
    small_rows[...] = weights[:, at_small:].astype(F32).T
    to_word[...] = whole_to_word(weights.at[:, at_to_word:at_small], 2 * counts[0] * counts[1])

    def rows_at(index):
        return pl.ds(pl.multiple_of(index * local, local), local)

    for m in range(members):
        there = jnp.bitwise_xor(member, m)
        pooled[rows_at(my_row * members + there), :] = pieces[2 * m][...]
        pooled[rows_at((1 - my_row) * members + there), :] = pieces[2 * m + 1][...]

    def embed(t, carry):
        here = pl.ds(pl.multiple_of(t * local, local), local)
        value = dot(pooled[here, :], to_word[...]) + small_rows[5:6, :]
        word_all[here, :] = value
        unit, _ = norm_parts(value)
        normed = (unit * small_rows[0:1, :] + small_rows[1:2, :]).astype(BF)
        normed_all[here, :] = normed
        pair[here, :] = dot(normed, weights[:, width : 3 * width]).astype(BF)
        return carry

    lax.fori_loop(0, all_words // local, embed, 0, unroll=4)
    origin = []
    for t in range(2):
        base = member * local + t * half
        origin.append(base)
        here = slice(t * local, (t + 1) * local)
        word_in_out[here, :] = word_all[rows_at(member + t * members), :]
        normed_out[here, :] = normed_all[rows_at(member + t * members), :]
    leaving[3].start()
    leaving[4].start()
    query[...] = dot(normed_out[...], weights[:, :width]).astype(BF)
    masks = head_masks(GROUP, 2)
    lower = lax.broadcasted_iota(jnp.int32, (local, GROUP), 1) < HEAD
    softs = (soft_near, soft_far)

    for t in range(2):
        seen = lax.broadcasted_iota(jnp.int32, (local, reach[t]), 1)
        asks = lax.broadcasted_iota(jnp.int32, (local, reach[t]), 0) + origin[t]
        blocked[t * local : (t + 1) * local, : reach[t]] = jnp.where((seen <= asks) & (seen < length), 0.0, MASKED)
    chains = [(slice(t * local, (t + 1) * local), t, h) for t in range(2) for h in range(2)]

    def attend(p, carry):
        lanes = pl.ds(pl.multiple_of(p * GROUP, GROUP), GROUP)
        after_lanes = pl.ds(pl.multiple_of(width + p * GROUP, GROUP), GROUP)
        scores = [dot_t(query[here, lanes] * masks[h], pair[: reach[t], lanes]) for here, t, h in chains]
        weights_of = []
        for (here, t, h), score in zip(chains, scores):
            score = score * SCALE + blocked[here, : reach[t]]
            score = jnp.exp(score - jnp.max(score, -1, keepdims=True))
            soft = (score * (1.0 / jnp.sum(score, -1, keepdims=True))).astype(BF)
            softs[t][2 * p + h] = soft
            weights_of.append(soft)
        outs = [dot(soft, pair[: reach[t], after_lanes]) for (_, t, h), soft in zip(chains, weights_of)]
        for t in range(2):
            mixed[t * local : (t + 1) * local, lanes] = jnp.where(lower, outs[2 * t], outs[2 * t + 1]).astype(BF)
        return carry

    lax.fori_loop(0, WHEADS // 2, attend, 0, unroll=4)
    for copy in late:
        copy.wait()
    value = word_in_out[...] + dot(mixed[...], weights[:, at_out : at_out + width])
    after[...] = value
    unit, spread = norm_parts(value)
    unit_two[...] = unit
    normed_two[...] = (unit * small_rows[2:3, :] + small_rows[3:4, :]).astype(BF)
    row = lax.broadcasted_iota(jnp.int32, (own_words, 1), 0)
    index = jnp.where(row < local, origin[0] + row, origin[1] + row - local)
    valid = index < length
    up_low[rows_at(my_row), :] = cotangent[my_row]
    up_low[rows_at(1 - my_row), :] = cotangent_other[...]
    up_low[...] = jnp.where(valid, up_low[...].astype(F32), 0.0).astype(BF)
    total[...] = jnp.zeros_like(total)
    grad_normed[...] = jnp.zeros_like(grad_normed)

    def feed(j, carry):
        expand = weights[:, pl.ds(pl.multiple_of(at_expand + j * width, GROUP), width)]
        shrink = weights[:, pl.ds(pl.multiple_of(at_reduce + j * width, GROUP), width)]
        pre = dot(normed_two[...], expand) + small_rows[pl.ds(6 + j, 1), :]
        act, slope = gelu_both(pre)
        act = act.astype(BF)
        total[...] += dot(act, shrink)
        grad_pre = dot_t(up_low[...], shrink) * slope
        sums_out[pl.ds(6 + j, 1), :] = jnp.sum(grad_pre, 0, keepdims=True)
        grad_pre = grad_pre.astype(BF)
        grad_normed[...] += dot_t(grad_pre, expand)
        cols = pl.multiple_of(j * width, GROUP)
        grads[:, pl.ds(cols, width)] = t_dot(normed_two[...], grad_pre).astype(BF)
        grads[:, pl.ds(pl.multiple_of(hidden + j * width, GROUP), width)] = t_dot(
            act, up_low[...]
        ).astype(BF)
        return carry

    lax.fori_loop(0, FOLD, feed, 0, unroll=4)
    total[...] = jnp.where(valid, after[...] + (total[...] + small_rows[4:5, :]), 0.0)
    for t in range(2):
        words_both[t] = total[t * local : (t + 1) * local, :]
    words_sent[...] = total[rows_at(1 - my_row), :]
    leaving[0].start()
    leaving[1].start()
    upstream = up_low[...].astype(F32)
    incoming = grad_normed[...]
    sums_out[2:3, :] = jnp.sum(incoming * unit_two[...], 0, keepdims=True)
    sums_out[3:4, :] = jnp.sum(incoming, 0, keepdims=True)
    sums_out[4:5, :] = jnp.sum(upstream, 0, keepdims=True)
    grad_after = upstream + norm_back(unit_two[...], spread, incoming * small_rows[2:3, :])
    grad_after_out[...] = grad_after
    leaving[2].start()
    grad_low = grad_after.astype(BF)
    grads[:, 2 * hidden :] = t_dot(mixed[...], grad_low).astype(BF)
    mixed[...] = dot_t(grad_low, weights[:, at_out : at_out + width]).astype(BF)
    unfold_into(natural, grads[:, :hidden], width)
    chosen = sorted_rows(place[CORE], counts, width)
    for from_ref, start, stop in ((natural, 0, hidden), (grads, hidden, grads.shape[1])):
        ranked = dot(chosen, from_ref[:, start:stop]).astype(BF)
        kept_out[:, start:stop] = ranked[: width // 2]
        sent_out[:, start:stop] = ranked[width // 2 :]
    leaving[5].start()
    leaving[6].start()

    def attend_back(p, carry):
        lanes = pl.ds(pl.multiple_of(p * GROUP, GROUP), GROUP)
        after_lanes = pl.ds(pl.multiple_of(width + p * GROUP, GROUP), GROUP)
        lows = [mixed[here, lanes] * masks[h] for here, t, h in chains]
        ones = [dot_t(low, pair[: reach[t], after_lanes]) for low, (_, t, h) in zip(lows, chains)]
        weights_of = [softs[t][2 * p + h] for _, t, h in chains]
        grads_of = []
        for one, soft in zip(ones, weights_of):
            wide = soft.astype(F32)
            grads_of.append((wide * (one - jnp.sum(wide * one, -1, keepdims=True))).astype(BF))
        grad_values = [dot(soft.T, low) for soft, low in zip(weights_of, lows)]
        grad_keys = [
            dot(one.T, query[here, lanes] * masks[h]) for one, (here, t, h) in zip(grads_of, chains)
        ]
        grad_queries = [dot(one, pair[: reach[t], lanes]) for one, (_, t, h) in zip(grads_of, chains)]
        grad_values = [grad_values[2 * t] + grad_values[2 * t + 1] for t in range(2)]
        grad_keys = [grad_keys[2 * t] + grad_keys[2 * t + 1] for t in range(2)]
        for t in range(2):
            grad_query = jnp.where(lower, grad_queries[2 * t], grad_queries[2 * t + 1])
            grad_query_out[t * local : (t + 1) * local, lanes] = (grad_query * SCALE).astype(BF)
        for parts, at, factor in ((grad_keys, lanes, SCALE), (grad_values, after_lanes, 1.0)):
            grad_pair[:half, at] = ((parts[0] + parts[1][:half]) * factor).astype(BF)
            grad_pair[half:, at] = (parts[1][half:] * factor).astype(BF)
        return carry

    lax.fori_loop(0, WHEADS // 2, attend_back, 0)
    for m in range(members):
        there = jnp.bitwise_xor(member, m)
        for t in range(2):
            pair_outs[m][t * local : (t + 1) * local, :] = grad_pair[rows_at(t * members + there), :]
    for copy in leaving:
        copy.wait()


def word_part(counts, place, pieces, weights, cotangent, cotangent_other):
    members = len(pieces) // 2
    local, narrow = pieces[0].shape
    all_words = local * len(pieces)
    width = cotangent.shape[2]
    own = 2 * local
    hidden = FOLD * width
    vmem = pl.BlockSpec(memory_space=pltpu.VMEM)
    hbm = pl.BlockSpec(memory_space=pltpu.HBM)
    share = ((width // 2, 2 * hidden + width), BF)
    away = (
        ((2, local, width), F32),
        ((local, width), F32),
        ((own, width), F32),
        ((own, width), BF),
        ((own, width), F32),
        share,
        share,
    )
    stay = (((own, width), BF), ((16, width), F32)) + (((own, 2 * width), BF),) * members
    return pl.pallas_call(
        functools.partial(word_kernel, counts, members),
        out_shape=tuple(jax.ShapeDtypeStruct(*out) for out in away + stay),
        in_specs=[pl.BlockSpec(memory_space=pltpu.SMEM), hbm] + [vmem] * (2 + len(pieces)),
        out_specs=(hbm,) * len(away) + (vmem,) * len(stay),
        scratch_shapes=[pltpu.VMEM(*out) for out in away]
        + [
            pltpu.SemaphoreType.DMA((len(away),)),
            pltpu.VMEM(weights.shape, BF),
            pltpu.VMEM((narrow, width), BF),
            pltpu.SemaphoreType.DMA((4,)),
            pltpu.VMEM((SMALL, width), F32),
            pltpu.VMEM((all_words, narrow), BF),
            pltpu.VMEM((all_words, width), F32),
            pltpu.VMEM((all_words, width), BF),
            pltpu.VMEM((all_words, 2 * width), BF),
            pltpu.VMEM((own, width), BF),
            pltpu.VMEM((own, all_words), F32),
            pltpu.VMEM((WHEADS, local, all_words // 2), BF),
            pltpu.VMEM((WHEADS, local, all_words), BF),
            pltpu.VMEM((own, width), BF),
            pltpu.VMEM((own, width), F32),
            pltpu.VMEM((own, width), F32),
            pltpu.VMEM((own, width), BF),
            pltpu.VMEM((own, width), BF),
            pltpu.VMEM((own, width), F32),
            pltpu.VMEM((own, width), F32),
            pltpu.VMEM((width, 2 * hidden + width), BF),
            pltpu.VMEM((width, hidden), BF),
            pltpu.VMEM((all_words, 2 * width), BF),
        ],
        compiler_params=pltpu.CompilerParams(vmem_limit_bytes=VMEM_LIMIT),
        cost_estimate=pl.CostEstimate(
            flops=own * width * width * 60, bytes_accessed=20 * MIB, transcendentals=own * 8192
        ),
    )(place, weights, cotangent, cotangent_other, *pieces)


def word_end_kernel(
    counts,
    place,
    pooled_kept,
    pooled_other,
    to_word_ref,
    weights,
    small,
    grad_query,
    normed,
    word_in,
    grad_after,
    sums,
    *refs,
):
    pairs, refs = refs[:-8], refs[-8:]
    up_kept, up_sent, grad_to_word, kept_out, sent_out, small_rows, small_grads, incoming = refs
    width = grad_query.shape[1]
    local, narrow = pooled_kept.shape
    to_word = whole_to_word(to_word_ref, 2 * counts[0] * counts[1])
    small_rows[...] = small[...].astype(F32).T
    incoming[:, :width] = grad_query[...]
    pair = pairs[0][...].astype(F32)
    for other in pairs[1:]:
        pair = pair + other[...].astype(F32)
    incoming[:, width:] = pair.astype(BF)
    grad_normed = dot_t(incoming[...], weights[...])
    unit, spread = norm_parts(word_in[...])
    small_grads[...] = jnp.zeros_like(small_grads)
    small_grads[0:1, :] = jnp.sum(grad_normed * unit, 0, keepdims=True)
    small_grads[1:2, :] = jnp.sum(grad_normed, 0, keepdims=True)
    small_grads[2:5, :] = sums[2:5, :]
    small_grads[6:10, :] = sums[6:10, :]
    value = grad_after[...] + norm_back(unit, spread, grad_normed * small_rows[0:1, :])
    small_grads[5:6, :] = jnp.sum(value, 0, keepdims=True)
    low = value.astype(BF)
    back = dot_t(low, to_word).astype(BF)
    first_half = place[ROW] == 0
    up_kept[...] = jnp.where(first_half, back[:local].astype(F32), back[local:].astype(F32)).astype(BF)
    up_sent[...] = jnp.where(first_half, back[local:].astype(F32), back[:local].astype(F32)).astype(BF)
    low_kept = jnp.where(first_half, value[:local], value[local:]).astype(BF)
    low_other = jnp.where(first_half, value[local:], value[:local]).astype(BF)
    grad_to_word[...] = (t_dot(pooled_kept[...], low_kept) + t_dot(pooled_other[...], low_other)).astype(BF)
    inward = t_dot(normed[...], incoming[...]).astype(BF)
    small_turned = small_grads[...].T.astype(BF)
    span = 3 * width + SMALL
    cuts = width // narrow
    chosen = sorted_rows(place[CORE], counts, width, cuts)
    ranked = dot(chosen, inward).astype(BF)
    ranked_small = dot(chosen, small_turned).astype(BF)
    some = narrow // 2
    for k in range(2 * cuts):
        out_ref = (kept_out, sent_out)[k // cuts]
        at = k % cuts * span
        out_ref[:, at : at + 3 * width] = ranked[k * some : (k + 1) * some]
        out_ref[:, at + 3 * width : at + span] = ranked_small[k * some : (k + 1) * some]


def word_end(
    counts,
    place,
    pooled_kept,
    pooled_other,
    weights,
    grad_query,
    normed,
    word_in,
    grad_after,
    sums,
    pairs,
):
    local, narrow = pooled_kept.shape
    own, width = grad_query.shape
    last = weights.shape[1] // SMALL - 1
    share = (narrow // 2, (3 * width + SMALL) * (width // narrow))
    outs = ((local, narrow), (local, narrow), (narrow, width), share, share)
    operands = (grad_query, normed, word_in, grad_after, sums) + tuple(pairs)
    return pl.pallas_call(
        functools.partial(word_end_kernel, counts),
        out_shape=tuple(jax.ShapeDtypeStruct(shape, BF) for shape in outs),
        grid_spec=pltpu.PrefetchScalarGridSpec(
            num_scalar_prefetch=1,
            grid=(1,),
            in_specs=[
                full(pooled_kept.shape),
                full(pooled_other.shape),
                columns(weights, width // 2, 12 * width)[1],
                pl.BlockSpec((width, 3 * width), lambda i, *_: (0, 0)),
                pl.BlockSpec((width, SMALL), lambda i, *_: (0, last)),
            ]
            + [full(operand.shape) for operand in operands],
            out_specs=tuple(full(shape) for shape in outs),
            scratch_shapes=[
                pltpu.VMEM((SMALL, width), F32),
                pltpu.VMEM((SMALL, width), F32),
                pltpu.VMEM((own, 3 * width), BF),
            ],
        ),
        compiler_params=pltpu.CompilerParams(vmem_limit_bytes=VMEM_LIMIT),
        cost_estimate=pl.CostEstimate(
            flops=own * width * width * 14, bytes_accessed=10 * MIB, transcendentals=0
        ),
    )(place, pooled_kept, pooled_other, weights, weights, weights, *operands)


def column(vector, rows):
    each = vector.shape[0] // rows
    wide = vector[...].astype(F32).reshape(1, rows * each)
    line = lax.broadcasted_iota(jnp.int32, (rows, rows * each), 0)
    lane = lax.broadcasted_iota(jnp.int32, (rows, rows * each), 1)
    return [
        jnp.sum(jnp.where(line * each + j == lane, wide, 0.0), 1, keepdims=True) for j in range(each)
    ]


def columns_beside(rows, vectors, at):
    lane = lax.broadcasted_iota(jnp.int32, (rows, SMALL), 1)
    block = jnp.zeros((rows, SMALL), F32)
    for vector in vectors:
        for one in column(vector, rows):
            block = block + jnp.where(lane == at, one, 0.0)
            at += 1
    return block


def fold_into(out, at, weights, width):
    size = FOLD * HEAD
    matrix = folding(False)
    for m in range(width // HEAD):
        block = dot(weights[:, m * size : (m + 1) * size], matrix).astype(BF)
        for j in range(FOLD):
            there = at + j * width + m * HEAD
            out[:, there : there + HEAD] = block[:, j * HEAD : (j + 1) * HEAD]


def fold_shard(weights):
    tall = weights.shape[0]
    rows = tall // FOLD
    line = lax.broadcasted_iota(jnp.int32, (rows, tall), 0)
    lane = lax.broadcasted_iota(jnp.int32, (rows, tall), 1)
    return [
        dot((lane == FOLD * line + j).astype(F32).astype(BF), weights[...]).astype(BF) for j in range(FOLD)
    ]


def char_shard_kernel(table, inward, outward, expand, reduced, *refs):
    vectors, out = refs[:-1], refs[-1]
    rows, langs = table.shape
    width = outward.shape[1]
    at_expand, at_reduce, at_small = 4 * width, (4 + FOLD) * width, (4 + 2 * FOLD) * width
    out[:, : 3 * width] = inward[...]
    out[:, 3 * width : 4 * width] = outward[...]
    line = lax.broadcasted_iota(jnp.int32, (langs, SMALL), 0)
    lane = lax.broadcasted_iota(jnp.int32, (langs, SMALL), 1)
    spread = (line == lane).astype(F32).astype(BF)
    small = dot(table[...], spread) + columns_beside(rows, vectors, langs)
    out[:, at_small:] = small.astype(BF)
    fold_into(out, at_expand, expand, width)
    for j, part in enumerate(fold_shard(reduced)):
        out[:, at_reduce + j * width : at_reduce + (j + 1) * width] = part


def char_shard(table, inward, outward, expand, reduced, vectors):
    rows, width = outward.shape
    vmem = pl.BlockSpec(memory_space=pltpu.VMEM)
    return pl.pallas_call(
        char_shard_kernel,
        out_shape=jax.ShapeDtypeStruct((rows, (4 + 2 * FOLD) * width + SMALL), BF),
        in_specs=[vmem] * (5 + len(vectors)),
        out_specs=vmem,
    )(table, inward, outward, expand, reduced, *vectors)


def word_shard_kernel(inward, outward, expand, reduced, to_word, *refs):
    vectors, out = refs[:-1], refs[-1]
    rows, width = outward.shape
    out[:, : 3 * width] = inward[...]
    out[:, 3 * width : 4 * width] = outward[...]
    fold_into(out, 4 * width, expand, width)
    for j, part in enumerate(fold_shard(reduced)):
        out[:, (8 + j) * width : (9 + j) * width] = part
    narrow, half = to_word.shape[0], width // 2
    for k in range(2):
        out[k * narrow : (k + 1) * narrow, 12 * width : 12 * width + half] = to_word[:, k * half : (k + 1) * half]
    out[:, 12 * width + half :] = columns_beside(rows, vectors, 0).astype(BF)


def word_shard(inward, outward, expand, reduced, to_word, vectors):
    rows, width = outward.shape
    vmem = pl.BlockSpec(memory_space=pltpu.VMEM)
    return pl.pallas_call(
        word_shard_kernel,
        out_shape=jax.ShapeDtypeStruct((rows, 12 * width + width // 2 + SMALL), BF),
        in_specs=[vmem] * (5 + len(vectors)),
        out_specs=vmem,
    )(inward, outward, expand, reduced, to_word, *vectors)


def assemble_kernel(masks, index, *refs):
    pieces, out = refs[:-1], refs[-1]
    me = index[0]
    size = pieces[0].shape[0]
    for k, piece in enumerate(pieces):
        for t in range(size):
            out[jnp.bitwise_xor(me, masks[k * size + t])] = piece[t]


def assemble(masks, index, pieces):
    size, rows, columns = pieces[0].shape
    vmem = pl.BlockSpec(memory_space=pltpu.VMEM)
    out = pl.pallas_call(
        functools.partial(assemble_kernel, tuple(masks)),
        out_shape=jax.ShapeDtypeStruct((size * len(pieces), rows, columns), BF),
        in_specs=[pl.BlockSpec(memory_space=pltpu.SMEM)] + [vmem] * len(pieces),
        out_specs=vmem,
        compiler_params=pltpu.CompilerParams(vmem_limit_bytes=VMEM_LIMIT),
        cost_estimate=pl.CostEstimate(
            flops=0, bytes_accessed=4 * size * len(pieces) * rows * columns, transcendentals=0
        ),
    )(index, *pieces)
    return out.reshape(-1, columns)


def add_and_cut_kernel(which, arrivals, place, *refs):
    arrived, outs = refs[:arrivals], refs[arrivals:]
    total = arrived[0][...].astype(F32)
    for one in arrived[1:]:
        total = total + one[...].astype(F32)
    total = total.astype(BF)
    rows = total.shape[0]
    each = rows // len(outs)
    line = lax.broadcasted_iota(jnp.int32, (rows, rows), 0)
    lane = lax.broadcasted_iota(jnp.int32, (rows, rows), 1)
    part = jnp.bitwise_xor(lax.div(line, each), place[which])
    chosen = (lane == part * each + lax.rem(line, each)).astype(F32).astype(BF)
    sorted_total = dot(chosen, total).astype(BF)
    for m, out in enumerate(outs):
        out[...] = sorted_total[m * each : (m + 1) * each]


def add_and_cut(arrived, parts, which, place):
    rows, columns = arrived[0].shape

    vmem = pl.BlockSpec(memory_space=pltpu.VMEM)
    return pl.pallas_call(
        functools.partial(add_and_cut_kernel, which, len(arrived)),
        out_shape=(jax.ShapeDtypeStruct((rows // parts, columns), BF),) * parts,
        in_specs=[pl.BlockSpec(memory_space=pltpu.SMEM)] + [vmem] * len(arrived),
        out_specs=(vmem,) * parts,
        compiler_params=pltpu.CompilerParams(vmem_limit_bytes=VMEM_LIMIT),
        cost_estimate=pl.CostEstimate(
            flops=0, bytes_accessed=sum(4 * one.size for one in arrived), transcendentals=0
        ),
    )(place, *arrived)


def unfold_rows(folded, rows, out):
    width = out.shape[1]
    line = lax.broadcasted_iota(jnp.int32, (FOLD * rows, rows), 0)
    lane = lax.broadcasted_iota(jnp.int32, (FOLD * rows, rows), 1)
    total = jnp.zeros(out.shape, F32)
    for j in range(FOLD):
        chosen = (line == FOLD * lane + j).astype(F32)
        total = total + lax.dot_general(
            chosen,
            folded[:, j * width : (j + 1) * width],
            (((1,), (0,)), ((), ())),
            precision=lax.Precision.HIGHEST,
            preferred_element_type=F32,
        )
    out[...] = total


def finish_kernel(plan, count, *refs):
    arrived, outs = refs[:count], refs[count:]
    total = arrived[0][...].astype(F32)
    for one in arrived[1:]:
        total = total + one[...].astype(F32)
    rows = total.shape[0]
    for (kind, start, stop), out in zip(plan, outs):
        if kind == "folded":
            unfold_rows(total[:, start:stop], rows, out)
        elif kind == "plain":
            out[...] = total[:, start:stop]
        elif kind == "halves":
            height, width = out.shape
            pieces = height // rows
            stride = (stop - start) // pieces
            for k in range(pieces):
                out[k * rows : (k + 1) * rows, :] = total[:, start + k * stride : start + k * stride + width]
        else:
            pieces = stop[0]
            height = rows * pieces
            each = out.shape[0] // height
            value = jnp.zeros((1, out.shape[0]), F32)
            for k in range(pieces):
                block = total[:, start + k * stop[1] : start + k * stop[1] + SMALL]
                line = lax.broadcasted_iota(jnp.int32, (rows, out.shape[0]), 0) + k * rows
                lane = lax.broadcasted_iota(jnp.int32, (rows, out.shape[0]), 1)
                for j in range(each):
                    at = stop[2] + j
                    found = jnp.where(lane == line * each + j, block[:, at : at + 1], 0.0)
                    value = value + jnp.sum(found, 0, keepdims=True)
            out[...] = value.reshape(out.shape[0])


def finish(arrived, plan):
    vmem = pl.BlockSpec(memory_space=pltpu.VMEM)
    return pl.pallas_call(
        functools.partial(finish_kernel, tuple(one[:3] for one in plan), len(arrived)),
        out_shape=tuple(jax.ShapeDtypeStruct(shape, F32) for _, _, _, shape in plan),
        in_specs=[vmem] * len(arrived),
        out_specs=(vmem,) * len(plan),
        compiler_params=pltpu.CompilerParams(vmem_limit_bytes=VMEM_LIMIT),
    )(*arrived)


def tie(values, after):
    return lax.optimization_barrier((values, after))[0]


def body(
    char_inputs,
    language_ids,
    char_counts,
    row_lengths,
    cotangent,
    language_table,
    char_gain_one,
    char_bias_one,
    char_inward,
    char_outward,
    char_gain_two,
    char_bias_two,
    char_expand,
    char_expand_bias,
    char_reduce,
    char_reduce_bias,
    char_to_word,
    char_to_word_bias,
    word_gain_one,
    word_bias_one,
    word_inward,
    word_outward,
    word_gain_two,
    word_bias_two,
    word_expand,
    word_expand_bias,
    word_reduce,
    word_reduce_bias,
):
    rows, local, slots, width = char_inputs.shape
    words = rows * local
    langs = language_table.shape[0]
    wide = word_inward.shape[1] // 3
    deep, share = lax.axis_size("dp"), lax.axis_size("fsdp")
    devices = deep * share
    members = share // rows
    axes = ("dp", "fsdp")
    at_deep, at_share = lax.axis_index("dp"), lax.axis_index("fsdp")

    def swap(values, mask):
        return lax.ppermute(values, axes, [(k, k ^ mask) for k in range(devices)])

    far, low = deep // 2, share // 2
    near = 2 * low
    far_masks = [m * 2 * share for m in range(far)]
    near_masks = [(m // low) * share + (m % low) * 2 for m in range(near)]
    core_masks = [0, 1]
    counts_of = (far, near)
    top = members
    my_row = at_share // members
    index = (at_deep * share + at_share).reshape(1)

    def swaps(values, masks):
        return [values] + [swap(values, m) for m in masks[1:]]

    def together(pieces, rows):
        return jnp.stack(pieces).reshape(-1, rows, pieces[0].shape[-1])

    order = [c | n | f for c in core_masks for n in near_masks for f in far_masks]

    char_piece = char_shard(
        language_table.T,
        char_inward,
        char_outward,
        char_expand,
        char_reduce,
        (char_gain_one, char_bias_one, char_gain_two, char_bias_two, char_reduce_bias, char_expand_bias),
    )
    each = char_piece.shape[0]
    counts = tie(char_counts, char_piece)
    offs, first, rows_of, blocks, place = offsets((share, members), counts, row_lengths, index, slots)
    char_piece = together(tie(swaps(char_piece, far_masks), offs), each)
    packed, bias, hot, inverse = pack(
        tie(counts, char_piece), offs, first, blocks, char_inputs.reshape(words, slots, width)
    )
    char_piece = together(swaps(char_piece, near_masks), each)
    char_full = assemble(order, index, swaps(tie(char_piece, packed), core_masks))
    word_full = lax.all_gather(
        word_shard(
            word_inward,
            word_outward,
            word_expand,
            word_reduce,
            char_to_word,
            (
                word_gain_one,
                word_bias_one,
                word_gain_two,
                word_bias_two,
                word_reduce_bias,
                char_to_word_bias,
                word_expand_bias,
            ),
        ),
        axes,
        axis=0,
        tiled=True,
    )

    qkv, soft, mixed, after, cotangent_sent = char_attend(
        langs, blocks, rows_of, language_ids, place, packed, bias, char_full, cotangent
    )
    cotangent_other = swap(cotangent_sent, top)
    act, slope, pooled_kept, pooled_sent = char_ffn(
        langs, blocks, first, place, after, hot, inverse, char_full
    )
    cotangent_other, pooled_kept, pooled_sent = lax.optimization_barrier(
        (cotangent_other, pooled_kept, pooled_sent)
    )
    pooled_other = swap(pooled_sent, top)
    pieces = []
    for m in range(members):
        pieces += [swap(pooled_kept, m), swap(pooled_other, m)] if m else [pooled_kept, pooled_other]
    words_both, words_sent, word_after_grad, word_normed, word_in, word_kept, word_sent, *others = word_part(
        counts_of, place, pieces, word_full, cotangent, cotangent_other
    )
    query_grad, word_sums, *pair_grads = others
    pairs = [pair_grads[0]] + [swap(pair_grads[m], m) for m in range(1, members)]
    word_sent, words_sent, pairs = lax.optimization_barrier((word_sent, words_sent, pairs))
    words_other = swap(words_sent, top)
    word_arrived = [word_kept, swap(word_sent, 1)]
    up_kept, up_sent, to_word_grad, inward_kept, inward_sent = word_end(
        counts_of,
        place,
        pooled_kept,
        pooled_other,
        word_full,
        query_grad,
        word_normed,
        word_in,
        word_after_grad,
        word_sums,
        pairs,
    )
    up_other = swap(up_sent, top)

    def phase(parts, masks):
        return [parts[0]] + [swap(parts[m], masks[m]) for m in range(1, len(masks))]

    word_parts = add_and_cut(word_arrived, near, NEAR, place)
    word_parts, words_other = lax.optimization_barrier((word_parts, words_other))
    up_kept = tie(up_kept, word_parts)
    after_grad, feed_kept, feed_sent, char_sums = char_ffn_back(
        (langs, counts_of),
        blocks,
        first,
        place,
        after,
        hot,
        act,
        slope,
        inverse,
        up_kept,
        up_other,
        char_full,
        to_word_grad,
        (inward_kept, inward_sent),
    )
    word_parts = add_and_cut(tie(phase(word_parts, near_masks), feed_kept), far, FAR, place)
    feed_sent = tie(feed_sent, word_parts)
    late_parts = add_and_cut([feed_kept, swap(feed_sent, 1)], near, NEAR, place)
    after_grad = tie(after_grad, (word_parts, late_parts))
    operands = (packed, qkv, soft, mixed, after_grad, char_full, char_sums)
    *start_grad, attend_kept, attend_sent = char_attend_back(
        (langs, counts_of), blocks, rows_of, language_ids, place, *operands
    )
    arrived_words, arrived_late, attend_kept, attend_sent = lax.optimization_barrier(
        (phase(word_parts, far_masks), phase(late_parts, near_masks), attend_kept, attend_sent)
    )
    late_parts = add_and_cut(arrived_late, far, FAR, place)
    hidden, wide_hidden = FOLD * width, FOLD * wide
    grad_word_expand, grad_word_reduce, grad_word_outward = finish(
        arrived_words,
        (
            ("plain", 0, wide_hidden, word_expand.shape),
            ("folded", wide_hidden, 2 * wide_hidden, word_reduce.shape),
            ("plain", 2 * wide_hidden, 2 * wide_hidden + wide, word_outward.shape),
        ),
    )
    words_out = lax.dynamic_update_index_in_dim(words_both, words_other, 1 - my_row, 0)
    earlier = (words_out, grad_word_expand, grad_word_reduce, grad_word_outward)
    arrived, earlier, late_parts = lax.optimization_barrier(
        ([attend_kept, swap(attend_sent, 1)], earlier, late_parts)
    )
    attend_parts = add_and_cut(arrived, near, NEAR, place)
    char_input_grad = unpack(offs, char_counts, tie(start_grad, attend_parts), slots)
    arrived, arrived_late, char_input_grad = lax.optimization_barrier(
        (phase(attend_parts, near_masks), phase(late_parts, far_masks), char_input_grad)
    )
    attend_parts = add_and_cut(arrived, far, FAR, place)
    char_input_grad = unpack(offs, char_counts, tie(start_grad, attend_parts), slots, char_input_grad)
    arrived, arrived_late, char_input_grad = lax.optimization_barrier(
        (phase(attend_parts, far_masks), arrived_late, char_input_grad)
    )
    at_inward = 2 * hidden + wide
    stop = at_inward + (3 * wide + SMALL) * (wide // width)
    grad_expand, grad_reduce, grad_to_word, grad_word_inward, *word_vectors = finish(
        arrived_late,
        (
            ("plain", 0, hidden, char_expand.shape),
            ("folded", hidden, 2 * hidden, char_reduce.shape),
            ("plain", 2 * hidden, at_inward, char_to_word.shape),
            ("halves", at_inward, stop, word_inward.shape),
        )
        + tuple(
            ("vector", at_inward + 3 * wide, (wide // width, 3 * wide + SMALL, at), vector.shape)
            for at, vector in (
                (0, word_gain_one),
                (1, word_bias_one),
                (2, word_gain_two),
                (3, word_bias_two),
                (4, word_reduce_bias),
                (5, char_to_word_bias),
                (6, word_expand_bias),
            )
        ),
    )
    grad_inward, grad_outward, grad_table, *char_vectors = finish(
        arrived,
        (
            ("plain", 0, 3 * width, char_inward.shape),
            ("plain", 3 * width, 4 * width, char_outward.shape),
            ("plain", 4 * width, 4 * width + langs, (char_inward.shape[0], langs)),
        )
        + tuple(
            ("vector", 4 * width, (1, 0, langs + at), vector.shape)
            for at, vector in (
                (0, char_gain_one),
                (1, char_bias_one),
                (2, char_gain_two),
                (3, char_bias_two),
                (4, char_reduce_bias),
                (5, char_expand_bias),
            )
        ),
    )
    words_out, grad_word_expand, grad_word_reduce, grad_word_outward = earlier

    gain_one, bias_one, gain_two, bias_two, reduce_bias, expand_bias = char_vectors
    wide_gain_one, wide_bias_one, wide_gain_two, wide_bias_two, wide_reduce_bias = word_vectors[:5]
    to_word_bias, wide_expand_bias = word_vectors[5:]
    return (
        words_out,
        char_input_grad.reshape(char_inputs.shape),
        grad_table.T,
        gain_one,
        bias_one,
        grad_inward,
        grad_outward,
        gain_two,
        bias_two,
        grad_expand,
        expand_bias,
        grad_reduce,
        reduce_bias,
        grad_to_word,
        to_word_bias,
        wide_gain_one,
        wide_bias_one,
        grad_word_inward,
        grad_word_outward,
        wide_gain_two,
        wide_bias_two,
        grad_word_expand,
        wide_expand_bias,
        grad_word_reduce,
        wide_reduce_bias,
    )


def solution(mesh):
    both = ("dp", "fsdp")
    vector, matrix = P(both), P(both, None)
    weights = (
        (P(None, both), vector, vector, matrix, matrix, vector, vector)
        + (matrix, vector, matrix, vector, matrix, vector)
        + (vector, vector, matrix, matrix, vector, vector, matrix, vector, matrix, vector)
    )
    in_specs = (
        P("dp", "fsdp", None, None),
        P("dp"),
        P("dp", "fsdp"),
        P("dp"),
        P("dp", "fsdp", None),
    ) + weights
    out_specs = (P("dp", "fsdp", None), P("dp", "fsdp", None, None)) + weights
    return jax.shard_map(body, mesh=mesh, in_specs=in_specs, out_specs=out_specs, check_vma=False)
```
